32 devices in a mesh: seq: 16 (over z, y, core), ch: 2 (over x).
Axes of the slice: x: 2, y: 2, z: 4, core: 2. Of those that a mesh axis runs over, the one named last changes fastest.
Arguments:
- tokens: bfloat16 [2, 32768, 1280], P(None, 'seq', 'ch'), may hold values from -6 to 6
- cotangent: bfloat16 [2, 32768, 1280], P(None, 'seq', 'ch'), may hold values from -6 to 6
- seq_lengths: int32 [2, 128], replicated, may hold values from 1 to 1024, 32768 in all within a row
- residue_mask: int32 [2, 32768], P(None, 'seq'), may hold values 0 or 1
- first_gain: float32 [1280], P('ch'), may hold values from 0.25 to 1.75
- first_shift: float32 [1280], P('ch'), may hold values from -2.5 to 2.5
- proj_in: bfloat16 [1280, 640], P('seq', 'ch'), may hold values from -0.15625 to 0.15625
- in_bias: float32 [640], P('ch'), may hold values from -2.5 to 2.5
- mid_gain: float32 [640], P('ch'), may hold values from 0.25 to 1.75
- mid_shift: float32 [640], P('ch'), may hold values from -2.5 to 2.5
- conv_weight: bfloat16 [5, 640, 640], P(None, 'seq', 'ch'), may hold values from -0.109375 to 0.109375
- conv_bias: float32 [640], P('ch'), may hold values from -2.5 to 2.5
- last_gain: float32 [640], P('ch'), may hold values from 0.25 to 1.75
- last_shift: float32 [640], P('ch'), may hold values from -2.5 to 2.5
- proj_out: bfloat16 [640, 1280], P('ch', 'seq'), may hold values from -0.25 to 0.25
- out_bias: float32 [1280], P('ch'), may hold values from -2.5 to 2.5
Outputs:
- block_out: bfloat16 [2, 32768, 1280], P(None, 'seq', 'ch')
- grad_tokens: float32 [2, 32768, 1280], P(None, 'seq', 'ch')
- grad_first_gain: float32 [1280], P('ch')
- grad_first_shift: float32 [1280], P('ch')
- grad_proj_in: float32 [1280, 640], P('seq', 'ch')
- grad_in_bias: float32 [640], P('ch')
- grad_mid_gain: float32 [640], P('ch')
- grad_mid_shift: float32 [640], P('ch')
- grad_conv_weight: float32 [5, 640, 640], P(None, 'seq', 'ch')
- grad_conv_bias: float32 [640], P('ch')
- grad_last_gain: float32 [640], P('ch')
- grad_last_shift: float32 [640], P('ch')
- grad_proj_out: float32 [640, 1280], P('ch', 'seq')
- grad_out_bias: float32 [1280], P('ch')
The draws below stay inside these ranges and needn't reach their ends.
Inputs may be any that keep to these rules, and one draw needn't show every extreme that they name: `seq_lengths`: each row sums to 32768; the longest protein of each row has exactly 1024 residues.
All inputs are finite; a program needn't handle non-finite values. No bound on the sum of `residue_mask` on one device may be relied on, other than what follows from the above.
Results may differ from the reference program's by a relative error of at most 0.0067.
Values may be sent and summed in bfloat16 or wider, within the bound.
A program may use at most 256 MiB of HBM per device.

```python
import math
import jax
import jax.numpy as jnp
import numpy as np
from jax import lax

D = 1280
INNER = 640
KERNEL_TAPS = 5
DILATION_STEP = 32
LONGEST = 1024
MICRO = 2
TOKEN_COUNT = 32768
NSEQ = 128
HALO = 64


def set_ends(result, rng, smallest, largest):
    place = [jax.random.randint(jax.random.fold_in(rng, axis), (), 0, length) for axis, length in enumerate(result.shape)]
    main_axis = result.shape.index(max(result.shape))
    neighbour = place[:main_axis] + [(place[main_axis] + 1) % result.shape[main_axis]] + place[main_axis + 1:]
    return result.at[tuple(place)].set(smallest).at[tuple(neighbour)].set(largest)


def levels(own_key, dims, cuts, smallest, top_value):
    def one(axis_at, blocks):
        heights = jax.random.uniform(jax.random.fold_in(jax.random.fold_in(own_key, 6), axis_at), (blocks,), jnp.float32, smallest / len(cuts), top_value / len(cuts))
        return jnp.repeat(jnp.exp(heights), dims[axis_at] // blocks).reshape((-1,) + (1,) * (len(dims) - axis_at - 1))

    level = one(*cuts[0])
    for cut in cuts[1:]:
        level = level * one(*cut)
    return level


def profile(count, total, bound, slope):
    loads = [(1 << 20) // math.isqrt(grade ** slope) + 1 for grade in range(2, count + 1)]
    rest, counts = total - bound - (count - 1), [1] * (count - 1)
    while rest > 0:
        free = [i for i in range(count - 1) if counts[i] < bound]
        whole, left = sum([loads[i] for i in free]), rest
        for i in free:
            more = min(bound - counts[i], max(1, left * loads[i] // whole), rest)
            counts[i] = counts[i] + more
            rest = rest - more
    return np.array([bound] + counts)


def uneven(own_key, amount, total, limit, lean):
    if amount == 2:
        one = jax.random.randint(own_key, (), max(1, total - limit), min(limit, total - 1) + 1)
        return jnp.stack([one, total - one])
    sizes = jnp.asarray(profile(amount, total, limit, lean), jnp.int32)
    twos = (amount - 1) // 2
    donor, sink = sizes[1:1 + 2 * twos:2], sizes[2:2 + 2 * twos:2]
    margin = jnp.minimum(donor - 1, limit - sink)
    moved = jax.random.randint(jax.random.fold_in(own_key, 1), (twos,), 0, 1 << 20) % (margin + 1)
    sizes = sizes.at[1:1 + 2 * twos:2].set(donor - moved).at[2:2 + 2 * twos:2].set(sink + moved)
    return sizes[jax.random.permutation(jax.random.fold_in(own_key, 2), amount)]


def scatter_about(own_key, extent, deviation, most, split=(), kind=jnp.bfloat16):
    array = deviation * jax.random.normal(own_key, extent, jnp.float32)
    if split:
        array = array * levels(own_key, extent, split, -0.22, 0.18)
    return jnp.clip(array, -most, most).astype(kind)


def setup_inputs(seed: int = 0) -> dict:
    key_of = jax.random.split(jax.random.key(seed), 17)
    tokens = scatter_about(key_of[0], (MICRO, TOKEN_COUNT, D), 1.0, 6.0, ((1, 16), (2, 2)))
    cotangent = scatter_about(key_of[1], (MICRO, TOKEN_COUNT, D), 1.0, 6.0, ((1, 16), (2, 2)))
    seq_lengths = jax.vmap(lambda own: uneven(own, NSEQ, TOKEN_COUNT, LONGEST, 1))(jax.random.split(key_of[2], MICRO)).reshape((MICRO, NSEQ)).astype(jnp.int32)
    residue_mask = set_ends((jax.random.randint(key_of[3], (MICRO, TOKEN_COUNT), 0, 8) < 7).astype(jnp.int32), jax.random.fold_in(key_of[3], 1), 0, 1)
    first_gain = jnp.clip(1.0 + 0.15 * jax.random.normal(key_of[4], (D,), jnp.float32), 0.25, 1.75)
    first_shift = scatter_about(key_of[5], (D,), 0.3, 2.5, ((0, 2),), jnp.float32)
    proj_in = scatter_about(key_of[6], (D, INNER), D ** -0.5, 0.15625, ((0, 16), (1, 2)))
    in_bias = scatter_about(key_of[7], (INNER,), 0.3, 2.5, ((0, 2),), jnp.float32)
    mid_gain = jnp.clip(1.0 + 0.15 * jax.random.normal(key_of[8], (INNER,), jnp.float32), 0.25, 1.75)
    mid_shift = scatter_about(key_of[9], (INNER,), 0.3, 2.5, ((0, 2),), jnp.float32)
    conv_weight = scatter_about(key_of[10], (KERNEL_TAPS, INNER, INNER), (KERNEL_TAPS * INNER) ** -0.5, 0.109375, ((1, 16), (2, 2)))
    conv_bias = scatter_about(key_of[11], (INNER,), 0.3, 2.5, ((0, 2),), jnp.float32)
    last_gain = jnp.clip(1.0 + 0.15 * jax.random.normal(key_of[12], (INNER,), jnp.float32), 0.25, 1.75)
    last_shift = scatter_about(key_of[13], (INNER,), 0.3, 2.5, ((0, 2),), jnp.float32)
    proj_out = scatter_about(key_of[14], (INNER, D), INNER ** -0.5, 0.25, ((0, 2), (1, 16)))
    out_bias = scatter_about(key_of[15], (D,), 0.3, 2.5, ((0, 2),), jnp.float32)
    return dict(tokens=tokens, cotangent=cotangent, seq_lengths=seq_lengths, residue_mask=residue_mask, first_gain=first_gain, first_shift=first_shift, proj_in=proj_in, in_bias=in_bias, mid_gain=mid_gain, mid_shift=mid_shift, conv_weight=conv_weight, conv_bias=conv_bias, last_gain=last_gain, last_shift=last_shift, proj_out=proj_out, out_bias=out_bias)


@jax.custom_vjp
def low(v):
    return lax.optimization_barrier(v.astype(jnp.bfloat16)).astype(jnp.float32)

@jax.custom_vjp
def low_back(v):
    return v

def low_keep(v):
    return (low(v), None)

def low_pass(kept, grad):
    return (grad,)

def back_keep(v):
    return (v, None)

def back_low(kept, grad):
    return (low(grad),)
low.defvjp(low_keep, low_pass)
low_back.defvjp(back_keep, back_low)
EPSILON = 1e-05
ROOT_HALF = 0.7071067811865476

def gelu_value(value):
    return 0.5 * value * (1.0 + lax.erf(value * ROOT_HALF))

def norm_rows(value, gain, shift):
    middle = lax.optimization_barrier(jnp.mean(value, axis=-1, keepdims=True))
    centred = value - middle
    spread = lax.optimization_barrier(jnp.mean(centred * centred, axis=-1, keepdims=True))
    return centred * lax.rsqrt(spread + EPSILON) * gain + shift

def tap_table(lengths):
    bounds = jnp.cumsum(lengths).astype(jnp.int32)[:-1]
    starts = jnp.zeros((TOKEN_COUNT,), jnp.int32).at[bounds].add(1)
    sequence_segment = jnp.cumsum(starts).astype(jnp.int32)
    padded_rows = jnp.pad(sequence_segment, (HALO, HALO), constant_values=-1)
    return [(padded_rows[tap_index * DILATION_STEP:tap_index * DILATION_STEP + TOKEN_COUNT] == sequence_segment).astype(jnp.float32) for tap_index in range(KERNEL_TAPS)]

def reference(tokens, cotangent, seq_lengths, residue_mask, first_gain, first_shift, proj_in, in_bias, mid_gain, mid_shift, conv_weight, conv_bias, last_gain, last_shift, proj_out, out_bias):
    high = lax.Precision.HIGHEST
    tables = [tap_table(seq_lengths[index]) for index in range(MICRO)]

    def forward(values, gain_one, shift_one, weight_in, bias_in, gain_two, shift_two, weight_conv, bias_conv, gain_three, shift_three, weight_out, bias_out):
        results = []
        for index in range(MICRO):
            keep_mask = residue_mask[index].astype(jnp.float32)[:, None]
            act_one = low(gelu_value(norm_rows(values[index], gain_one, shift_one)))
            hidden_one = low_back(jnp.dot(act_one, weight_in, precision=high) + bias_in)
            act_two = low(gelu_value(norm_rows(hidden_one, gain_two, shift_two)) * keep_mask)
            framed_rows = jnp.pad(act_two, ((HALO, HALO), (0, 0)))
            hidden_three = jnp.zeros((TOKEN_COUNT, INNER), jnp.float32) + bias_conv
            for tap_index in range(KERNEL_TAPS):
                sliding_window = framed_rows[tap_index * DILATION_STEP:tap_index * DILATION_STEP + TOKEN_COUNT]
                hidden_three = hidden_three + tables[index][tap_index][:, None] * jnp.dot(sliding_window, weight_conv[tap_index], precision=high)
            hidden_three = low_back(hidden_three)
            act_three = low(gelu_value(norm_rows(hidden_three, gain_three, shift_three)))
            results.append(values[index] + jnp.dot(act_three, weight_out, precision=high) + bias_out)
        return jnp.stack(results, 0)
    floats = (tokens.astype(jnp.float32), first_gain, first_shift, proj_in.astype(jnp.float32), in_bias, mid_gain, mid_shift, conv_weight.astype(jnp.float32), conv_bias, last_gain, last_shift, proj_out.astype(jnp.float32), out_bias)
    output, pullback = jax.vjp(forward, *floats)
    grads = pullback(cotangent.astype(jnp.float32))
    return (output.astype(jnp.bfloat16), grads[0], grads[1], grads[2], grads[3], grads[4], grads[5], grads[6], grads[7], grads[8], grads[9], grads[10], grads[11], grads[12])
```

```python
import jax
import jax.numpy as jnp
from jax import lax
from jax.sharding import PartitionSpec as P

KERNEL_TAPS = 5
DILATION_STEP = 32
HALO = 64

EPSILON = 1e-05
ROOT_HALF = 0.7071067811865476
ROOT_TAU = 0.3989422804014327
SWAP = [(0, 1), (1, 0)]


def gelu_both(value):
    half = 0.5 * (1.0 + lax.erf(value * ROOT_HALF))
    return value * half, half + value * jnp.exp(-0.5 * value * value) * ROOT_TAU


def norm(value, gain, shift):
    middle = jnp.mean(value, axis=1, keepdims=True)
    centred = value - middle
    scale = lax.rsqrt(jnp.mean(centred * centred, axis=1, keepdims=True) + EPSILON)
    normed = centred * scale
    return normed, scale, normed * gain + shift


def norm_back(grad_zed, normed, scale, gain):
    grad_normed = grad_zed * gain
    first = jnp.mean(grad_normed, axis=1, keepdims=True)
    second = jnp.mean(grad_normed * normed, axis=1, keepdims=True)
    grad_value = scale * (grad_normed - first - normed * second)
    return grad_value, jnp.sum(grad_zed * normed, axis=0), jnp.sum(grad_zed, axis=0)


def dot(left, right, over=((1,), (0,))):
    return lax.dot_general(left, right, (over, ((), ())), preferred_element_type=jnp.float32)


def framed(block, width):
    count = lax.axis_size("seq")
    forward = [(i, i + 1) for i in range(count - 1)]
    backward = [(i + 1, i) for i in range(count - 1)]
    low = lax.ppermute(block[block.shape[0] - width :], "seq", forward)
    high = lax.ppermute(block[:width], "seq", backward)
    return jnp.concatenate([low, block, high], axis=0)


def windows(block, taps, rows):
    return jnp.concatenate(
        [
            block[tap * DILATION_STEP : tap * DILATION_STEP + rows] * taps[tap]
            for tap in range(KERNEL_TAPS)
        ],
        axis=1,
    )


def body(
    tokens,
    cotangent,
    seq_lengths,
    residue_mask,
    first_gain,
    first_shift,
    proj_in,
    in_bias,
    mid_gain,
    mid_shift,
    conv_weight,
    conv_bias,
    last_gain,
    last_shift,
    proj_out,
    out_bias,
):
    micro, rows, half = tokens.shape
    inner_half = in_bias.shape[0]
    inner = 2 * inner_half
    side = lax.axis_index("ch")
    low_side = side == 0

    def swap(value):
        return lax.ppermute(value, "ch", SWAP)

    def whole(own, other, axis):
        return jnp.where(
            low_side,
            jnp.concatenate([own, other], axis=axis),
            jnp.concatenate([other, own], axis=axis),
        )

    def own_of(value):
        return lax.dynamic_index_in_dim(value, side, 0, keepdims=False)

    def other_of(value):
        return lax.dynamic_index_in_dim(value, 1 - side, 0, keepdims=False)

    def halves(value, width):
        left, right = value[:, :width], value[:, width:]
        return jnp.where(low_side, left, right), jnp.where(low_side, right, left)

    weight_in = lax.all_gather(whole(proj_in, swap(proj_in), 1), "seq", axis=0, tiled=True)
    weight_conv = lax.all_gather(whole(conv_weight, swap(conv_weight), 2), "seq", axis=1, tiled=True)
    weight_out = lax.all_gather(whole(proj_out, swap(proj_out), 0), "seq", axis=1, tiled=True)
    vectors = lax.all_gather(
        jnp.concatenate(
            [first_gain, first_shift, out_bias, in_bias, mid_gain, mid_shift, conv_bias, last_gain, last_shift]
        ),
        "ch",
        axis=0,
        tiled=False,
    )
    wide = [vectors[:, i * half : (i + 1) * half].reshape(-1) for i in range(3)]
    narrow = [
        vectors[:, 3 * half + i * inner_half : 3 * half + (i + 1) * inner_half].reshape(-1) for i in range(6)
    ]
    g1, b1, bias_out = wide
    bias_in, g2, b2, bias_conv, g3, b3 = narrow

    x = whole(own_of(tokens), swap(other_of(tokens)), 1).astype(jnp.float32)
    gy = whole(own_of(cotangent), swap(other_of(cotangent)), 1)

    places = lax.axis_index("seq") * rows + jnp.arange(rows + 2 * HALO, dtype=jnp.int32) - HALO
    inside = (places >= 0) & (places < rows * lax.axis_size("seq"))
    bounds = jnp.cumsum(own_of(seq_lengths))[:-1]
    segment = jnp.sum((places[:, None] >= bounds[None, :]).astype(jnp.int32), axis=1)
    segment = jnp.where(inside, segment, -1)
    middle = segment[HALO : HALO + rows]
    taps = [
        (segment[tap * DILATION_STEP : tap * DILATION_STEP + rows] == middle).astype(jnp.bfloat16)[:, None]
        for tap in range(KERNEL_TAPS)
    ]
    keep = own_of(residue_mask).astype(jnp.float32)[:, None]

    n1, r1, z1 = norm(x, g1, b1)
    a1, s1 = gelu_both(z1)
    a1 = a1.astype(jnp.bfloat16)
    h1 = dot(a1, weight_in) + bias_in
    n2, r2, z2 = norm(h1, g2, b2)
    a2, s2 = gelu_both(z2)
    a2 = framed((a2 * keep).astype(jnp.bfloat16), HALO)
    s2 = s2 * keep
    a_win = windows(a2, taps, rows)
    h3 = dot(a_win, weight_conv.reshape(KERNEL_TAPS * inner, inner)) + bias_conv
    n3, r3, z3 = norm(h3, g3, b3)
    a3, s3 = gelu_both(z3)
    a3 = a3.astype(jnp.bfloat16)
    out = (x + dot(a3, weight_out) + bias_out).astype(jnp.bfloat16)
    out_own, out_other = halves(out, half)
    out_back = swap(out_other)

    grad_out = dot(a3, gy, ((0,), (0,)))
    da3 = dot(gy, weight_out, ((1,), (1,)))
    dh3, grad_g3, grad_b3 = norm_back(da3 * s3, n3, r3, g3)
    dh3 = dh3.astype(jnp.bfloat16)
    d_win = windows(framed(dh3, HALO), taps, rows)
    grad_conv = dot(a_win, dh3, ((0,), (0,))).reshape(KERNEL_TAPS, inner, inner)
    flipped = jnp.flip(weight_conv, 0).transpose(0, 2, 1).reshape(KERNEL_TAPS * inner, inner)
    da2 = dot(d_win, flipped)
    dh1, grad_g2, grad_b2 = norm_back(da2 * s2, n2, r2, g2)
    dh1 = dh1.astype(jnp.bfloat16)
    grad_in = dot(a1, dh1, ((0,), (0,)))
    da1 = dot(dh1, weight_in, ((1,), (1,)))
    dx, grad_g1, grad_b1 = norm_back(da1 * s1, n1, r1, g1)
    dx_own, dx_other = halves(dx, half)
    dx_back = swap(dx_other.astype(jnp.bfloat16))

    def placed(own, back):
        return jnp.where(low_side, jnp.stack([own, back], 0), jnp.stack([back, own], 0))

    block_out = placed(out_own, out_back)
    grad_tokens = placed(dx_own, dx_back.astype(jnp.float32)) + cotangent.astype(jnp.float32)

    def owned(value, seq_dim, ch_dim):
        part = lax.psum_scatter(value, "seq", scatter_dimension=seq_dim, tiled=True)
        return lax.psum_scatter(part, "ch", scatter_dimension=ch_dim, tiled=True)

    smalls = [
        grad_g1,
        grad_b1,
        jnp.sum(gy.astype(jnp.float32), axis=0),
        jnp.sum(dh1.astype(jnp.float32), axis=0),
        grad_g2,
        grad_b2,
        jnp.sum(dh3.astype(jnp.float32), axis=0),
        grad_g3,
        grad_b3,
    ]
    totals = lax.psum(jnp.concatenate([small.reshape(2, -1) for small in smalls], axis=1), ("seq", "ch"))
    totals = lax.dynamic_index_in_dim(totals, side, 0, keepdims=False)
    sizes = [half] * 3 + [inner_half] * 6
    parts = []
    at = 0
    for size in sizes:
        parts.append(totals[at : at + size])
        at += size
    return (
        block_out,
        grad_tokens,
        parts[0],
        parts[1],
        owned(grad_in, 0, 1),
        parts[3],
        parts[4],
        parts[5],
        owned(grad_conv, 1, 2),
        parts[6],
        parts[7],
        parts[8],
        owned(grad_out, 1, 0),
        parts[2],
    )


def solution(mesh):
    placed = (
        P(None, "seq", "ch"),
        P(None, "seq", "ch"),
        P(),
        P(None, "seq"),
        P("ch"),
        P("ch"),
        P("seq", "ch"),
        P("ch"),
        P("ch"),
        P("ch"),
        P(None, "seq", "ch"),
        P("ch"),
        P("ch"),
        P("ch"),
        P("ch", "seq"),
        P("ch"),
    )
    return jax.shard_map(
        body,
        mesh=mesh,
        in_specs=placed,
        out_specs=(
            P(None, "seq", "ch"),
            P(None, "seq", "ch"),
            P("ch"),
            P("ch"),
            P("seq", "ch"),
            P("ch"),
            P("ch"),
            P("ch"),
            P(None, "seq", "ch"),
            P("ch"),
            P("ch"),
            P("ch"),
            P("ch", "seq"),
            P("ch"),
        ),
        check_vma=False,
    )
```

```python
import jax
import jax.numpy as jnp
from jax import lax
from jax.experimental import pallas as pl
from jax.experimental.pallas import tpu as pltpu
from jax.sharding import PartitionSpec as P

KERNEL_TAPS = 5
DILATION_STEP = 32
HALO = 64

EPSILON = 1e-05
ROOT_HALF = 0.7071067811865476
ROOT_TAU = 0.3989422804014327
SWAP = [(0, 1), (1, 0)]


def gelu_both(value):
    half = 0.5 * (1.0 + lax.erf(value * ROOT_HALF))
    return value * half, half + value * jnp.exp(-0.5 * value * value) * ROOT_TAU


def norm(value):
    middle = jnp.mean(value, axis=1, keepdims=True)
    centred = value - middle
    scale = lax.rsqrt(jnp.mean(centred * centred, axis=1, keepdims=True) + EPSILON)
    return centred * scale, scale


def norm_back(grad_zed, normed, scale, gain):
    grad_normed = grad_zed * gain
    first = jnp.mean(grad_normed, axis=1, keepdims=True)
    second = jnp.mean(grad_normed * normed, axis=1, keepdims=True)
    return scale * (grad_normed - first - normed * second)


def dot(left, right, over=((1,), (0,))):
    return lax.dot_general(left, right, (over, ((), ())), preferred_element_type=jnp.float32)


def column_sums(value):
    return jnp.sum(value, axis=0, keepdims=True)


def ordered(side, own, other):
    low = side == 0
    own, other = own.astype(jnp.float32), other.astype(jnp.float32)
    return jnp.where(low, own, other), jnp.where(low, other, own)


def windowed(framed_ref, taps, base, count):
    return jnp.concatenate(
        [
            framed_ref[pl.ds(base + tap * DILATION_STEP, count), :] * taps[:, tap : tap + 1]
            for tap in range(KERNEL_TAPS)
        ],
        axis=1,
    )


def first_kernel(side_ref, own_ref, other_ref, keep_ref, weight_ref, wide_ref, narrow_ref, a1_ref, s1_ref, h1_ref, a2_ref, s2_ref):
    x = jnp.concatenate(ordered(side_ref[0], own_ref[...], other_ref[...]), axis=1)
    normed, _ = norm(x)
    act, slope = gelu_both(normed * wide_ref[0:1, :] + wide_ref[1:2, :])
    act = act.astype(jnp.bfloat16)
    a1_ref[...] = act
    s1_ref[...] = slope
    h1 = dot(act, weight_ref[...]) + narrow_ref[0:1, :]
    h1_ref[...] = h1
    normed, _ = norm(h1)
    act, slope = gelu_both(normed * narrow_ref[1:2, :] + narrow_ref[2:3, :])
    keep = keep_ref[...]
    a2_ref[...] = (act * keep).astype(jnp.bfloat16)
    s2_ref[...] = slope * keep


def second_kernel(side_ref, own_ref, other_ref, taps_ref, framed_ref, conv_ref, weight_ref, wide_ref, narrow_ref, h3_ref, a3_ref, s3_ref, out_own_ref, out_other_ref):
    count = own_ref.shape[0]
    half = own_ref.shape[1]
    base = pl.multiple_of(pl.program_id(0) * count, count)
    h3 = dot(windowed(framed_ref, taps_ref[...], base, count), conv_ref[...]) + narrow_ref[3:4, :]
    h3_ref[...] = h3
    normed, _ = norm(h3)
    act, slope = gelu_both(normed * narrow_ref[4:5, :] + narrow_ref[5:6, :])
    act = act.astype(jnp.bfloat16)
    a3_ref[...] = act
    s3_ref[...] = slope
    mixed = dot(act, weight_ref[...], ((1,), (1,))) + wide_ref[2:3, :]
    left, right = mixed[:, :half], mixed[:, half:]
    low = side_ref[0] == 0
    out_own_ref[...] = (own_ref[...].astype(jnp.float32) + jnp.where(low, left, right)).astype(jnp.bfloat16)
    out_other_ref[...] = (other_ref[...].astype(jnp.float32) + jnp.where(low, right, left)).astype(jnp.bfloat16)


def third_kernel(side_ref, own_ref, other_ref, h3_ref, s3_ref, weight_ref, narrow_ref, dh3_ref, gy_ref, wide_sum_ref, sum_ref):
    @pl.when(pl.program_id(0) == 0)
    def _():
        wide_sum_ref[...] = jnp.zeros_like(wide_sum_ref)
        sum_ref[...] = jnp.zeros_like(sum_ref)

    gy = jnp.concatenate(ordered(side_ref[0], own_ref[...], other_ref[...]), axis=1)
    wide_sum_ref[0:1, :] += column_sums(gy)
    gy = gy.astype(jnp.bfloat16)
    gy_ref[...] = gy
    dz3 = dot(gy, weight_ref[...]) * s3_ref[...]
    normed, scale = norm(h3_ref[...])
    dh3 = norm_back(dz3, normed, scale, narrow_ref[4:5, :]).astype(jnp.bfloat16)
    dh3_ref[...] = dh3
    sum_ref[0:1, :] += column_sums(dh3.astype(jnp.float32))
    sum_ref[1:2, :] += column_sums(dz3 * normed)
    sum_ref[2:3, :] += column_sums(dz3)


def fourth_kernel(side_ref, own_ref, other_ref, gy_own_ref, taps_ref, framed_ref, conv_ref, h1_ref, s2_ref, s1_ref, weight_ref, wide_ref, narrow_ref, dh1_ref, dx_own_ref, dx_other_ref, wide_sum_ref, sum_ref):
    @pl.when(pl.program_id(0) == 0)
    def _():
        wide_sum_ref[...] = jnp.zeros_like(wide_sum_ref)
        sum_ref[...] = jnp.zeros_like(sum_ref)

    count = own_ref.shape[0]
    half = own_ref.shape[1]
    base = pl.multiple_of(pl.program_id(0) * count, count)
    dz2 = dot(windowed(framed_ref, taps_ref[...], base, count), conv_ref[...]) * s2_ref[...]
    normed, scale = norm(h1_ref[...])
    dh1 = norm_back(dz2, normed, scale, narrow_ref[1:2, :]).astype(jnp.bfloat16)
    dh1_ref[...] = dh1
    sum_ref[0:1, :] += column_sums(dh1.astype(jnp.float32))
    sum_ref[1:2, :] += column_sums(dz2 * normed)
    sum_ref[2:3, :] += column_sums(dz2)
    dz1 = dot(dh1, weight_ref[...], ((1,), (1,))) * s1_ref[...]
    x = jnp.concatenate(ordered(side_ref[0], own_ref[...], other_ref[...]), axis=1)
    normed, scale = norm(x)
    dx = norm_back(dz1, normed, scale, wide_ref[0:1, :])
    wide_sum_ref[0:1, :] += column_sums(dz1 * normed)
    wide_sum_ref[1:2, :] += column_sums(dz1)
    low = side_ref[0] == 0
    left, right = dx[:, :half], dx[:, half:]
    dx_own_ref[...] = jnp.where(low, left, right) + gy_own_ref[...].astype(jnp.float32)
    dx_other_ref[...] = jnp.where(low, right, left).astype(jnp.bfloat16)


def grad_kernel(left_ref, right_ref, out_ref):
    out_ref[...] = dot(left_ref[...], right_ref[...], ((0,), (0,)))


def conv_grad_kernel(framed_ref, taps_ref, right_ref, out_ref):
    tap = pl.program_id(0)
    count = right_ref.shape[0]
    base = pl.multiple_of(tap * DILATION_STEP, DILATION_STEP)
    left = framed_ref[pl.ds(base, count), :] * taps_ref[0]
    out_ref[0] = dot(left, right_ref[...], ((0,), (0,)))


VMEM_LIMIT = 56 * 2**20


def once(shape):
    return pl.BlockSpec(shape, lambda *_: (0,) * len(shape), pipeline_mode=pl.Buffered(1))


def by_rows(count, width):
    return pl.BlockSpec((count, width), lambda i, *_: (i, 0))


def row_call(kernel, side, rows, count, operands, outs, flops):
    in_specs = [by_rows(count, a.shape[1]) if how == "rows" else once(a.shape) for a, how in operands]
    out_specs = [
        by_rows(count, width) if how == "rows" else pl.BlockSpec((8, width), lambda i, *_: (0, 0))
        for width, _, how in outs
    ]
    out_shape = [
        jax.ShapeDtypeStruct((rows if how == "rows" else 8, width), dtype) for width, dtype, how in outs
    ]
    moved = sum(a.size * a.dtype.itemsize for a, _ in operands)
    moved += sum(o.size * o.dtype.itemsize for o in out_shape)
    return pl.pallas_call(
        kernel,
        grid_spec=pltpu.PrefetchScalarGridSpec(
            num_scalar_prefetch=1, grid=(rows // count,), in_specs=in_specs, out_specs=out_specs
        ),
        out_shape=out_shape,
        compiler_params=pltpu.CompilerParams(
            dimension_semantics=("arbitrary",), vmem_limit_bytes=VMEM_LIMIT
        ),
        cost_estimate=pl.CostEstimate(flops=flops // 32, bytes_accessed=moved // 32, transcendentals=0),
    )(side, *[a for a, _ in operands])


def matrix_grad(left, right, tiles):
    rows, height = left.shape
    width = right.shape[1]
    return pl.pallas_call(
        grad_kernel,
        grid=(tiles,),
        in_specs=[pl.BlockSpec((rows, height // tiles), lambda i: (0, i)), once((rows, width))],
        out_specs=pl.BlockSpec((height // tiles, width), lambda i: (i, 0)),
        out_shape=jax.ShapeDtypeStruct((height, width), jnp.float32),
        compiler_params=pltpu.CompilerParams(
            dimension_semantics=("arbitrary",), vmem_limit_bytes=VMEM_LIMIT
        ),
        cost_estimate=pl.CostEstimate(
            flops=rows * height * width // 16, bytes_accessed=rows * (height + width) // 16, transcendentals=0
        ),
    )(left, right)


def conv_grad(framed_rows, taps, right):
    rows, width = right.shape
    return pl.pallas_call(
        conv_grad_kernel,
        grid=(KERNEL_TAPS,),
        in_specs=[
            once(framed_rows.shape),
            pl.BlockSpec((1, rows, 1), lambda i: (i, 0, 0)),
            once((rows, width)),
        ],
        out_specs=pl.BlockSpec((1, width, width), lambda i: (i, 0, 0)),
        out_shape=jax.ShapeDtypeStruct((KERNEL_TAPS, width, width), jnp.float32),
        compiler_params=pltpu.CompilerParams(
            dimension_semantics=("arbitrary",), vmem_limit_bytes=VMEM_LIMIT
        ),
        cost_estimate=pl.CostEstimate(
            flops=KERNEL_TAPS * rows * width * width // 16, bytes_accessed=rows * width // 8, transcendentals=0
        ),
    )(framed_rows, taps, right)


def framed(block, width):
    count = lax.axis_size("seq")
    forward = [(i, i + 1) for i in range(count - 1)]
    backward = [(i + 1, i) for i in range(count - 1)]
    low = lax.ppermute(block[block.shape[0] - width :], "seq", forward)
    high = lax.ppermute(block[:width], "seq", backward)
    return jnp.concatenate([low, block, high], axis=0)


def scattered(value, order):
    count = lax.axis_size("seq")
    place = lax.axis_index("seq")
    bits = count.bit_length() - 1
    value = value.reshape((2,) * bits + value.shape[1:])
    left = list(range(bits))
    for bit in order:
        dim = left.index(bits - 1 - bit)
        left.remove(bits - 1 - bit)
        mine = (place >> bit) & 1
        keep = lax.dynamic_index_in_dim(value, mine, dim, keepdims=False)
        send = lax.dynamic_index_in_dim(value, 1 - mine, dim, keepdims=False).astype(jnp.bfloat16)
        came = lax.ppermute(send, "seq", [(i, i ^ (1 << bit)) for i in range(count)])
        value = keep + came.astype(jnp.float32)
    return value


def body(
    tokens,
    cotangent,
    seq_lengths,
    residue_mask,
    first_gain,
    first_shift,
    proj_in,
    in_bias,
    mid_gain,
    mid_shift,
    conv_weight,
    conv_bias,
    last_gain,
    last_shift,
    proj_out,
    out_bias,
):
    micro, rows, half = tokens.shape
    inner_half = in_bias.shape[0]
    inner = 2 * inner_half
    model = 2 * half
    seq_count = lax.axis_size("seq")
    count = 256
    side = lax.axis_index("ch")
    side_array = side.astype(jnp.int32).reshape(1)
    low_side = side == 0

    def swap(value):
        return lax.ppermute(value, "ch", SWAP)

    def whole(own, other, axis):
        return jnp.where(
            low_side,
            jnp.concatenate([own, other], axis=axis),
            jnp.concatenate([other, own], axis=axis),
        )

    def own_of(value):
        return lax.dynamic_index_in_dim(value, side, 0, keepdims=False)

    def other_of(value):
        return lax.dynamic_index_in_dim(value, 1 - side, 0, keepdims=False)

    own_vectors = jnp.concatenate(
        [first_gain, first_shift, out_bias, in_bias, mid_gain, mid_shift, conv_bias, last_gain, last_shift]
    )
    part_in = proj_in.shape[0]
    part_conv = conv_weight.shape[1]
    own_weights = jnp.concatenate(
        [proj_in, proj_out.T, conv_weight.reshape(KERNEL_TAPS * part_conv, inner_half)], axis=0
    )
    own_vectors, own_weights = lax.optimization_barrier((own_vectors, own_weights))
    other_vectors, other_weights = swap(own_vectors), swap(own_weights)
    tokens_tied, other_vectors, other_weights = lax.optimization_barrier(
        (other_of(tokens), other_vectors, other_weights)
    )
    both = whole(own_weights, other_weights, 1)
    vectors = jnp.where(
        low_side, jnp.stack([own_vectors, other_vectors]), jnp.stack([other_vectors, own_vectors])
    )
    x_own = own_of(tokens)
    x_other = swap(tokens_tied)
    gy_own = own_of(cotangent)
    gy_tied, _ = lax.optimization_barrier((other_of(cotangent), x_other))
    gy_other = swap(gy_tied)

    gathered = lax.all_gather(both, "seq", axis=0)
    weight_in = gathered[:, :part_in].reshape(model, inner)
    weight_out = gathered[:, part_in : 2 * part_in].reshape(model, inner)
    weight_conv = (
        gathered[:, 2 * part_in :]
        .reshape(seq_count, KERNEL_TAPS, part_conv, inner)
        .transpose(1, 0, 2, 3)
        .reshape(KERNEL_TAPS, inner, inner)
    )
    wide = jnp.stack([vectors[:, i * half : (i + 1) * half].reshape(-1) for i in range(3)])
    narrow = jnp.stack(
        [
            vectors[:, 3 * half + i * inner_half : 3 * half + (i + 1) * inner_half].reshape(-1)
            for i in range(6)
        ]
    )

    places = lax.axis_index("seq") * rows + jnp.arange(rows + 2 * HALO, dtype=jnp.int32) - HALO
    inside = (places >= 0) & (places < rows * seq_count)
    bounds = jnp.cumsum(own_of(seq_lengths))[:-1]
    segment = jnp.sum((places[:, None] >= bounds[None, :]).astype(jnp.int32), axis=1)
    segment = jnp.where(inside, segment, -1)
    middle = segment[HALO : HALO + rows]
    tap_list = [
        (segment[tap * DILATION_STEP : tap * DILATION_STEP + rows] == middle).astype(jnp.bfloat16)
        for tap in range(KERNEL_TAPS)
    ]
    taps = jnp.stack(tap_list, axis=1)
    keep = own_of(residue_mask).astype(jnp.float32)[:, None]
    f32, bf16 = jnp.float32, jnp.bfloat16
    product = 2 * rows * model * inner

    a1, s1, h1, a2, s2 = row_call(
        first_kernel,
        side_array,
        rows,
        count,
        [(x_own, "rows"), (x_other, "rows"), (keep, "rows"), (weight_in, "once"), (wide, "once"), (narrow, "once")],
        [(model, bf16, "rows"), (model, f32, "rows"), (inner, f32, "rows"), (inner, bf16, "rows"), (inner, f32, "rows")],
        product,
    )
    a2 = framed(a2, HALO)
    h3, a3, s3, out_own, out_other = row_call(
        second_kernel,
        side_array,
        rows,
        count,
        [
            (x_own, "rows"),
            (x_other, "rows"),
            (taps, "rows"),
            (a2, "once"),
            (weight_conv.reshape(KERNEL_TAPS * inner, inner), "once"),
            (weight_out, "once"),
            (wide, "once"),
            (narrow, "once"),
        ],
        [(inner, f32, "rows"), (inner, bf16, "rows"), (inner, f32, "rows"), (half, bf16, "rows"), (half, bf16, "rows")],
        4 * product,
    )
    out_back = swap(out_other)

    dh3, gy, wide_sum_3, sum_3 = row_call(
        third_kernel,
        side_array,
        rows,
        count,
        [(gy_own, "rows"), (gy_other, "rows"), (h3, "rows"), (s3, "rows"), (weight_out, "once"), (narrow, "once")],
        [(inner, bf16, "rows"), (model, bf16, "rows"), (model, f32, "sum"), (inner, f32, "sum")],
        product,
    )
    dh3_framed = framed(dh3, HALO)
    grad_out = matrix_grad(gy, a3, 2)
    grad_conv = conv_grad(a2, jnp.stack(tap_list, axis=0)[:, :, None], dh3)
    dh3_framed, out_back = lax.optimization_barrier((dh3_framed, out_back))
    flipped = jnp.flip(weight_conv, 0).transpose(0, 2, 1).reshape(KERNEL_TAPS * inner, inner)
    dh1, dx_own, dx_other, wide_sum_1, sum_1 = row_call(
        fourth_kernel,
        side_array,
        rows,
        count,
        [
            (x_own, "rows"),
            (x_other, "rows"),
            (gy_own, "rows"),
            (taps, "rows"),
            (dh3_framed, "once"),
            (flipped, "once"),
            (h1, "rows"),
            (s2, "rows"),
            (s1, "rows"),
            (weight_in, "once"),
            (wide, "once"),
            (narrow, "once"),
        ],
        [(inner, bf16, "rows"), (half, f32, "rows"), (half, bf16, "rows"), (model, f32, "sum"), (inner, f32, "sum")],
        4 * product,
    )
    dx_back = swap(dx_other)
    grad_in = matrix_grad(a1, dh1, 2)

    def placed(own, back):
        return jnp.where(low_side, jnp.stack([own, back], 0), jnp.stack([back, own], 0))

    block_out = placed(out_own, out_back)
    grad_tokens = placed(
        dx_own, dx_back.astype(f32) + other_of(cotangent).astype(f32)
    )

    bits = list(range(seq_count.bit_length() - 1))
    swapped_bits = [bits[0]] + bits[2:] + [bits[1]]
    part = jnp.concatenate(
        [
            scattered(grad_in.reshape(seq_count, part_in, inner), bits),
            scattered(grad_out.reshape(seq_count, part_in, inner), swapped_bits),
            scattered(
                grad_conv.reshape(KERNEL_TAPS, seq_count, part_conv, inner).transpose(1, 0, 2, 3), bits
            ).reshape(KERNEL_TAPS * part_conv, inner),
        ],
        axis=0,
    )
    left, right = part[:, :inner_half], part[:, inner_half:]
    part_other = swap(jnp.where(low_side, right, left).astype(bf16))
    part = jnp.where(low_side, left, right) + part_other.astype(f32)

    smalls = jnp.concatenate(
        [
            small.reshape(2, -1)
            for small in (wide_sum_1[0], wide_sum_1[1], wide_sum_3[0], sum_1[0], sum_1[1], sum_1[2], sum_3[0], sum_3[1], sum_3[2])
        ],
        axis=1,
    )
    totals = smalls
    for bit in bits:
        totals = totals + lax.ppermute(totals, "seq", [(i, i ^ (1 << bit)) for i in range(seq_count)])
    totals = own_of(totals) + swap(other_of(totals))
    sizes = [half] * 3 + [inner_half] * 6
    parts = []
    at = 0
    for size in sizes:
        parts.append(totals[at : at + size])
        at += size
    return (
        block_out,
        grad_tokens,
        parts[0],
        parts[1],
        part[:part_in],
        parts[3],
        parts[4],
        parts[5],
        part[2 * part_in :].reshape(KERNEL_TAPS, part_conv, inner_half),
        parts[6],
        parts[7],
        parts[8],
        part[part_in : 2 * part_in].T,
        parts[2],
    )


BLOCK = 256
CHUNKS = 4
CONV_PAD = 8


def fast_kernel(
    tokens, x_other, cot, masks, w_in, w_out, w_conv, wide, narrow,
    out_own, out_back, dx_own, dx_back, grads, smalls,
    gy_other, out_send, dx_send, s1, h1, s2, h3, s3,
    a1v, a2f, a3v, gyv, dh3f,
    k_in, s_in, r0_in, r1_in, r2_in, r3_in,
    k_out, s_out, r0_out, r1_out, r2_out, r3_out,
    k_conv, s_conv, r0_conv, r1_conv, r2_conv, r3_conv,
    cross_send, cross_recv, small_send, small_recv,
    gy_sems, out_sems, dx_sems, a2_sems, dh3_sems, in_sems, out_rs_sems, conv_sems, cross_sems, small_sems,
):
    rows = a1v.shape[0]
    half = tokens.shape[2]
    inner = narrow.shape[1]
    part = rows // CHUNKS
    side = lax.axis_index("ch")
    place = lax.axis_index("seq")
    last = lax.axis_size("seq") - 1
    low = side == 0
    bits = [lax.rem(place // (1 << bit), 2) for bit in range(4)]
    across = {"ch": 1 - side}
    pairs = [{"seq": place + (1 << bit) * (1 - 2 * bits[bit])} for bit in range(4)]
    before, after = {"seq": place - 1}, {"seq": place + 1}

    def remote(src, dst, sems, at, device):
        return pltpu.make_async_remote_copy(
            src_ref=src,
            dst_ref=dst,
            send_sem=sems.at[0, at],
            recv_sem=sems.at[1, at],
            device_id=device,
            device_id_type=pl.DeviceIdType.MESH,
        )

    def chunk(ref, at):
        return ref.at[pl.ds(pl.multiple_of(at * part, part), part)]

    def gy_copy(at):
        return remote(chunk(cot.at[1 - side], at), chunk(gy_other, at), gy_sems, at, across)

    def out_copy(at):
        return remote(chunk(out_send, at), chunk(out_back, at), out_sems, at, across)

    def dx_copy(at):
        return remote(chunk(dx_send, at), chunk(dx_back, at), dx_sems, at, across)

    def halo_low(framed_rows, sems):
        return remote(framed_rows.at[pl.ds(HALO, HALO)], framed_rows.at[pl.ds(HALO + rows, HALO)], sems, 0, before)

    def halo_high(framed_rows, sems):
        return remote(framed_rows.at[pl.ds(rows, HALO)], framed_rows.at[pl.ds(0, HALO)], sems, 1, after)

    def halo_start(framed_rows, sems):
        @pl.when(place > 0)
        def _():
            halo_low(framed_rows, sems).start()

        @pl.when(place < last)
        def _():
            halo_high(framed_rows, sems).start()

    def halo_wait(framed_rows, sems):
        @pl.when(place > 0)
        def _():
            halo_low(framed_rows, sems).wait_send()
            halo_high(framed_rows, sems).wait_recv()

        @pl.when(place < last)
        def _():
            halo_high(framed_rows, sems).wait_send()
            halo_low(framed_rows, sems).wait_recv()

    def middle_first(step):
        late = step // 2
        return (step + 1) * (1 - late) + late * (step - 2) * 3

    def pipeline(step, blocks, ins, outs):
        def spec(ref):
            return pl.BlockSpec((BLOCK, ref.shape[-1]), lambda i: (i, 0))

        pltpu.emit_pipeline(
            step, grid=(blocks,), in_specs=[spec(r) for r in ins], out_specs=[spec(r) for r in outs]
        )(*ins, *outs)

    barrier = pltpu.get_barrier_semaphore()
    ring = [{"seq": lax.rem(place + last, last + 1)}, {"seq": lax.rem(place + 1, last + 1)}]
    for device in [across] + pairs + ring:
        pl.semaphore_signal(barrier, inc=1, device_id=device, device_id_type=pl.DeviceIdType.MESH)
    pl.semaphore_wait(barrier, 7)

    for at in range(CHUNKS):
        gy_copy(at).start()
    smalls[...] = jnp.zeros_like(smalls)

    @pl.when(place == 0)
    def _():
        a2f[0:HALO, :] = jnp.zeros((HALO, inner), jnp.bfloat16)
        dh3f[0:HALO, :] = jnp.zeros((HALO, inner), jnp.bfloat16)

    @pl.when(place == last)
    def _():
        a2f[HALO + rows :, :] = jnp.zeros((HALO, inner), jnp.bfloat16)
        dh3f[HALO + rows :, :] = jnp.zeros((HALO, inner), jnp.bfloat16)

    def first(own, other, s1_block, h1_block, s2_block):
        base = pl.multiple_of(pl.program_id(0) * BLOCK, BLOCK)
        x = jnp.concatenate(ordered(side, own[...], other[...]), axis=1)
        normed, _ = norm(x)
        act, slope = gelu_both(normed * wide[0:1, :] + wide[1:2, :])
        act = act.astype(jnp.bfloat16)
        a1v[pl.ds(base, BLOCK), :] = act
        s1_block[...] = slope
        value = dot(act, w_in[...]) + narrow[0:1, :]
        h1_block[...] = value
        normed, _ = norm(value)
        act, slope = gelu_both(normed * narrow[1:2, :] + narrow[2:3, :])
        keep = masks[pl.ds(base, BLOCK), KERNEL_TAPS : KERNEL_TAPS + 1].astype(jnp.float32)
        a2f[pl.ds(HALO + base, BLOCK), :] = (act * keep).astype(jnp.bfloat16)
        s2_block[...] = slope * keep

    pipeline(first, rows // BLOCK, [tokens.at[side], x_other], [s1, h1, s2])
    halo_start(a2f, a2_sems)

    def forward_chunk(step, _):
        at = middle_first(step)

        @pl.when(step == 2)
        def _():
            halo_wait(a2f, a2_sems)

        def second(own, other, h3_block, s3_block, own_block, other_block):
            base = pl.multiple_of(at * part + pl.program_id(0) * BLOCK, BLOCK)
            taps = masks[pl.ds(base, BLOCK), :]
            value = dot(windowed(a2f, taps, base, BLOCK), w_conv[...]) + narrow[3:4, :]
            h3_block[...] = value
            normed, _ = norm(value)
            act, slope = gelu_both(normed * narrow[4:5, :] + narrow[5:6, :])
            act = act.astype(jnp.bfloat16)
            a3v[pl.ds(base, BLOCK), :] = act
            s3_block[...] = slope
            mixed = dot(act, w_out[...], ((1,), (1,))) + wide[2:3, :]
            left, right = mixed[:, :half], mixed[:, half:]
            own_block[...] = (own[...].astype(jnp.float32) + jnp.where(low, left, right)).astype(jnp.bfloat16)
            other_block[...] = (other[...].astype(jnp.float32) + jnp.where(low, right, left)).astype(jnp.bfloat16)

        pipeline(
            second,
            part // BLOCK,
            [chunk(tokens.at[side], at), chunk(x_other, at)],
            [chunk(h3, at), chunk(s3, at), chunk(out_own, at), chunk(out_send, at)],
        )
        out_copy(at).start()
        return 0

    lax.fori_loop(0, CHUNKS, forward_chunk, 0)

    def add_small(row, value):
        smalls[row : row + 1, :] += value

    def add_wide(row, value):
        smalls[row : row + 1, :] += value[:, :half]
        smalls[row + 1 : row + 2, :] += value[:, half:]

    def third_chunk(at, _):
        gy_copy(at).wait_recv()

        def third(own, other, h3_block, s3_block):
            base = pl.multiple_of(at * part + pl.program_id(0) * BLOCK, BLOCK)
            gy = jnp.concatenate(ordered(side, own[...], other[...]), axis=1)
            add_wide(4, column_sums(gy))
            gy = gy.astype(jnp.bfloat16)
            gyv[pl.ds(base, BLOCK), :] = gy
            dz3 = dot(gy, w_out[...]) * s3_block[...]
            normed, scale = norm(h3_block[...])
            dh3 = norm_back(dz3, normed, scale, narrow[4:5, :]).astype(jnp.bfloat16)
            dh3f[pl.ds(HALO + base, BLOCK), :] = dh3
            add_small(9, column_sums(dh3.astype(jnp.float32)))
            add_small(10, column_sums(dz3 * normed))
            add_small(11, column_sums(dz3))

        pipeline(
            third,
            part // BLOCK,
            [chunk(cot.at[side], at), chunk(gy_other, at), chunk(h3, at), chunk(s3, at)],
            [],
        )
        return 0

    lax.fori_loop(0, CHUNKS, third_chunk, 0)
    halo_start(dh3f, dh3_sems)

    def split(keep_ref, send_ref, at, row, even, odd):
        height = even.shape[0]
        mine_first = bits[0] == 0
        keep_ref[at, row : row + height, :] = jnp.where(mine_first, even, odd)
        send_ref[at, row : row + height, :] = jnp.where(mine_first, odd, even).astype(jnp.bfloat16)

    def wide_grad(left_ref, right_ref, keep_ref, send_ref):
        height = keep_ref.shape[1]

        def tile(at, _):
            columns = pl.ds(pl.multiple_of(at * half, 128), half)
            value = dot(left_ref[:, columns], right_ref[...], ((0,), (0,)))
            for pair in range(half // (2 * height)):
                top = 2 * pair * height
                split(
                    keep_ref,
                    send_ref,
                    at * (half // (2 * height)) + pair,
                    0,
                    value[top : top + height],
                    value[top + height : top + 2 * height],
                )
            return 0

        lax.fori_loop(0, 2, tile, 0)

    def conv_grads():
        height = inner // 16
        right = dh3f.at[pl.ds(HALO, rows)]
        for taps in ((0, 1), (2, 3), (4,)):
            values = []
            for tap in taps:
                left = a2f[tap * DILATION_STEP : tap * DILATION_STEP + rows, :] * masks[:, tap : tap + 1]
                values.append(dot(left, right[...], ((0,), (0,))))
            if len(values) == 1:
                tail = [jnp.zeros((CONV_PAD, inner), jnp.float32)]
            else:
                tail = []
            for pair in range(8):
                top = 2 * pair * height
                even = jnp.concatenate([v[top : top + height] for v in values] + tail, axis=0)
                odd = jnp.concatenate([v[top + height : top + 2 * height] for v in values] + tail, axis=0)
                split(k_conv, s_conv, pair, taps[0] * height, even, odd)

    in_set = (k_in, s_in, (r0_in, r1_in, r2_in, r3_in), in_sems)
    out_set = (k_out, s_out, (r0_out, r1_out, r2_out, r3_out), out_rs_sems)
    conv_set = (k_conv, s_conv, (r0_conv, r1_conv, r2_conv, r3_conv), conv_sems)
    starts = (0, 0, 4, 6)
    lengths = (8, 4, 2, 1)

    def sum_copy(group, level):
        _, send, received, sems = group
        return remote(
            send.at[pl.ds(starts[level], lengths[level])], received[level], sems, level, pairs[level]
        )

    def sum_step(group, level):
        keep, send, received, _ = group
        sum_copy(group, level).wait()
        came = received[level]
        fixed = 0
        for bit in range(level):
            fixed = fixed + bits[bit + 1] * (1 << bit)
        if level == 3:
            keep[fixed] = keep[fixed] + came[0].astype(jnp.float32)
            return
        mine = bits[level + 1]

        def one(item, _):
            other = 2 * item + 1 - mine
            same = 2 * item + mine
            send[starts[level + 1] + item] = (
                keep[other * (1 << level) + fixed] + came[other].astype(jnp.float32)
            ).astype(jnp.bfloat16)
            at = same * (1 << level) + fixed
            keep[at] = keep[at] + came[same].astype(jnp.float32)
            return 0

        lax.fori_loop(0, lengths[level + 1], one, 0)
        sum_copy(group, level + 1).start()

    wide_grad(gyv, a3v, k_out, s_out)
    sum_copy(out_set, 0).start()
    conv_grads()
    sum_copy(conv_set, 0).start()
    sum_step(out_set, 0)
    halo_wait(dh3f, dh3_sems)

    def fourth_chunk(step, _):
        at = middle_first(step)

        def fourth(own, other, gy_own, h1_block, s2_block, s1_block, own_block, other_block):
            base = pl.multiple_of(at * part + pl.program_id(0) * BLOCK, BLOCK)
            taps = masks[pl.ds(base, BLOCK), :]
            da2 = jnp.zeros((BLOCK, inner), jnp.float32)
            for tap in range(KERNEL_TAPS):
                window = dh3f[pl.ds(base + tap * DILATION_STEP, BLOCK), :] * taps[:, tap : tap + 1]
                weight = w_conv[(KERNEL_TAPS - 1 - tap) * inner : (KERNEL_TAPS - tap) * inner, :]
                da2 = da2 + dot(window, weight, ((1,), (1,)))
            dz2 = da2 * s2_block[...]
            normed, scale = norm(h1_block[...])
            dh1 = norm_back(dz2, normed, scale, narrow[1:2, :]).astype(jnp.bfloat16)
            a3v[pl.ds(base, BLOCK), :] = dh1
            add_small(6, column_sums(dh1.astype(jnp.float32)))
            add_small(7, column_sums(dz2 * normed))
            add_small(8, column_sums(dz2))
            dz1 = dot(dh1, w_in[...], ((1,), (1,))) * s1_block[...]
            x = jnp.concatenate(ordered(side, own[...], other[...]), axis=1)
            normed, scale = norm(x)
            dx = norm_back(dz1, normed, scale, wide[0:1, :])
            add_wide(0, column_sums(dz1 * normed))
            add_wide(2, column_sums(dz1))
            left, right = dx[:, :half], dx[:, half:]
            own_block[...] = jnp.where(low, left, right) + gy_own[...].astype(jnp.float32)
            other_block[...] = jnp.where(low, right, left).astype(jnp.bfloat16)

        pipeline(
            fourth,
            part // BLOCK,
            [
                chunk(tokens.at[side], at),
                chunk(x_other, at),
                chunk(cot.at[side], at),
                chunk(h1, at),
                chunk(s2, at),
                chunk(s1, at),
            ],
            [chunk(dx_own, at), chunk(dx_send, at)],
        )
        dx_copy(at).start()
        for level in range(3):

            @pl.when(step == level)
            def _():
                sum_step(out_set, level + 1)
                sum_step(conv_set, level)

        return 0

    lax.fori_loop(0, CHUNKS, fourth_chunk, 0)

    wide_grad(a1v, a3v, k_in, s_in)
    sum_copy(in_set, 0).start()

    def small_copy(level):
        device = pairs[level] if level < 4 else across
        return remote(small_send.at[level], small_recv.at[level], small_sems, level, device)

    def small_start(level):
        small_send[level] = smalls[...]
        small_copy(level).start()

    def small_step(level):
        small_copy(level).wait()
        smalls[...] += small_recv[level]

    small_start(0)
    sum_step(conv_set, 3)
    for level in range(4):
        sum_step(in_set, level)
        small_step(level)
        small_start(level + 1)

    wanted = half // 2 + 64
    mine = 4 * bits[3] + 2 * bits[2] + bits[1]
    row = 0
    for keep in (k_in, k_out, k_conv):
        height = keep.shape[1]
        value = keep[mine]
        left, right = value[:, :wanted], value[:, inner - wanted :]
        grads[row : row + height, :] = jnp.where(low, left, right)
        cross_send[row : row + height, :] = jnp.where(low, right, left).astype(jnp.bfloat16)
        row += height
    cross = remote(cross_send, cross_recv, cross_sems, 0, across)
    cross.start()
    for at in range(CHUNKS):
        gy_copy(at).wait_send()
        out_copy(at).wait()
    small_step(4)
    cross.wait()
    grads[...] += cross_recv[...].astype(jnp.float32)
    for at in range(CHUNKS):
        dx_copy(at).wait()


def fast_call(tokens, x_other, cot, masks, w_in, w_out, w_conv, wide, narrow, part_in, part_conv):
    _, rows, half = tokens.shape
    model = 2 * half
    inner = narrow.shape[1]
    f32, bf16 = jnp.float32, jnp.bfloat16
    tall = KERNEL_TAPS * part_conv + CONV_PAD
    any_spec = pl.BlockSpec(memory_space=pl.ANY)
    vmem_spec = pl.BlockSpec(memory_space=pltpu.VMEM)
    total = 2 * part_in + tall
    wanted = half // 2 + 64

    def sums(height):
        return [pltpu.VMEM((8, height, inner), f32), pltpu.VMEM((8, height, inner), bf16)] + [
            pltpu.VMEM((length, height, inner), bf16) for length in (8, 4, 2, 1)
        ]

    def sems(count):
        return pltpu.SemaphoreType.DMA((2, count))

    shapes = [
        ((rows, half), bf16),
        ((rows, half), bf16),
        ((rows, half), f32),
        ((rows, half), bf16),
        ((total, wanted), f32),
        ((16, inner), f32),
        ((rows, half), bf16),
        ((rows, half), bf16),
        ((rows, half), bf16),
        ((rows, model), f32),
        ((rows, inner), f32),
        ((rows, inner), f32),
        ((rows, inner), f32),
        ((rows, inner), f32),
    ]
    flops = 6 * rows * (2 * model * inner + KERNEL_TAPS * inner * inner)
    results = pl.pallas_call(
        fast_kernel,
        out_shape=[jax.ShapeDtypeStruct(shape, dtype) for shape, dtype in shapes],
        in_specs=[any_spec] * 3 + [vmem_spec] * 6,
        out_specs=[any_spec] * 4 + [vmem_spec] * 2 + [any_spec] * 8,
        scratch_shapes=[
            pltpu.VMEM((rows, model), bf16),
            pltpu.VMEM((rows + 2 * HALO, inner), bf16),
            pltpu.VMEM((rows, inner), bf16),
            pltpu.VMEM((rows, model), bf16),
            pltpu.VMEM((rows + 2 * HALO, inner), bf16),
        ]
        + sums(part_in)
        + sums(part_in)
        + sums(tall)
        + [
            pltpu.VMEM((total, wanted), bf16),
            pltpu.VMEM((total, wanted), bf16),
            pltpu.VMEM((5, 16, inner), f32),
            pltpu.VMEM((5, 16, inner), f32),
            sems(CHUNKS),
            sems(CHUNKS),
            sems(CHUNKS),
            sems(2),
            sems(2),
            sems(4),
            sems(4),
            sems(4),
            sems(1),
            sems(5),
        ],
        compiler_params=pltpu.CompilerParams(
            collective_id=0, has_side_effects=True, vmem_limit_bytes=63 * 2**20
        ),
        cost_estimate=pl.CostEstimate(flops=flops, bytes_accessed=120 * 2**20, transcendentals=0),
    )(tokens, x_other, cot, masks, w_in, w_out, w_conv, wide, narrow)
    return results[:6]


def fast_body(
    tokens,
    cotangent,
    seq_lengths,
    residue_mask,
    first_gain,
    first_shift,
    proj_in,
    in_bias,
    mid_gain,
    mid_shift,
    conv_weight,
    conv_bias,
    last_gain,
    last_shift,
    proj_out,
    out_bias,
):
    micro, rows, half = tokens.shape
    inner_half = in_bias.shape[0]
    inner = 2 * inner_half
    model = 2 * half
    seq_count = lax.axis_size("seq")
    side = lax.axis_index("ch")
    low_side = side == 0
    f32, bf16 = jnp.float32, jnp.bfloat16

    def swap(value):
        return lax.ppermute(value, "ch", SWAP)

    def own_of(value):
        return lax.dynamic_index_in_dim(value, side, 0, keepdims=False)

    def other_of(value):
        return lax.dynamic_index_in_dim(value, 1 - side, 0, keepdims=False)

    own_vectors = jnp.concatenate(
        [first_gain, first_shift, out_bias, in_bias, mid_gain, mid_shift, conv_bias, last_gain, last_shift]
    )
    part_in = proj_in.shape[0]
    part_conv = conv_weight.shape[1]
    own_weights = jnp.concatenate(
        [proj_in, proj_out.T, conv_weight.reshape(KERNEL_TAPS * part_conv, inner_half)], axis=0
    )
    own_vectors, own_weights = lax.optimization_barrier((own_vectors, own_weights))
    other_vectors, other_weights = swap(own_vectors), swap(own_weights)
    tokens_tied, other_vectors, other_weights = lax.optimization_barrier(
        (other_of(tokens), other_vectors, other_weights)
    )
    both = jnp.where(
        low_side,
        jnp.concatenate([own_weights, other_weights], axis=1),
        jnp.concatenate([other_weights, own_weights], axis=1),
    )
    vectors = jnp.where(
        low_side, jnp.stack([own_vectors, other_vectors]), jnp.stack([other_vectors, own_vectors])
    )
    x_other = swap(tokens_tied)
    gathered = lax.all_gather(both, "seq", axis=0)
    weight_in = gathered[:, :part_in].reshape(model, inner)
    weight_out = gathered[:, part_in : 2 * part_in].reshape(model, inner)
    weight_conv = (
        gathered[:, 2 * part_in :]
        .reshape(seq_count, KERNEL_TAPS, part_conv, inner)
        .transpose(1, 0, 2, 3)
        .reshape(KERNEL_TAPS * inner, inner)
    )
    wide = jnp.stack([vectors[:, i * half : (i + 1) * half].reshape(-1) for i in range(3)])
    narrow = jnp.stack(
        [
            vectors[:, 3 * half + i * inner_half : 3 * half + (i + 1) * inner_half].reshape(-1)
            for i in range(6)
        ]
    )

    places = lax.axis_index("seq") * rows + jnp.arange(rows + 2 * HALO, dtype=jnp.int32) - HALO
    inside = (places >= 0) & (places < rows * seq_count)
    bounds = jnp.cumsum(own_of(seq_lengths))[:-1]
    segment = jnp.sum((places[:, None] >= bounds[None, :]).astype(jnp.int32), axis=1)
    segment = jnp.where(inside, segment, -1)
    middle = segment[HALO : HALO + rows]
    columns = [
        (segment[tap * DILATION_STEP : tap * DILATION_STEP + rows] == middle).astype(bf16)
        for tap in range(KERNEL_TAPS)
    ]
    zero = jnp.zeros((rows,), bf16)
    masks = jnp.stack(columns + [own_of(residue_mask).astype(bf16), zero, zero], axis=1)

    out_own, out_back, dx_own, dx_back, grads, smalls = fast_call(
        tokens, x_other, cotangent, masks, weight_in, weight_out, weight_conv, wide, narrow, part_in, part_conv
    )

    def placed(own, back):
        return jnp.where(low_side, jnp.stack([own, back], 0), jnp.stack([back, own], 0))

    block_out = placed(out_own, out_back)
    grad_tokens = placed(dx_own, dx_back.astype(f32) + other_of(cotangent).astype(f32))
    grads = jnp.where(low_side, grads[:, :inner_half], grads[:, grads.shape[1] - inner_half :])

    def wide_part(row):
        return lax.dynamic_index_in_dim(smalls, row + side, 0, keepdims=False)

    def narrow_part(row):
        return lax.dynamic_slice_in_dim(smalls[row], side * inner_half, inner_half, 0)

    return (
        block_out,
        grad_tokens,
        wide_part(0),
        wide_part(2),
        grads[:part_in],
        narrow_part(6),
        narrow_part(7),
        narrow_part(8),
        grads[2 * part_in : 2 * part_in + KERNEL_TAPS * part_conv].reshape(KERNEL_TAPS, part_conv, inner_half),
        narrow_part(9),
        narrow_part(10),
        narrow_part(11),
        grads[part_in : 2 * part_in].T,
        wide_part(4),
    )


def solution(mesh):
    placed = (
        P(None, "seq", "ch"),
        P(None, "seq", "ch"),
        P(),
        P(None, "seq"),
        P("ch"),
        P("ch"),
        P("seq", "ch"),
        P("ch"),
        P("ch"),
        P("ch"),
        P(None, "seq", "ch"),
        P("ch"),
        P("ch"),
        P("ch"),
        P("ch", "seq"),
        P("ch"),
    )
    run = fast_body if mesh.shape["seq"] == 16 else body
    return jax.shard_map(
        run,
        mesh=mesh,
        in_specs=placed,
        out_specs=(
            P(None, "seq", "ch"),
            P(None, "seq", "ch"),
            P("ch"),
            P("ch"),
            P("seq", "ch"),
            P("ch"),
            P("ch"),
            P("ch"),
            P(None, "seq", "ch"),
            P("ch"),
            P("ch"),
            P("ch"),
            P("ch", "seq"),
            P("ch"),
        ),
        check_vma=False,
    )
```

```python
import jax
import jax.numpy as jnp
from jax import lax
from jax.experimental import pallas as pl
from jax.experimental.pallas import tpu as pltpu
from jax.sharding import PartitionSpec as P

KERNEL_TAPS = 5
DILATION_STEP = 32
HALO = 64

EPSILON = 1e-05
ROOT_HALF = 0.7071067811865476
ROOT_TAU = 0.3989422804014327
SWAP = [(0, 1), (1, 0)]


def gelu_both(value):
    half = 0.5 * (1.0 + lax.erf(value * ROOT_HALF))
    return value * half, half + value * jnp.exp(-0.5 * value * value) * ROOT_TAU


def norm(value):
    middle = jnp.mean(value, axis=1, keepdims=True)
    centred = value - middle
    scale = lax.rsqrt(jnp.mean(centred * centred, axis=1, keepdims=True) + EPSILON)
    return centred * scale, scale


def norm_back(grad_zed, normed, scale, gain):
    grad_normed = grad_zed * gain
    first = jnp.mean(grad_normed, axis=1, keepdims=True)
    second = jnp.mean(grad_normed * normed, axis=1, keepdims=True)
    return scale * (grad_normed - first - normed * second)


def dot(left, right, over=((1,), (0,))):
    return lax.dot_general(left, right, (over, ((), ())), preferred_element_type=jnp.float32)


def column_sums(value):
    return jnp.sum(value, axis=0, keepdims=True)


def ordered(side, own, other):
    low = side == 0
    own, other = own.astype(jnp.float32), other.astype(jnp.float32)
    return jnp.where(low, own, other), jnp.where(low, other, own)


def windowed(framed_ref, taps, base, count):
    return jnp.concatenate(
        [
            framed_ref[pl.ds(base + tap * DILATION_STEP, count), :] * taps[:, tap : tap + 1]
            for tap in range(KERNEL_TAPS)
        ],
        axis=1,
    )


def first_kernel(side_ref, own_ref, other_ref, keep_ref, weight_ref, wide_ref, narrow_ref, a1_ref, s1_ref, h1_ref, a2_ref, s2_ref):
    x = jnp.concatenate(ordered(side_ref[0], own_ref[...], other_ref[...]), axis=1)
    normed, _ = norm(x)
    act, slope = gelu_both(normed * wide_ref[0:1, :] + wide_ref[1:2, :])
    act = act.astype(jnp.bfloat16)
    a1_ref[...] = act
    s1_ref[...] = slope
    h1 = dot(act, weight_ref[...]) + narrow_ref[0:1, :]
    h1_ref[...] = h1
    normed, _ = norm(h1)
    act, slope = gelu_both(normed * narrow_ref[1:2, :] + narrow_ref[2:3, :])
    keep = keep_ref[...]
    a2_ref[...] = (act * keep).astype(jnp.bfloat16)
    s2_ref[...] = slope * keep


def second_kernel(side_ref, own_ref, other_ref, taps_ref, framed_ref, conv_ref, weight_ref, wide_ref, narrow_ref, h3_ref, a3_ref, s3_ref, out_own_ref, out_other_ref):
    count = own_ref.shape[0]
    half = own_ref.shape[1]
    base = pl.multiple_of(pl.program_id(0) * count, count)
    h3 = dot(windowed(framed_ref, taps_ref[...], base, count), conv_ref[...]) + narrow_ref[3:4, :]
    h3_ref[...] = h3
    normed, _ = norm(h3)
    act, slope = gelu_both(normed * narrow_ref[4:5, :] + narrow_ref[5:6, :])
    act = act.astype(jnp.bfloat16)
    a3_ref[...] = act
    s3_ref[...] = slope
    mixed = dot(act, weight_ref[...], ((1,), (1,))) + wide_ref[2:3, :]
    left, right = mixed[:, :half], mixed[:, half:]
    low = side_ref[0] == 0
    out_own_ref[...] = (own_ref[...].astype(jnp.float32) + jnp.where(low, left, right)).astype(jnp.bfloat16)
    out_other_ref[...] = (other_ref[...].astype(jnp.float32) + jnp.where(low, right, left)).astype(jnp.bfloat16)


def third_kernel(side_ref, own_ref, other_ref, h3_ref, s3_ref, weight_ref, narrow_ref, dh3_ref, gy_ref, wide_sum_ref, sum_ref):
    @pl.when(pl.program_id(0) == 0)
    def _():
        wide_sum_ref[...] = jnp.zeros_like(wide_sum_ref)
        sum_ref[...] = jnp.zeros_like(sum_ref)

    gy = jnp.concatenate(ordered(side_ref[0], own_ref[...], other_ref[...]), axis=1)
    wide_sum_ref[0:1, :] += column_sums(gy)
    gy = gy.astype(jnp.bfloat16)
    gy_ref[...] = gy
    dz3 = dot(gy, weight_ref[...]) * s3_ref[...]
    normed, scale = norm(h3_ref[...])
    dh3 = norm_back(dz3, normed, scale, narrow_ref[4:5, :]).astype(jnp.bfloat16)
    dh3_ref[...] = dh3
    sum_ref[0:1, :] += column_sums(dh3.astype(jnp.float32))
    sum_ref[1:2, :] += column_sums(dz3 * normed)
    sum_ref[2:3, :] += column_sums(dz3)


def fourth_kernel(side_ref, own_ref, other_ref, gy_own_ref, taps_ref, framed_ref, conv_ref, h1_ref, s2_ref, s1_ref, weight_ref, wide_ref, narrow_ref, dh1_ref, dx_own_ref, dx_other_ref, wide_sum_ref, sum_ref):
    @pl.when(pl.program_id(0) == 0)
    def _():
        wide_sum_ref[...] = jnp.zeros_like(wide_sum_ref)
        sum_ref[...] = jnp.zeros_like(sum_ref)

    count = own_ref.shape[0]
    half = own_ref.shape[1]
    base = pl.multiple_of(pl.program_id(0) * count, count)
    dz2 = dot(windowed(framed_ref, taps_ref[...], base, count), conv_ref[...]) * s2_ref[...]
    normed, scale = norm(h1_ref[...])
    dh1 = norm_back(dz2, normed, scale, narrow_ref[1:2, :]).astype(jnp.bfloat16)
    dh1_ref[...] = dh1
    sum_ref[0:1, :] += column_sums(dh1.astype(jnp.float32))
    sum_ref[1:2, :] += column_sums(dz2 * normed)
    sum_ref[2:3, :] += column_sums(dz2)
    dz1 = dot(dh1, weight_ref[...], ((1,), (1,))) * s1_ref[...]
    x = jnp.concatenate(ordered(side_ref[0], own_ref[...], other_ref[...]), axis=1)
    normed, scale = norm(x)
    dx = norm_back(dz1, normed, scale, wide_ref[0:1, :])
    wide_sum_ref[0:1, :] += column_sums(dz1 * normed)
    wide_sum_ref[1:2, :] += column_sums(dz1)
    low = side_ref[0] == 0
    left, right = dx[:, :half], dx[:, half:]
    dx_own_ref[...] = jnp.where(low, left, right) + gy_own_ref[...].astype(jnp.float32)
    dx_other_ref[...] = jnp.where(low, right, left).astype(jnp.bfloat16)


def grad_kernel(left_ref, right_ref, out_ref):
    out_ref[...] = dot(left_ref[...], right_ref[...], ((0,), (0,)))


def conv_grad_kernel(framed_ref, taps_ref, right_ref, out_ref):
    tap = pl.program_id(0)
    count = right_ref.shape[0]
    base = pl.multiple_of(tap * DILATION_STEP, DILATION_STEP)
    left = framed_ref[pl.ds(base, count), :] * taps_ref[0]
    out_ref[0] = dot(left, right_ref[...], ((0,), (0,)))


VMEM_LIMIT = 56 * 2**20


def once(shape):
    return pl.BlockSpec(shape, lambda *_: (0,) * len(shape), pipeline_mode=pl.Buffered(1))


def by_rows(count, width):
    return pl.BlockSpec((count, width), lambda i, *_: (i, 0))


def row_call(kernel, side, rows, count, operands, outs, flops):
    in_specs = [by_rows(count, a.shape[1]) if how == "rows" else once(a.shape) for a, how in operands]
    out_specs = [
        by_rows(count, width) if how == "rows" else pl.BlockSpec((8, width), lambda i, *_: (0, 0))
        for width, _, how in outs
    ]
    out_shape = [
        jax.ShapeDtypeStruct((rows if how == "rows" else 8, width), dtype) for width, dtype, how in outs
    ]
    moved = sum(a.size * a.dtype.itemsize for a, _ in operands)
    moved += sum(o.size * o.dtype.itemsize for o in out_shape)
    return pl.pallas_call(
        kernel,
        grid_spec=pltpu.PrefetchScalarGridSpec(
            num_scalar_prefetch=1, grid=(rows // count,), in_specs=in_specs, out_specs=out_specs
        ),
        out_shape=out_shape,
        compiler_params=pltpu.CompilerParams(
            dimension_semantics=("arbitrary",), vmem_limit_bytes=VMEM_LIMIT
        ),
        cost_estimate=pl.CostEstimate(flops=flops // 32, bytes_accessed=moved // 32, transcendentals=0),
    )(side, *[a for a, _ in operands])


def matrix_grad(left, right, tiles):
    rows, height = left.shape
    width = right.shape[1]
    return pl.pallas_call(
        grad_kernel,
        grid=(tiles,),
        in_specs=[pl.BlockSpec((rows, height // tiles), lambda i: (0, i)), once((rows, width))],
        out_specs=pl.BlockSpec((height // tiles, width), lambda i: (i, 0)),
        out_shape=jax.ShapeDtypeStruct((height, width), jnp.float32),
        compiler_params=pltpu.CompilerParams(
            dimension_semantics=("arbitrary",), vmem_limit_bytes=VMEM_LIMIT
        ),
        cost_estimate=pl.CostEstimate(
            flops=rows * height * width // 16, bytes_accessed=rows * (height + width) // 16, transcendentals=0
        ),
    )(left, right)


def conv_grad(framed_rows, taps, right):
    rows, width = right.shape
    return pl.pallas_call(
        conv_grad_kernel,
        grid=(KERNEL_TAPS,),
        in_specs=[
            once(framed_rows.shape),
            pl.BlockSpec((1, rows, 1), lambda i: (i, 0, 0)),
            once((rows, width)),
        ],
        out_specs=pl.BlockSpec((1, width, width), lambda i: (i, 0, 0)),
        out_shape=jax.ShapeDtypeStruct((KERNEL_TAPS, width, width), jnp.float32),
        compiler_params=pltpu.CompilerParams(
            dimension_semantics=("arbitrary",), vmem_limit_bytes=VMEM_LIMIT
        ),
        cost_estimate=pl.CostEstimate(
            flops=KERNEL_TAPS * rows * width * width // 16, bytes_accessed=rows * width // 8, transcendentals=0
        ),
    )(framed_rows, taps, right)


def framed(block, width):
    count = lax.axis_size("seq")
    forward = [(i, i + 1) for i in range(count - 1)]
    backward = [(i + 1, i) for i in range(count - 1)]
    low = lax.ppermute(block[block.shape[0] - width :], "seq", forward)
    high = lax.ppermute(block[:width], "seq", backward)
    return jnp.concatenate([low, block, high], axis=0)


def scattered(value, order):
    count = lax.axis_size("seq")
    place = lax.axis_index("seq")
    bits = count.bit_length() - 1
    value = value.reshape((2,) * bits + value.shape[1:])
    left = list(range(bits))
    for bit in order:
        dim = left.index(bits - 1 - bit)
        left.remove(bits - 1 - bit)
        mine = (place >> bit) & 1
        keep = lax.dynamic_index_in_dim(value, mine, dim, keepdims=False)
        send = lax.dynamic_index_in_dim(value, 1 - mine, dim, keepdims=False).astype(jnp.bfloat16)
        came = lax.ppermute(send, "seq", [(i, i ^ (1 << bit)) for i in range(count)])
        value = keep + came.astype(jnp.float32)
    return value


def body(
    tokens,
    cotangent,
    seq_lengths,
    residue_mask,
    first_gain,
    first_shift,
    proj_in,
    in_bias,
    mid_gain,
    mid_shift,
    conv_weight,
    conv_bias,
    last_gain,
    last_shift,
    proj_out,
    out_bias,
):
    micro, rows, half = tokens.shape
    inner_half = in_bias.shape[0]
    inner = 2 * inner_half
    model = 2 * half
    seq_count = lax.axis_size("seq")
    count = 256
    side = lax.axis_index("ch")
    side_array = side.astype(jnp.int32).reshape(1)
    low_side = side == 0

    def swap(value):
        return lax.ppermute(value, "ch", SWAP)

    def whole(own, other, axis):
        return jnp.where(
            low_side,
            jnp.concatenate([own, other], axis=axis),
            jnp.concatenate([other, own], axis=axis),
        )

    def own_of(value):
        return lax.dynamic_index_in_dim(value, side, 0, keepdims=False)

    def other_of(value):
        return lax.dynamic_index_in_dim(value, 1 - side, 0, keepdims=False)

    own_vectors = jnp.concatenate(
        [first_gain, first_shift, out_bias, in_bias, mid_gain, mid_shift, conv_bias, last_gain, last_shift]
    )
    part_in = proj_in.shape[0]
    part_conv = conv_weight.shape[1]
    own_weights = jnp.concatenate(
        [proj_in, proj_out.T, conv_weight.reshape(KERNEL_TAPS * part_conv, inner_half)], axis=0
    )
    own_vectors, own_weights = lax.optimization_barrier((own_vectors, own_weights))
    other_vectors, other_weights = swap(own_vectors), swap(own_weights)
    tokens_tied, other_vectors, other_weights = lax.optimization_barrier(
        (other_of(tokens), other_vectors, other_weights)
    )
    both = whole(own_weights, other_weights, 1)
    vectors = jnp.where(
        low_side, jnp.stack([own_vectors, other_vectors]), jnp.stack([other_vectors, own_vectors])
    )
    x_own = own_of(tokens)
    x_other = swap(tokens_tied)
    gy_own = own_of(cotangent)
    gy_tied, _ = lax.optimization_barrier((other_of(cotangent), x_other))
    gy_other = swap(gy_tied)

    gathered = lax.all_gather(both, "seq", axis=0)
    weight_in = gathered[:, :part_in].reshape(model, inner)
    weight_out = gathered[:, part_in : 2 * part_in].reshape(model, inner)
    weight_conv = (
        gathered[:, 2 * part_in :]
        .reshape(seq_count, KERNEL_TAPS, part_conv, inner)
        .transpose(1, 0, 2, 3)
        .reshape(KERNEL_TAPS, inner, inner)
    )
    wide = jnp.stack([vectors[:, i * half : (i + 1) * half].reshape(-1) for i in range(3)])
    narrow = jnp.stack(
        [
            vectors[:, 3 * half + i * inner_half : 3 * half + (i + 1) * inner_half].reshape(-1)
            for i in range(6)
        ]
    )

    places = lax.axis_index("seq") * rows + jnp.arange(rows + 2 * HALO, dtype=jnp.int32) - HALO
    inside = (places >= 0) & (places < rows * seq_count)
    bounds = jnp.cumsum(own_of(seq_lengths))[:-1]
    segment = jnp.sum((places[:, None] >= bounds[None, :]).astype(jnp.int32), axis=1)
    segment = jnp.where(inside, segment, -1)
    middle = segment[HALO : HALO + rows]
    tap_list = [
        (segment[tap * DILATION_STEP : tap * DILATION_STEP + rows] == middle).astype(jnp.bfloat16)
        for tap in range(KERNEL_TAPS)
    ]
    taps = jnp.stack(tap_list, axis=1)
    keep = own_of(residue_mask).astype(jnp.float32)[:, None]
    f32, bf16 = jnp.float32, jnp.bfloat16
    product = 2 * rows * model * inner

    a1, s1, h1, a2, s2 = row_call(
        first_kernel,
        side_array,
        rows,
        count,
        [(x_own, "rows"), (x_other, "rows"), (keep, "rows"), (weight_in, "once"), (wide, "once"), (narrow, "once")],
        [(model, bf16, "rows"), (model, f32, "rows"), (inner, f32, "rows"), (inner, bf16, "rows"), (inner, f32, "rows")],
        product,
    )
    a2 = framed(a2, HALO)
    h3, a3, s3, out_own, out_other = row_call(
        second_kernel,
        side_array,
        rows,
        count,
        [
            (x_own, "rows"),
            (x_other, "rows"),
            (taps, "rows"),
            (a2, "once"),
            (weight_conv.reshape(KERNEL_TAPS * inner, inner), "once"),
            (weight_out, "once"),
            (wide, "once"),
            (narrow, "once"),
        ],
        [(inner, f32, "rows"), (inner, bf16, "rows"), (inner, f32, "rows"), (half, bf16, "rows"), (half, bf16, "rows")],
        4 * product,
    )
    out_back = swap(out_other)

    dh3, gy, wide_sum_3, sum_3 = row_call(
        third_kernel,
        side_array,
        rows,
        count,
        [(gy_own, "rows"), (gy_other, "rows"), (h3, "rows"), (s3, "rows"), (weight_out, "once"), (narrow, "once")],
        [(inner, bf16, "rows"), (model, bf16, "rows"), (model, f32, "sum"), (inner, f32, "sum")],
        product,
    )
    dh3_framed = framed(dh3, HALO)
    grad_out = matrix_grad(gy, a3, 2)
    grad_conv = conv_grad(a2, jnp.stack(tap_list, axis=0)[:, :, None], dh3)
    dh3_framed, out_back = lax.optimization_barrier((dh3_framed, out_back))
    flipped = jnp.flip(weight_conv, 0).transpose(0, 2, 1).reshape(KERNEL_TAPS * inner, inner)
    dh1, dx_own, dx_other, wide_sum_1, sum_1 = row_call(
        fourth_kernel,
        side_array,
        rows,
        count,
        [
            (x_own, "rows"),
            (x_other, "rows"),
            (gy_own, "rows"),
            (taps, "rows"),
            (dh3_framed, "once"),
            (flipped, "once"),
            (h1, "rows"),
            (s2, "rows"),
            (s1, "rows"),
            (weight_in, "once"),
            (wide, "once"),
            (narrow, "once"),
        ],
        [(inner, bf16, "rows"), (half, f32, "rows"), (half, bf16, "rows"), (model, f32, "sum"), (inner, f32, "sum")],
        4 * product,
    )
    dx_back = swap(dx_other)
    grad_in = matrix_grad(a1, dh1, 2)

    def placed(own, back):
        return jnp.where(low_side, jnp.stack([own, back], 0), jnp.stack([back, own], 0))

    block_out = placed(out_own, out_back)
    grad_tokens = placed(
        dx_own, dx_back.astype(f32) + other_of(cotangent).astype(f32)
    )

    bits = list(range(seq_count.bit_length() - 1))
    swapped_bits = [bits[0]] + bits[2:] + [bits[1]]
    part = jnp.concatenate(
        [
            scattered(grad_in.reshape(seq_count, part_in, inner), bits),
            scattered(grad_out.reshape(seq_count, part_in, inner), swapped_bits),
            scattered(
                grad_conv.reshape(KERNEL_TAPS, seq_count, part_conv, inner).transpose(1, 0, 2, 3), bits
            ).reshape(KERNEL_TAPS * part_conv, inner),
        ],
        axis=0,
    )
    left, right = part[:, :inner_half], part[:, inner_half:]
    part_other = swap(jnp.where(low_side, right, left).astype(bf16))
    part = jnp.where(low_side, left, right) + part_other.astype(f32)

    smalls = jnp.concatenate(
        [
            small.reshape(2, -1)
            for small in (wide_sum_1[0], wide_sum_1[1], wide_sum_3[0], sum_1[0], sum_1[1], sum_1[2], sum_3[0], sum_3[1], sum_3[2])
        ],
        axis=1,
    )
    totals = smalls
    for bit in bits:
        totals = totals + lax.ppermute(totals, "seq", [(i, i ^ (1 << bit)) for i in range(seq_count)])
    totals = own_of(totals) + swap(other_of(totals))
    sizes = [half] * 3 + [inner_half] * 6
    parts = []
    at = 0
    for size in sizes:
        parts.append(totals[at : at + size])
        at += size
    return (
        block_out,
        grad_tokens,
        parts[0],
        parts[1],
        part[:part_in],
        parts[3],
        parts[4],
        parts[5],
        part[2 * part_in :].reshape(KERNEL_TAPS, part_conv, inner_half),
        parts[6],
        parts[7],
        parts[8],
        part[part_in : 2 * part_in].T,
        parts[2],
    )


BLOCK = 256
CHUNKS = 4
CONV_PAD = 8
EARLY = 384
FIRST = 512
HEAD = 4


def fast_kernel(
    tokens, x_other, cot, gy_early, gathered, masks, wide, narrow,
    out_own, out_back, dx_own, dx_back, dx_tail, grads_out, sums_out,
    s1, h1, s2, h3, s3,
    a1v, a2f, a3v, gyv, dh3f, out_send, w_in, w_out, w_conv,
    k_in, s_in, r0_in, r1_in, r2_in, r3_in,
    k_out, s_out, r0_out, r1_out, r2_out, r3_out,
    k_low, s_low, r0_low, r1_low, r2_low, r3_low,
    k_mid, s_mid, r0_mid, r1_mid, r2_mid, r3_mid,
    k_top, s_top, r0_top, r1_top, r2_top, r3_top,
    smalls, grads, cross_send, cross_recv, small_send, small_recv, load_sems,
    gy_sems, out_sems, dx_sems, a2_sems, dh3_sems, in_sems, out_rs_sems, low_sems, mid_sems, top_sems, cross_sems, small_sems,
):
    rows = a1v.shape[0]
    half = tokens.shape[2]
    inner = narrow.shape[1]
    part = rows // CHUNKS
    side = lax.axis_index("ch")
    place = lax.axis_index("seq")
    last = lax.axis_size("seq") - 1
    low = side == 0
    bits = [lax.rem(place // (1 << bit), 2) for bit in range(4)]
    across = {"ch": 1 - side}
    pairs = [{"seq": place + (1 << bit) * (1 - 2 * bits[bit])} for bit in range(4)]
    before, after = {"seq": place - 1}, {"seq": place + 1}

    def remote(src, dst, sems, at, device):
        return pltpu.make_async_remote_copy(
            src_ref=src,
            dst_ref=dst,
            send_sem=sems.at[0, at],
            recv_sem=sems.at[1, at],
            device_id=device,
            device_id_type=pl.DeviceIdType.MESH,
        )

    def block(ref, at):
        return ref.at[pl.ds(pl.multiple_of(at * BLOCK, BLOCK), BLOCK)]

    early = gy_early.shape[0]

    def gy_copy(at):
        begin = max(at * part, early)
        piece = pl.ds(begin, (at + 1) * part - begin)
        return remote(cot.at[1 - side, piece], gyv.at[side, piece], gy_sems, at, across)

    gy_chunks = [at for at in range(CHUNKS) if (at + 1) * part > early]
    part_in = w_in.shape[1]
    tail_rows = k_top.shape[1]
    loads = [
        pltpu.make_async_copy(src, dst, load_sems.at[at])
        for at, (src, dst) in enumerate(
            (
                (gathered.at[:, pl.ds(0, part_in)], w_in),
                (gathered.at[:, pl.ds(part_in, part_in)], w_out),
                (gathered.at[pl.ds(0, 8), pl.ds(2 * part_in, part_in)], s_low),
                (gathered.at[pl.ds(8, 8), pl.ds(2 * part_in, part_in)], r0_low),
                (gathered.at[pl.ds(0, 8), pl.ds(3 * part_in, part_in)], s_mid),
                (gathered.at[pl.ds(8, 8), pl.ds(3 * part_in, part_in)], r0_mid),
                (gathered.at[pl.ds(0, 8), pl.ds(4 * part_in, tail_rows)], s_top),
                (gathered.at[pl.ds(8, 8), pl.ds(4 * part_in, tail_rows)], r0_top),
                (gy_early, gyv.at[1 - side, pl.ds(0, early)]),
                (cot.at[side], gyv.at[side]),
            )
        )
    ]

    def out_copy(at):
        return remote(block(out_send, at), block(out_back, at), out_sems, at, across)

    def dx_copy(at):
        return remote(block(gyv.at[1 - side], at), block(dx_back, at), dx_sems, at, across)

    def halo_low(framed_rows, sems):
        return remote(framed_rows.at[pl.ds(HALO, HALO)], framed_rows.at[pl.ds(HALO + rows, HALO)], sems, 0, before)

    def halo_high(framed_rows, sems):
        return remote(framed_rows.at[pl.ds(rows, HALO)], framed_rows.at[pl.ds(0, HALO)], sems, 1, after)

    def halo_start(framed_rows, sems):
        @pl.when(place > 0)
        def _():
            halo_low(framed_rows, sems).start()

        @pl.when(place < last)
        def _():
            halo_high(framed_rows, sems).start()

    def halo_wait(framed_rows, sems):
        @pl.when(place > 0)
        def _():
            halo_low(framed_rows, sems).wait_send()
            halo_high(framed_rows, sems).wait_recv()

        @pl.when(place < last)
        def _():
            halo_high(framed_rows, sems).wait_send()
            halo_low(framed_rows, sems).wait_recv()

    blocks = rows // BLOCK

    def middle_first(step):
        late = step // (blocks - 2)
        return (step + 1) * (1 - late) + late * (step - (blocks - 2)) * (blocks - 1)

    def in_order(step):
        return step

    def pipeline(step, order, ins, outs, tail=None):
        def spec(ref):
            return pl.BlockSpec((BLOCK, ref.shape[-1]), lambda i: (order(i), 0))

        out_specs = [spec(r) for r in outs]
        if tail is not None:
            outs = outs + [tail]
            out_specs.append(pl.BlockSpec((BLOCK, half), lambda i: (jnp.maximum(i - HEAD, 0), 0)))
        pltpu.emit_pipeline(step, grid=(blocks,), in_specs=[spec(r) for r in ins], out_specs=out_specs)(*ins, *outs)

    barrier = pltpu.get_barrier_semaphore()
    ring = [{"seq": lax.rem(place + last, last + 1)}, {"seq": lax.rem(place + 1, last + 1)}]
    for device in [across] + pairs + ring:
        pl.semaphore_signal(barrier, inc=1, device_id=device, device_id_type=pl.DeviceIdType.MESH)
    pl.semaphore_wait(barrier, 7)

    for at in gy_chunks:
        gy_copy(at).start()
    for load in loads:
        load.start()
    smalls[...] = jnp.zeros_like(smalls)

    @pl.when(place == 0)
    def _():
        a2f[0:HALO, :] = jnp.zeros((HALO, inner), jnp.bfloat16)
        dh3f[0:HALO, :] = jnp.zeros((HALO, inner), jnp.bfloat16)

    @pl.when(place == last)
    def _():
        a2f[HALO + rows :, :] = jnp.zeros((HALO, inner), jnp.bfloat16)
        dh3f[HALO + rows :, :] = jnp.zeros((HALO, inner), jnp.bfloat16)

    def first(own, other, s1_block, h1_block, s2_block):
        base = pl.multiple_of(pl.program_id(0) * BLOCK, BLOCK)
        x = jnp.concatenate(ordered(side, own[...], other[...]), axis=1)
        normed, _ = norm(x)
        act, slope = gelu_both(normed * wide[0:1, :] + wide[1:2, :])
        act = act.astype(jnp.bfloat16)
        a1v[pl.ds(base, BLOCK), :] = act
        s1_block[...] = slope
        value = dot(act, w_in[...].reshape(2 * half, inner)) + narrow[0:1, :]
        h1_block[...] = value
        normed, _ = norm(value)
        act, slope = gelu_both(normed * narrow[1:2, :] + narrow[2:3, :])
        keep = masks[pl.ds(base, BLOCK), KERNEL_TAPS : KERNEL_TAPS + 1].astype(jnp.float32)
        a2f[pl.ds(HALO + base, BLOCK), :] = (act * keep).astype(jnp.bfloat16)
        s2_block[...] = slope * keep

    loads[0].wait()
    pipeline(first, in_order, [tokens.at[side], x_other], [s1, h1, s2])
    for at in range(2, 8):
        loads[at].wait()
    height = inner // 16

    def relay(pair, _):
        for group, sources in enumerate(((s_low, s_mid, s_top), (r0_low, r0_mid, r0_top))):
            at = pl.multiple_of((4 * group + pair) * 2 * height, 2 * height)
            tap = 0
            for source in sources:
                even = source[2 * pair].astype(jnp.float32)
                odd = source[2 * pair + 1].astype(jnp.float32)
                for top in range(0, source.shape[1] - CONV_PAD, height):
                    w_conv[tap, pl.ds(at, 2 * height), :] = jnp.concatenate(
                        [even[top : top + height], odd[top : top + height]], axis=0
                    ).astype(jnp.bfloat16)
                    tap += 1
        return 0

    lax.fori_loop(0, 4, relay, 0)
    loads[1].wait()
    halo_start(a2f, a2_sems)

    def second(own, other, h3_block, s3_block, own_block):
        step = pl.program_id(0)
        at = middle_first(step)
        base = pl.multiple_of(at * BLOCK, BLOCK)

        @pl.when(step == blocks - 2)
        def _():
            halo_wait(a2f, a2_sems)

        taps = masks[pl.ds(base, BLOCK), :]
        weight = w_conv[...].reshape(KERNEL_TAPS * inner, inner)
        value = dot(windowed(a2f, taps, base, BLOCK), weight) + narrow[3:4, :]
        h3_block[...] = value
        normed, _ = norm(value)
        act, slope = gelu_both(normed * narrow[4:5, :] + narrow[5:6, :])
        act = act.astype(jnp.bfloat16)
        a3v[pl.ds(base, BLOCK), :] = act
        s3_block[...] = slope
        mixed = dot(act, w_out[...].reshape(2 * half, inner), ((1,), (1,))) + wide[2:3, :]
        left, right = mixed[:, :half], mixed[:, half:]
        own_block[...] = (own[...].astype(jnp.float32) + jnp.where(low, left, right)).astype(jnp.bfloat16)
        out_send[pl.ds(base, BLOCK), :] = (
            other[...].astype(jnp.float32) + jnp.where(low, right, left)
        ).astype(jnp.bfloat16)
        out_copy(at).start()

    pipeline(second, middle_first, [tokens.at[side], x_other], [h3, s3, out_own])

    def add_small(row, value):
        smalls[row : row + 1, :] += value

    def add_wide(row, value):
        smalls[row : row + 1, :] += value[:, :half]
        smalls[row + 1 : row + 2, :] += value[:, half:]

    per = part // BLOCK

    def third(h3_block, s3_block):
        at = pl.program_id(0)
        base = pl.multiple_of(at * BLOCK, BLOCK)
        for later in gy_chunks:

            @pl.when(at == later * per)
            def _():
                gy_copy(later).wait_recv()

        gy = jnp.concatenate([gyv[0, pl.ds(base, BLOCK), :], gyv[1, pl.ds(base, BLOCK), :]], axis=1)
        add_wide(4, column_sums(gy.astype(jnp.float32)))
        dz3 = dot(gy, w_out[...].reshape(2 * half, inner)) * s3_block[...]
        normed, scale = norm(h3_block[...])
        dh3 = norm_back(dz3, normed, scale, narrow[4:5, :]).astype(jnp.bfloat16)
        dh3f[pl.ds(HALO + base, BLOCK), :] = dh3
        add_small(9, column_sums(dh3.astype(jnp.float32)))
        add_small(10, column_sums(dz3 * normed))
        add_small(11, column_sums(dz3))

    loads[8].wait()
    loads[9].wait()
    pipeline(third, in_order, [h3, s3], [])
    halo_start(dh3f, dh3_sems)

    def slot(pair, order):
        two = (pair % 4) if order[0] == 1 else (pair % 4) // 2 + 2 * (pair % 2)
        return pair // 4 * 4 + two

    def split(group, at, even, odd):
        keep_ref, send_ref = group[0], group[1]
        mine_first = bits[0] == 0
        keep_ref[at] = jnp.where(mine_first, even, odd)
        send_ref[at] = jnp.where(mine_first, odd, even).astype(jnp.bfloat16)

    def wide_grad(left_of, right_ref, group):
        tall_rows = group[0].shape[1]

        def tile(at, _):
            value = dot(left_of(at), right_ref[...], ((0,), (0,)))
            for pair in range(4):
                top = 2 * pair * tall_rows
                split(
                    group,
                    at * 4 + slot(pair, group[4]),
                    value[top : top + tall_rows],
                    value[top + tall_rows : top + 2 * tall_rows],
                )
            return 0

        lax.fori_loop(0, 2, tile, 0)
        sum_copy(group, 0).start()

    def conv_grad_of(taps, group):
        right = dh3f.at[pl.ds(HALO, rows)]
        values = []
        for tap in taps:
            left = a2f[tap * DILATION_STEP : tap * DILATION_STEP + rows, :] * masks[:, tap : tap + 1]
            values.append(dot(left, right[...], ((0,), (0,))))
        if len(values) == 1:
            tail = [jnp.zeros((CONV_PAD, inner), jnp.float32)]
        else:
            tail = []
        for pair in range(8):
            top = 2 * pair * height
            split(
                group,
                slot(pair, group[4]),
                jnp.concatenate([v[top : top + height] for v in values] + tail, axis=0),
                jnp.concatenate([v[top + height : top + 2 * height] for v in values] + tail, axis=0),
            )
        sum_copy(group, 0).start()

    y_first, z_first = (1, 2, 3), (2, 1, 3)
    in_set = (k_in, s_in, (r0_in, r1_in, r2_in, r3_in), in_sems, y_first)
    out_set = (k_out, s_out, (r0_out, r1_out, r2_out, r3_out), out_rs_sems, z_first)
    low_set = (k_low, s_low, (r0_low, r1_low, r2_low, r3_low), low_sems, y_first)
    mid_set = (k_mid, s_mid, (r0_mid, r1_mid, r2_mid, r3_mid), mid_sems, z_first)
    top_set = (k_top, s_top, (r0_top, r1_top, r2_top, r3_top), top_sems, y_first)
    starts = (0, 0, 4, 6)
    lengths = (8, 4, 2, 1)

    def sum_copy(group, level):
        _, send, received, sems, order = group
        bit = 0 if level == 0 else order[level - 1]
        return remote(
            send.at[pl.ds(starts[level], lengths[level])], received[level], sems, level, pairs[bit]
        )

    def sum_step(group, level):
        keep, send, received, _, order = group
        sum_copy(group, level).wait()
        came = received[level]
        fixed = 0
        for at in range(level):
            fixed = fixed + bits[order[at]] * (1 << at)
        if level == 3:
            keep[fixed] = keep[fixed] + came[0].astype(jnp.float32)
            return
        mine = bits[order[level]]

        def one(item, _):
            other = 2 * item + 1 - mine
            same = 2 * item + mine
            send[starts[level + 1] + item] = (
                keep[other * (1 << level) + fixed] + came[other].astype(jnp.float32)
            ).astype(jnp.bfloat16)
            at = same * (1 << level) + fixed
            keep[at] = keep[at] + came[same].astype(jnp.float32)
            return 0

        lax.fori_loop(0, lengths[level + 1], one, 0)
        sum_copy(group, level + 1).start()

    def at_step(step, when, *steps):
        @pl.when(step == when)
        def _():
            for group, level in steps:
                sum_step(group, level)

    conv_grad_of((0, 1), low_set)
    conv_grad_of((2, 3), mid_set)
    conv_grad_of((4,), top_set)
    wide_grad(lambda at: gyv[at], a3v, out_set)

    def fourth(h1_block, s2_block):
        step = pl.program_id(0)
        base = pl.multiple_of(step * BLOCK, BLOCK)
        taps = masks[pl.ds(base, BLOCK), :]
        da2 = jnp.zeros((BLOCK, inner), jnp.float32)
        for tap in range(KERNEL_TAPS):
            window = dh3f[pl.ds(base + tap * DILATION_STEP, BLOCK), :] * taps[:, tap : tap + 1]
            da2 = da2 + dot(window, w_conv[KERNEL_TAPS - 1 - tap], ((1,), (1,)))
        dz2 = da2 * s2_block[...]
        normed, scale = norm(h1_block[...])
        dh1 = norm_back(dz2, normed, scale, narrow[1:2, :]).astype(jnp.bfloat16)
        a3v[pl.ds(base, BLOCK), :] = dh1
        add_small(6, column_sums(dh1.astype(jnp.float32)))
        add_small(7, column_sums(dz2 * normed))
        add_small(8, column_sums(dz2))
        at_step(step, 0, (low_set, 0), (mid_set, 0), (top_set, 0))
        at_step(step, 1, (out_set, 0))
        at_step(step, 5, (low_set, 1))
        at_step(step, 6, (mid_set, 1))
        at_step(step, 7, (top_set, 1))

    halo_wait(dh3f, dh3_sems)
    pipeline(fourth, in_order, [h1, s2], [])
    wide_grad(lambda at: a1v[:, pl.ds(pl.multiple_of(at * half, 128), half)], a3v, in_set)
    sum_step(out_set, 1)
    sum_step(low_set, 2)

    def fifth(own, other, s1_block, own_block, tail_block):
        step = pl.program_id(0)
        base = pl.multiple_of(step * BLOCK, BLOCK)
        dh1 = a3v[pl.ds(base, BLOCK), :]
        dz1 = dot(dh1, w_in[...].reshape(2 * half, inner), ((1,), (1,))) * s1_block[...]
        x = jnp.concatenate(ordered(side, own[...], other[...]), axis=1)
        normed, scale = norm(x)
        dx = norm_back(dz1, normed, scale, wide[0:1, :])
        add_wide(0, column_sums(dz1 * normed))
        add_wide(2, column_sums(dz1))
        left, right = dx[:, :half], dx[:, half:]
        own_block[...] = jnp.where(low, left, right) + gyv[side, pl.ds(base, BLOCK), :].astype(jnp.float32)
        sent = jnp.where(low, right, left).astype(jnp.bfloat16)
        gyv[1 - side, pl.ds(base, BLOCK), :] = sent
        tail_block[...] = sent

        @pl.when(step < HEAD)
        def _():
            dx_copy(step).start()

        at_step(step, 0, (mid_set, 2), (in_set, 0))
        at_step(step, 2, (out_set, 2), (top_set, 2))
        at_step(step, 4, (low_set, 3))
        at_step(step, 5, (mid_set, 3))
        at_step(step, 6, (in_set, 1))
        at_step(step, 7, (top_set, 3), (out_set, 3))

    pipeline(fifth, in_order, [tokens.at[side], x_other, s1], [dx_own], dx_tail)


    def small_copy(level):
        device = pairs[level] if level < 4 else across
        return remote(small_send.at[level], small_recv.at[level], small_sems, level, device)

    def small_start(level):
        small_send[level] = smalls[...]
        small_copy(level).start()

    def small_step(level):
        small_copy(level).wait()
        smalls[...] += small_recv[level]

    small_start(0)
    sum_step(in_set, 2)
    small_step(0)
    small_start(1)
    small_step(1)
    small_start(2)
    small_step(2)
    small_start(3)
    sum_step(in_set, 3)
    small_step(3)
    small_start(4)

    wanted = half // 2 + 64
    row = 0
    for keep, _, _, _, order in (in_set, out_set, low_set, mid_set, top_set):
        mine = bits[order[0]] + 2 * bits[order[1]] + 4 * bits[order[2]]
        height = keep.shape[1]
        value = keep[mine]
        left, right = value[:, :wanted], value[:, inner - wanted :]
        grads[row : row + height, :] = jnp.where(low, left, right)
        cross_send[row : row + height, :] = jnp.where(low, right, left).astype(jnp.bfloat16)
        row += height
    cross = remote(cross_send, cross_recv, cross_sems, 0, across)
    cross.start()
    for at in gy_chunks:
        gy_copy(at).wait_send()
    for at in range(blocks):
        out_copy(at).wait()
    small_step(4)
    quarter = half // 2
    for index in range(3):
        both = smalls[2 * index : 2 * index + 2, :]
        sums_out[:, index * half : (index + 1) * half] = jnp.where(low, both[0:1], both[1:2])
    for index in range(6):
        both = smalls[6 + index : 7 + index, :]
        at = 3 * half + index * wanted
        sums_out[:, at : at + quarter] = jnp.where(low, both[:, :quarter], both[:, quarter:])
    cross.wait()
    total = grads[...] + cross_recv[...].astype(jnp.float32)
    grads_out[...] = jnp.where(low, total[:, :quarter], total[:, wanted - quarter :])
    for at in range(HEAD):
        dx_copy(at).wait()


def fast_call(tokens, x_other, cot, gy_early, gathered, masks, wide, narrow, part_in, part_conv):
    _, rows, half = tokens.shape
    model = 2 * half
    inner = narrow.shape[1]
    f32, bf16 = jnp.float32, jnp.bfloat16
    tall = KERNEL_TAPS * part_conv + CONV_PAD
    any_spec = pl.BlockSpec(memory_space=pl.ANY)
    vmem_spec = pl.BlockSpec(memory_space=pltpu.VMEM)
    total = 2 * part_in + tall
    wanted = half // 2 + 64

    def sums(height):
        return [pltpu.VMEM((8, height, inner), f32), pltpu.VMEM((8, height, inner), bf16)] + [
            pltpu.VMEM((length, height, inner), bf16) for length in (8, 4, 2, 1)
        ]

    def sems(count):
        return pltpu.SemaphoreType.DMA((2, count))

    shapes = [
        ((rows, half), bf16),
        ((rows, half), bf16),
        ((rows, half), f32),
        ((rows, half), bf16),
        ((rows - HEAD * BLOCK, half), bf16),
        ((total, half // 2), f32),
        ((1, 3 * half + 6 * wanted), f32),
        ((rows, model), f32),
        ((rows, inner), f32),
        ((rows, inner), f32),
        ((rows, inner), f32),
        ((rows, inner), f32),
    ]
    flops = 6 * rows * (2 * model * inner + KERNEL_TAPS * inner * inner)
    results = pl.pallas_call(
        fast_kernel,
        out_shape=[jax.ShapeDtypeStruct(shape, dtype) for shape, dtype in shapes],
        in_specs=[any_spec] * 5 + [vmem_spec] * 3,
        out_specs=[any_spec] * 5 + [vmem_spec] * 2 + [any_spec] * 5,
        scratch_shapes=[
            pltpu.VMEM((rows, model), bf16),
            pltpu.VMEM((rows + 2 * HALO, inner), bf16),
            pltpu.VMEM((rows, inner), bf16),
            pltpu.VMEM((2, rows, half), bf16),
            pltpu.VMEM((rows + 2 * HALO, inner), bf16),
            pltpu.VMEM((rows, half), bf16),
            pltpu.VMEM((16, part_in, inner), bf16),
            pltpu.VMEM((16, part_in, inner), bf16),
            pltpu.VMEM((KERNEL_TAPS, inner, inner), bf16),
        ]
        + sums(part_in) * 4
        + sums(tall - 2 * part_in)
        + [
            pltpu.VMEM((16, inner), f32),
            pltpu.VMEM((total, wanted), f32),
            pltpu.VMEM((total, wanted), bf16),
            pltpu.VMEM((total, wanted), bf16),
            pltpu.VMEM((5, 16, inner), f32),
            pltpu.VMEM((5, 16, inner), f32),
            pltpu.SemaphoreType.DMA((10,)),
            sems(CHUNKS),
            sems(rows // BLOCK),
            sems(HEAD),
            sems(2),
            sems(2),
            sems(4),
            sems(4),
            sems(4),
            sems(4),
            sems(4),
            sems(1),
            sems(5),
        ],
        compiler_params=pltpu.CompilerParams(
            collective_id=0, has_side_effects=True, vmem_limit_bytes=63 * 2**20
        ),
        cost_estimate=pl.CostEstimate(flops=flops, bytes_accessed=120 * 2**20, transcendentals=0),
    )(tokens, x_other, cot, gy_early, gathered, masks, wide, narrow)
    return results[:7]


def finish_kernel(side_ref, tail_ref, cot_ref, whole_ref, out_ref):
    out_ref[0] = tail_ref[...].astype(jnp.float32) + cot_ref[0].astype(jnp.float32)


def finish_call(side, tail, cot, grad_tokens, first):
    half = tail.shape[1]

    def theirs(i, side_ref):
        return (1 - side_ref[0], first + i, 0)

    return pl.pallas_call(
        finish_kernel,
        grid_spec=pltpu.PrefetchScalarGridSpec(
            num_scalar_prefetch=1,
            grid=(tail.shape[0] // BLOCK,),
            in_specs=[
                pl.BlockSpec((BLOCK, half), lambda i, side_ref: (i, 0)),
                pl.BlockSpec((1, BLOCK, half), theirs),
                pl.BlockSpec(memory_space=pl.ANY),
            ],
            out_specs=pl.BlockSpec((1, BLOCK, half), theirs),
        ),
        out_shape=jax.ShapeDtypeStruct(grad_tokens.shape, grad_tokens.dtype),
        input_output_aliases={3: 0},
        compiler_params=pltpu.CompilerParams(
            dimension_semantics=("arbitrary",), vmem_limit_bytes=56 * 2**20
        ),
        cost_estimate=pl.CostEstimate(flops=tail.size, bytes_accessed=8 * tail.size, transcendentals=0),
    )(side, tail, cot, grad_tokens)


def fast_body(
    tokens,
    cotangent,
    seq_lengths,
    residue_mask,
    first_gain,
    first_shift,
    proj_in,
    in_bias,
    mid_gain,
    mid_shift,
    conv_weight,
    conv_bias,
    last_gain,
    last_shift,
    proj_out,
    out_bias,
):
    micro, rows, half = tokens.shape
    inner_half = in_bias.shape[0]
    inner = 2 * inner_half
    model = 2 * half
    seq_count = lax.axis_size("seq")
    side = lax.axis_index("ch")
    low_side = side == 0
    f32, bf16 = jnp.float32, jnp.bfloat16

    def swap(value):
        return lax.ppermute(value, "ch", SWAP)

    def own_of(value):
        return lax.dynamic_index_in_dim(value, side, 0, keepdims=False)

    def other_of(value):
        return lax.dynamic_index_in_dim(value, 1 - side, 0, keepdims=False)

    own_vectors = jnp.concatenate(
        [first_gain, first_shift, out_bias, in_bias, mid_gain, mid_shift, conv_bias, last_gain, last_shift]
    )
    part_in = proj_in.shape[0]
    part_conv = conv_weight.shape[1]
    own_weights = jnp.concatenate(
        [
            proj_in,
            proj_out.T,
            conv_weight.reshape(KERNEL_TAPS * part_conv, inner_half),
            jnp.zeros((CONV_PAD, inner_half), bf16),
        ],
        axis=0,
    )
    x_send = other_of(tokens)
    own_vectors, own_weights, first_send = lax.optimization_barrier(
        (own_vectors, own_weights, x_send[:FIRST])
    )
    other_vectors, other_weights = swap(own_vectors), swap(own_weights)
    both = jnp.where(
        low_side,
        jnp.concatenate([own_weights, other_weights], axis=1),
        jnp.concatenate([other_weights, own_weights], axis=1),
    )
    vectors = jnp.where(
        low_side, jnp.stack([own_vectors, other_vectors]), jnp.stack([other_vectors, own_vectors])
    )
    x_first, x_second = swap(first_send), swap(x_send[FIRST:])
    gy_tied, x_first = lax.optimization_barrier((cotangent[:, :EARLY], x_first))
    gy_early = swap(other_of(gy_tied))
    x_other = jnp.concatenate([x_first, x_second], axis=0)
    gathered = lax.all_gather(both, "seq", axis=0)
    wide = jnp.stack([vectors[:, i * half : (i + 1) * half].reshape(-1) for i in range(3)])
    narrow = jnp.stack(
        [
            vectors[:, 3 * half + i * inner_half : 3 * half + (i + 1) * inner_half].reshape(-1)
            for i in range(6)
        ]
    )

    places = lax.axis_index("seq") * rows + jnp.arange(rows + 2 * HALO, dtype=jnp.int32) - HALO
    inside = (places >= 0) & (places < rows * seq_count)
    bounds = jnp.cumsum(own_of(seq_lengths))[:-1]
    segment = jnp.sum((places[:, None] >= bounds[None, :]).astype(jnp.int32), axis=1)
    segment = jnp.where(inside, segment, -1)
    middle = segment[HALO : HALO + rows]
    columns = [
        (segment[tap * DILATION_STEP : tap * DILATION_STEP + rows] == middle).astype(bf16)
        for tap in range(KERNEL_TAPS)
    ]
    zero = jnp.zeros((rows,), bf16)
    masks = jnp.stack(columns + [own_of(residue_mask).astype(bf16), zero, zero], axis=1)

    out_own, out_back, dx_own, dx_back, dx_tail, grads, sums = fast_call(
        tokens,
        x_other,
        cotangent,
        gy_early,
        gathered,
        masks,
        wide,
        narrow,
        part_in,
        part_conv,
    )

    def placed(own, back):
        return jnp.where(low_side, jnp.stack([own, back], 0), jnp.stack([back, own], 0))

    block_out = placed(out_own, out_back)
    grad_tokens = placed(dx_own, dx_back.astype(f32) + other_of(cotangent).astype(f32))
    side_array = side.astype(jnp.int32).reshape(1)
    grad_tokens = finish_call(side_array, swap(dx_tail), cotangent, grad_tokens, HEAD)
    wanted = inner_half + 64

    def narrow_part(index):
        at = 3 * half + index * wanted
        return sums[0, at : at + inner_half]

    return (
        block_out,
        grad_tokens,
        sums[0, :half],
        sums[0, half : 2 * half],
        grads[:part_in],
        narrow_part(0),
        narrow_part(1),
        narrow_part(2),
        grads[2 * part_in : 2 * part_in + KERNEL_TAPS * part_conv].reshape(KERNEL_TAPS, part_conv, inner_half),
        narrow_part(3),
        narrow_part(4),
        narrow_part(5),
        grads[part_in : 2 * part_in].T,
        sums[0, 2 * half : 3 * half],
    )


def solution(mesh):
    placed = (
        P(None, "seq", "ch"),
        P(None, "seq", "ch"),
        P(),
        P(None, "seq"),
        P("ch"),
        P("ch"),
        P("seq", "ch"),
        P("ch"),
        P("ch"),
        P("ch"),
        P(None, "seq", "ch"),
        P("ch"),
        P("ch"),
        P("ch"),
        P("ch", "seq"),
        P("ch"),
    )
    run = fast_body if mesh.shape["seq"] == 16 else body
    return jax.shard_map(
        run,
        mesh=mesh,
        in_specs=placed,
        out_specs=(
            P(None, "seq", "ch"),
            P(None, "seq", "ch"),
            P("ch"),
            P("ch"),
            P("seq", "ch"),
            P("ch"),
            P("ch"),
            P("ch"),
            P(None, "seq", "ch"),
            P("ch"),
            P("ch"),
            P("ch"),
            P("ch", "seq"),
            P("ch"),
        ),
        check_vma=False,
    )
```

```python
import jax
import jax.numpy as jnp
from jax import lax
from jax.experimental import pallas as pl
from jax.experimental.pallas import tpu as pltpu
from jax.sharding import PartitionSpec as P

KERNEL_TAPS = 5
DILATION_STEP = 32
HALO = 64

EPSILON = 1e-05
ROOT_HALF = 0.7071067811865476
ROOT_TAU = 0.3989422804014327
SWAP = [(0, 1), (1, 0)]


def gelu_both(value):
    half = 0.5 * (1.0 + lax.erf(value * ROOT_HALF))
    return value * half, half + value * jnp.exp(-0.5 * value * value) * ROOT_TAU


def norm(value):
    middle = jnp.mean(value, axis=1, keepdims=True)
    centred = value - middle
    scale = lax.rsqrt(jnp.mean(centred * centred, axis=1, keepdims=True) + EPSILON)
    return centred * scale, scale


def norm_back(grad_zed, normed, scale, gain):
    grad_normed = grad_zed * gain
    first = jnp.mean(grad_normed, axis=1, keepdims=True)
    second = jnp.mean(grad_normed * normed, axis=1, keepdims=True)
    return scale * (grad_normed - first - normed * second)


def dot(left, right, over=((1,), (0,))):
    return lax.dot_general(left, right, (over, ((), ())), preferred_element_type=jnp.float32)


def column_sums(value):
    return jnp.sum(value, axis=0, keepdims=True)


def ordered(side, own, other):
    low = side == 0
    own, other = own.astype(jnp.float32), other.astype(jnp.float32)
    return jnp.where(low, own, other), jnp.where(low, other, own)


def windowed(framed_ref, taps, base, count):
    return jnp.concatenate(
        [
            framed_ref[pl.ds(base + tap * DILATION_STEP, count), :] * taps[:, tap : tap + 1]
            for tap in range(KERNEL_TAPS)
        ],
        axis=1,
    )


def first_kernel(side_ref, own_ref, other_ref, keep_ref, weight_ref, wide_ref, narrow_ref, a1_ref, s1_ref, h1_ref, a2_ref, s2_ref):
    x = jnp.concatenate(ordered(side_ref[0], own_ref[...], other_ref[...]), axis=1)
    normed, _ = norm(x)
    act, slope = gelu_both(normed * wide_ref[0:1, :] + wide_ref[1:2, :])
    act = act.astype(jnp.bfloat16)
    a1_ref[...] = act
    s1_ref[...] = slope
    h1 = dot(act, weight_ref[...]) + narrow_ref[0:1, :]
    h1_ref[...] = h1
    normed, _ = norm(h1)
    act, slope = gelu_both(normed * narrow_ref[1:2, :] + narrow_ref[2:3, :])
    keep = keep_ref[...]
    a2_ref[...] = (act * keep).astype(jnp.bfloat16)
    s2_ref[...] = slope * keep


def second_kernel(side_ref, own_ref, other_ref, taps_ref, framed_ref, conv_ref, weight_ref, wide_ref, narrow_ref, h3_ref, a3_ref, s3_ref, out_own_ref, out_other_ref):
    count = own_ref.shape[0]
    half = own_ref.shape[1]
    base = pl.multiple_of(pl.program_id(0) * count, count)
    h3 = dot(windowed(framed_ref, taps_ref[...], base, count), conv_ref[...]) + narrow_ref[3:4, :]
    h3_ref[...] = h3
    normed, _ = norm(h3)
    act, slope = gelu_both(normed * narrow_ref[4:5, :] + narrow_ref[5:6, :])
    act = act.astype(jnp.bfloat16)
    a3_ref[...] = act
    s3_ref[...] = slope
    mixed = dot(act, weight_ref[...], ((1,), (1,))) + wide_ref[2:3, :]
    left, right = mixed[:, :half], mixed[:, half:]
    low = side_ref[0] == 0
    out_own_ref[...] = (own_ref[...].astype(jnp.float32) + jnp.where(low, left, right)).astype(jnp.bfloat16)
    out_other_ref[...] = (other_ref[...].astype(jnp.float32) + jnp.where(low, right, left)).astype(jnp.bfloat16)


def third_kernel(side_ref, own_ref, other_ref, h3_ref, s3_ref, weight_ref, narrow_ref, dh3_ref, gy_ref, wide_sum_ref, sum_ref):
    @pl.when(pl.program_id(0) == 0)
    def _():
        wide_sum_ref[...] = jnp.zeros_like(wide_sum_ref)
        sum_ref[...] = jnp.zeros_like(sum_ref)

    gy = jnp.concatenate(ordered(side_ref[0], own_ref[...], other_ref[...]), axis=1)
    wide_sum_ref[0:1, :] += column_sums(gy)
    gy = gy.astype(jnp.bfloat16)
    gy_ref[...] = gy
    dz3 = dot(gy, weight_ref[...]) * s3_ref[...]
    normed, scale = norm(h3_ref[...])
    dh3 = norm_back(dz3, normed, scale, narrow_ref[4:5, :]).astype(jnp.bfloat16)
    dh3_ref[...] = dh3
    sum_ref[0:1, :] += column_sums(dh3.astype(jnp.float32))
    sum_ref[1:2, :] += column_sums(dz3 * normed)
    sum_ref[2:3, :] += column_sums(dz3)


def fourth_kernel(side_ref, own_ref, other_ref, gy_own_ref, taps_ref, framed_ref, conv_ref, h1_ref, s2_ref, s1_ref, weight_ref, wide_ref, narrow_ref, dh1_ref, dx_own_ref, dx_other_ref, wide_sum_ref, sum_ref):
    @pl.when(pl.program_id(0) == 0)
    def _():
        wide_sum_ref[...] = jnp.zeros_like(wide_sum_ref)
        sum_ref[...] = jnp.zeros_like(sum_ref)

    count = own_ref.shape[0]
    half = own_ref.shape[1]
    base = pl.multiple_of(pl.program_id(0) * count, count)
    dz2 = dot(windowed(framed_ref, taps_ref[...], base, count), conv_ref[...]) * s2_ref[...]
    normed, scale = norm(h1_ref[...])
    dh1 = norm_back(dz2, normed, scale, narrow_ref[1:2, :]).astype(jnp.bfloat16)
    dh1_ref[...] = dh1
    sum_ref[0:1, :] += column_sums(dh1.astype(jnp.float32))
    sum_ref[1:2, :] += column_sums(dz2 * normed)
    sum_ref[2:3, :] += column_sums(dz2)
    dz1 = dot(dh1, weight_ref[...], ((1,), (1,))) * s1_ref[...]
    x = jnp.concatenate(ordered(side_ref[0], own_ref[...], other_ref[...]), axis=1)
    normed, scale = norm(x)
    dx = norm_back(dz1, normed, scale, wide_ref[0:1, :])
    wide_sum_ref[0:1, :] += column_sums(dz1 * normed)
    wide_sum_ref[1:2, :] += column_sums(dz1)
    low = side_ref[0] == 0
    left, right = dx[:, :half], dx[:, half:]
    dx_own_ref[...] = jnp.where(low, left, right) + gy_own_ref[...].astype(jnp.float32)
    dx_other_ref[...] = jnp.where(low, right, left).astype(jnp.bfloat16)


def grad_kernel(left_ref, right_ref, out_ref):
    out_ref[...] = dot(left_ref[...], right_ref[...], ((0,), (0,)))


def conv_grad_kernel(framed_ref, taps_ref, right_ref, out_ref):
    tap = pl.program_id(0)
    count = right_ref.shape[0]
    base = pl.multiple_of(tap * DILATION_STEP, DILATION_STEP)
    left = framed_ref[pl.ds(base, count), :] * taps_ref[0]
    out_ref[0] = dot(left, right_ref[...], ((0,), (0,)))


VMEM_LIMIT = 56 * 2**20


def once(shape):
    return pl.BlockSpec(shape, lambda *_: (0,) * len(shape), pipeline_mode=pl.Buffered(1))


def by_rows(count, width):
    return pl.BlockSpec((count, width), lambda i, *_: (i, 0))


def row_call(kernel, side, rows, count, operands, outs, flops):
    in_specs = [by_rows(count, a.shape[1]) if how == "rows" else once(a.shape) for a, how in operands]
    out_specs = [
        by_rows(count, width) if how == "rows" else pl.BlockSpec((8, width), lambda i, *_: (0, 0))
        for width, _, how in outs
    ]
    out_shape = [
        jax.ShapeDtypeStruct((rows if how == "rows" else 8, width), dtype) for width, dtype, how in outs
    ]
    moved = sum(a.size * a.dtype.itemsize for a, _ in operands)
    moved += sum(o.size * o.dtype.itemsize for o in out_shape)
    return pl.pallas_call(
        kernel,
        grid_spec=pltpu.PrefetchScalarGridSpec(
            num_scalar_prefetch=1, grid=(rows // count,), in_specs=in_specs, out_specs=out_specs
        ),
        out_shape=out_shape,
        compiler_params=pltpu.CompilerParams(
            dimension_semantics=("arbitrary",), vmem_limit_bytes=VMEM_LIMIT
        ),
        cost_estimate=pl.CostEstimate(flops=flops // 32, bytes_accessed=moved // 32, transcendentals=0),
    )(side, *[a for a, _ in operands])


def matrix_grad(left, right, tiles):
    rows, height = left.shape
    width = right.shape[1]
    return pl.pallas_call(
        grad_kernel,
        grid=(tiles,),
        in_specs=[pl.BlockSpec((rows, height // tiles), lambda i: (0, i)), once((rows, width))],
        out_specs=pl.BlockSpec((height // tiles, width), lambda i: (i, 0)),
        out_shape=jax.ShapeDtypeStruct((height, width), jnp.float32),
        compiler_params=pltpu.CompilerParams(
            dimension_semantics=("arbitrary",), vmem_limit_bytes=VMEM_LIMIT
        ),
        cost_estimate=pl.CostEstimate(
            flops=rows * height * width // 16, bytes_accessed=rows * (height + width) // 16, transcendentals=0
        ),
    )(left, right)


def conv_grad(framed_rows, taps, right):
    rows, width = right.shape
    return pl.pallas_call(
        conv_grad_kernel,
        grid=(KERNEL_TAPS,),
        in_specs=[
            once(framed_rows.shape),
            pl.BlockSpec((1, rows, 1), lambda i: (i, 0, 0)),
            once((rows, width)),
        ],
        out_specs=pl.BlockSpec((1, width, width), lambda i: (i, 0, 0)),
        out_shape=jax.ShapeDtypeStruct((KERNEL_TAPS, width, width), jnp.float32),
        compiler_params=pltpu.CompilerParams(
            dimension_semantics=("arbitrary",), vmem_limit_bytes=VMEM_LIMIT
        ),
        cost_estimate=pl.CostEstimate(
            flops=KERNEL_TAPS * rows * width * width // 16, bytes_accessed=rows * width // 8, transcendentals=0
        ),
    )(framed_rows, taps, right)


def framed(block, width):
    count = lax.axis_size("seq")
    forward = [(i, i + 1) for i in range(count - 1)]
    backward = [(i + 1, i) for i in range(count - 1)]
    low = lax.ppermute(block[block.shape[0] - width :], "seq", forward)
    high = lax.ppermute(block[:width], "seq", backward)
    return jnp.concatenate([low, block, high], axis=0)


def scattered(value, order):
    count = lax.axis_size("seq")
    place = lax.axis_index("seq")
    bits = count.bit_length() - 1
    value = value.reshape((2,) * bits + value.shape[1:])
    left = list(range(bits))
    for bit in order:
        dim = left.index(bits - 1 - bit)
        left.remove(bits - 1 - bit)
        mine = (place >> bit) & 1
        keep = lax.dynamic_index_in_dim(value, mine, dim, keepdims=False)
        send = lax.dynamic_index_in_dim(value, 1 - mine, dim, keepdims=False).astype(jnp.bfloat16)
        came = lax.ppermute(send, "seq", [(i, i ^ (1 << bit)) for i in range(count)])
        value = keep + came.astype(jnp.float32)
    return value


def body(
    tokens,
    cotangent,
    seq_lengths,
    residue_mask,
    first_gain,
    first_shift,
    proj_in,
    in_bias,
    mid_gain,
    mid_shift,
    conv_weight,
    conv_bias,
    last_gain,
    last_shift,
    proj_out,
    out_bias,
):
    micro, rows, half = tokens.shape
    inner_half = in_bias.shape[0]
    inner = 2 * inner_half
    model = 2 * half
    seq_count = lax.axis_size("seq")
    count = 256
    side = lax.axis_index("ch")
    side_array = side.astype(jnp.int32).reshape(1)
    low_side = side == 0

    def swap(value):
        return lax.ppermute(value, "ch", SWAP)

    def whole(own, other, axis):
        return jnp.where(
            low_side,
            jnp.concatenate([own, other], axis=axis),
            jnp.concatenate([other, own], axis=axis),
        )

    def own_of(value):
        return lax.dynamic_index_in_dim(value, side, 0, keepdims=False)

    def other_of(value):
        return lax.dynamic_index_in_dim(value, 1 - side, 0, keepdims=False)

    own_vectors = jnp.concatenate(
        [first_gain, first_shift, out_bias, in_bias, mid_gain, mid_shift, conv_bias, last_gain, last_shift]
    )
    part_in = proj_in.shape[0]
    part_conv = conv_weight.shape[1]
    own_weights = jnp.concatenate(
        [proj_in, proj_out.T, conv_weight.reshape(KERNEL_TAPS * part_conv, inner_half)], axis=0
    )
    own_vectors, own_weights = lax.optimization_barrier((own_vectors, own_weights))
    other_vectors, other_weights = swap(own_vectors), swap(own_weights)
    tokens_tied, other_vectors, other_weights = lax.optimization_barrier(
        (other_of(tokens), other_vectors, other_weights)
    )
    both = whole(own_weights, other_weights, 1)
    vectors = jnp.where(
        low_side, jnp.stack([own_vectors, other_vectors]), jnp.stack([other_vectors, own_vectors])
    )
    x_own = own_of(tokens)
    x_other = swap(tokens_tied)
    gy_own = own_of(cotangent)
    gy_tied, _ = lax.optimization_barrier((other_of(cotangent), x_other))
    gy_other = swap(gy_tied)

    gathered = lax.all_gather(both, "seq", axis=0)
    weight_in = gathered[:, :part_in].reshape(model, inner)
    weight_out = gathered[:, part_in : 2 * part_in].reshape(model, inner)
    weight_conv = (
        gathered[:, 2 * part_in :]
        .reshape(seq_count, KERNEL_TAPS, part_conv, inner)
        .transpose(1, 0, 2, 3)
        .reshape(KERNEL_TAPS, inner, inner)
    )
    wide = jnp.stack([vectors[:, i * half : (i + 1) * half].reshape(-1) for i in range(3)])
    narrow = jnp.stack(
        [
            vectors[:, 3 * half + i * inner_half : 3 * half + (i + 1) * inner_half].reshape(-1)
            for i in range(6)
        ]
    )

    places = lax.axis_index("seq") * rows + jnp.arange(rows + 2 * HALO, dtype=jnp.int32) - HALO
    inside = (places >= 0) & (places < rows * seq_count)
    bounds = jnp.cumsum(own_of(seq_lengths))[:-1]
    segment = jnp.sum((places[:, None] >= bounds[None, :]).astype(jnp.int32), axis=1)
    segment = jnp.where(inside, segment, -1)
    middle = segment[HALO : HALO + rows]
    tap_list = [
        (segment[tap * DILATION_STEP : tap * DILATION_STEP + rows] == middle).astype(jnp.bfloat16)
        for tap in range(KERNEL_TAPS)
    ]
    taps = jnp.stack(tap_list, axis=1)
    keep = own_of(residue_mask).astype(jnp.float32)[:, None]
    f32, bf16 = jnp.float32, jnp.bfloat16
    product = 2 * rows * model * inner

    a1, s1, h1, a2, s2 = row_call(
        first_kernel,
        side_array,
        rows,
        count,
        [(x_own, "rows"), (x_other, "rows"), (keep, "rows"), (weight_in, "once"), (wide, "once"), (narrow, "once")],
        [(model, bf16, "rows"), (model, f32, "rows"), (inner, f32, "rows"), (inner, bf16, "rows"), (inner, f32, "rows")],
        product,
    )
    a2 = framed(a2, HALO)
    h3, a3, s3, out_own, out_other = row_call(
        second_kernel,
        side_array,
        rows,
        count,
        [
            (x_own, "rows"),
            (x_other, "rows"),
            (taps, "rows"),
            (a2, "once"),
            (weight_conv.reshape(KERNEL_TAPS * inner, inner), "once"),
            (weight_out, "once"),
            (wide, "once"),
            (narrow, "once"),
        ],
        [(inner, f32, "rows"), (inner, bf16, "rows"), (inner, f32, "rows"), (half, bf16, "rows"), (half, bf16, "rows")],
        4 * product,
    )
    out_back = swap(out_other)

    dh3, gy, wide_sum_3, sum_3 = row_call(
        third_kernel,
        side_array,
        rows,
        count,
        [(gy_own, "rows"), (gy_other, "rows"), (h3, "rows"), (s3, "rows"), (weight_out, "once"), (narrow, "once")],
        [(inner, bf16, "rows"), (model, bf16, "rows"), (model, f32, "sum"), (inner, f32, "sum")],
        product,
    )
    dh3_framed = framed(dh3, HALO)
    grad_out = matrix_grad(gy, a3, 2)
    grad_conv = conv_grad(a2, jnp.stack(tap_list, axis=0)[:, :, None], dh3)
    dh3_framed, out_back = lax.optimization_barrier((dh3_framed, out_back))
    flipped = jnp.flip(weight_conv, 0).transpose(0, 2, 1).reshape(KERNEL_TAPS * inner, inner)
    dh1, dx_own, dx_other, wide_sum_1, sum_1 = row_call(
        fourth_kernel,
        side_array,
        rows,
        count,
        [
            (x_own, "rows"),
            (x_other, "rows"),
            (gy_own, "rows"),
            (taps, "rows"),
            (dh3_framed, "once"),
            (flipped, "once"),
            (h1, "rows"),
            (s2, "rows"),
            (s1, "rows"),
            (weight_in, "once"),
            (wide, "once"),
            (narrow, "once"),
        ],
        [(inner, bf16, "rows"), (half, f32, "rows"), (half, bf16, "rows"), (model, f32, "sum"), (inner, f32, "sum")],
        4 * product,
    )
    dx_back = swap(dx_other)
    grad_in = matrix_grad(a1, dh1, 2)

    def placed(own, back):
        return jnp.where(low_side, jnp.stack([own, back], 0), jnp.stack([back, own], 0))

    block_out = placed(out_own, out_back)
    grad_tokens = placed(
        dx_own, dx_back.astype(f32) + other_of(cotangent).astype(f32)
    )

    bits = list(range(seq_count.bit_length() - 1))
    swapped_bits = [bits[0]] + bits[2:] + [bits[1]]
    part = jnp.concatenate(
        [
            scattered(grad_in.reshape(seq_count, part_in, inner), bits),
            scattered(grad_out.reshape(seq_count, part_in, inner), swapped_bits),
            scattered(
                grad_conv.reshape(KERNEL_TAPS, seq_count, part_conv, inner).transpose(1, 0, 2, 3), bits
            ).reshape(KERNEL_TAPS * part_conv, inner),
        ],
        axis=0,
    )
    left, right = part[:, :inner_half], part[:, inner_half:]
    part_other = swap(jnp.where(low_side, right, left).astype(bf16))
    part = jnp.where(low_side, left, right) + part_other.astype(f32)

    smalls = jnp.concatenate(
        [
            small.reshape(2, -1)
            for small in (wide_sum_1[0], wide_sum_1[1], wide_sum_3[0], sum_1[0], sum_1[1], sum_1[2], sum_3[0], sum_3[1], sum_3[2])
        ],
        axis=1,
    )
    totals = smalls
    for bit in bits:
        totals = totals + lax.ppermute(totals, "seq", [(i, i ^ (1 << bit)) for i in range(seq_count)])
    totals = own_of(totals) + swap(other_of(totals))
    sizes = [half] * 3 + [inner_half] * 6
    parts = []
    at = 0
    for size in sizes:
        parts.append(totals[at : at + size])
        at += size
    return (
        block_out,
        grad_tokens,
        parts[0],
        parts[1],
        part[:part_in],
        parts[3],
        parts[4],
        parts[5],
        part[2 * part_in :].reshape(KERNEL_TAPS, part_conv, inner_half),
        parts[6],
        parts[7],
        parts[8],
        part[part_in : 2 * part_in].T,
        parts[2],
    )


BLOCK = 256
CHUNKS = 4
CONV_PAD = 8
HEAD = 5


def fast_kernel(
    tokens, cot, own_weights, own_vectors, masks,
    out_own, out_back, dx_own, dx_back, dx_tail, dx_end, grads_out, sums_out,
    x_other, g_conv, s1, h1, s2, h3, s3,
    other_vectors, other_weights, wide, narrow, stage,
    a1v, a2f, a3v, gyv, dh3f, out_send, w_in, w_out, w_conv,
    k_in, s_in, r0_in, r1_in, r2_in, r3_in,
    k_out, s_out, r0_out, r1_out, r2_out, r3_out,
    k_low, s_low, r0_low, r1_low, r2_low, r3_low,
    k_mid, s_mid, r0_mid, r1_mid, r2_mid, r3_mid,
    k_top, s_top, r0_top, r1_top, r2_top, r3_top,
    smalls, grads, cross_send, cross_recv, small_send, small_recv, load_sems,
    swap_sems, token_sems, in_gather, out_gather, conv_gather, gy_sems, out_sems, dx_sems, a2_sems, dh3_sems, in_sems, out_rs_sems, low_sems, mid_sems, top_sems, cross_sems, small_sems,
):
    rows = a1v.shape[0]
    half = tokens.shape[2]
    inner = narrow.shape[1]
    part = rows // CHUNKS
    side = lax.axis_index("ch")
    place = lax.axis_index("seq")
    last = lax.axis_size("seq") - 1
    low = side == 0
    bits = [lax.rem(place // (1 << bit), 2) for bit in range(4)]
    across = {"ch": 1 - side}
    pairs = [{"seq": place + (1 << bit) * (1 - 2 * bits[bit])} for bit in range(4)]
    before, after = {"seq": place - 1}, {"seq": place + 1}

    def remote(src, dst, sems, at, device):
        return pltpu.make_async_remote_copy(
            src_ref=src,
            dst_ref=dst,
            send_sem=sems.at[0, at],
            recv_sem=sems.at[1, at],
            device_id=device,
            device_id_type=pl.DeviceIdType.MESH,
        )

    def block(ref, at):
        return ref.at[pl.ds(pl.multiple_of(at * BLOCK, BLOCK), BLOCK)]


    def gy_copy(at):
        piece = pl.ds(at * part, part)
        return remote(cot.at[1 - side, piece], gyv.at[side, piece], gy_sems, at, across)

    def token_copy(at):
        piece = pl.ds(pl.multiple_of(at * part, part), part)
        return remote(tokens.at[1 - side, piece], x_other.at[piece], token_sems, at, across)

    part_in = w_in.shape[4]
    tail_rows = k_top.shape[1]
    own_gy = pltpu.make_async_copy(cot.at[side], gyv.at[side], load_sems.at[0])
    def out_copy(at):
        return remote(block(out_send, at), block(out_back, at), out_sems, at, across)

    def dx_copy(at):
        return remote(block(gyv.at[1 - side], at), block(dx_back, at), dx_sems, at, across)

    def halo_low(framed_rows, sems):
        return remote(framed_rows.at[pl.ds(HALO, HALO)], framed_rows.at[pl.ds(HALO + rows, HALO)], sems, 0, before)

    def halo_high(framed_rows, sems):
        return remote(framed_rows.at[pl.ds(rows, HALO)], framed_rows.at[pl.ds(0, HALO)], sems, 1, after)

    def halo_start(framed_rows, sems):
        @pl.when(place > 0)
        def _():
            halo_low(framed_rows, sems).start()

        @pl.when(place < last)
        def _():
            halo_high(framed_rows, sems).start()

    def halo_wait(framed_rows, sems):
        @pl.when(place > 0)
        def _():
            halo_low(framed_rows, sems).wait_send()
            halo_high(framed_rows, sems).wait_recv()

        @pl.when(place < last)
        def _():
            halo_high(framed_rows, sems).wait_send()
            halo_low(framed_rows, sems).wait_recv()

    blocks = rows // BLOCK
    per = part // BLOCK

    def middle_first(step):
        late = step // (blocks - 2)
        return (step + 1) * (1 - late) + late * (step - (blocks - 2)) * (blocks - 1)

    def in_order(step):
        return step

    def pipeline(step, order, ins, outs, tail=None, count=None):
        def spec(ref):
            return pl.BlockSpec((BLOCK, ref.shape[-1]), lambda i: (order(i), 0))

        out_specs = [spec(r) for r in outs]
        if tail is not None:
            ahead, end = tail
            most = blocks - 2 - HEAD
            outs = outs + [ahead, end]
            out_specs.append(
                pl.BlockSpec((BLOCK, half), lambda i: (jnp.minimum(jnp.maximum(i - HEAD, 0), most), 0))
            )
            out_specs.append(pl.BlockSpec((BLOCK, half), lambda i: (0, 0)))
        pltpu.emit_pipeline(step, grid=(count or blocks,), in_specs=[spec(r) for r in ins], out_specs=out_specs)(*ins, *outs)

    barrier = pltpu.get_barrier_semaphore()
    ring = [{"seq": lax.rem(place + last, last + 1)}, {"seq": lax.rem(place + 1, last + 1)}]
    for device in [across] + pairs + ring:
        pl.semaphore_signal(barrier, inc=1, device_id=device, device_id_type=pl.DeviceIdType.MESH)
    pl.semaphore_wait(barrier, 7)

    swaps = [
        remote(own_weights, other_weights, swap_sems, 0, across),
        remote(own_vectors, other_vectors, swap_sems, 1, across),
    ]
    for swap in swaps:
        swap.start()
    for at in range(CHUNKS):
        token_copy(at).start()
    for at in range(CHUNKS):
        gy_copy(at).start()
    own_gy.start()
    smalls[...] = jnp.zeros_like(smalls)

    @pl.when(place == 0)
    def _():
        a2f[0:HALO, :] = jnp.zeros((HALO, inner), jnp.bfloat16)
        dh3f[0:HALO, :] = jnp.zeros((HALO, inner), jnp.bfloat16)

    @pl.when(place == last)
    def _():
        a2f[HALO + rows :, :] = jnp.zeros((HALO, inner), jnp.bfloat16)
        dh3f[HALO + rows :, :] = jnp.zeros((HALO, inner), jnp.bfloat16)

    def both(own, other):
        left, right = ordered(side, own, other)
        return jnp.concatenate([left, right], axis=1)

    for swap in swaps:
        swap.wait()
    rows_here = both(own_weights[...], other_weights[...]).astype(jnp.bfloat16)
    here = (bits[3], bits[2], bits[1], bits[0])
    w_in[here] = rows_here[:part_in]
    w_out[here] = rows_here[part_in : 2 * part_in]
    stage[0, 0, 0] = rows_here[2 * part_in :]
    own_conv = pltpu.make_async_copy(stage.at[0, 0, 0], g_conv.at[here], load_sems.at[1])
    own_conv.start()
    quarter = half // 2
    wanted = quarter + 64
    for index in range(3):
        lanes = slice(index * half, (index + 1) * half)
        wide[index : index + 1, :] = both(own_vectors[:, lanes], other_vectors[:, lanes])
    for index in range(6):
        lanes = slice(3 * half + index * wanted, 3 * half + index * wanted + quarter)
        narrow[index : index + 1, :] = both(own_vectors[:, lanes], other_vectors[:, lanes])

    def gather_copy(group, level):
        ref, sems, order = group
        every = slice(None)
        at = tuple(every if bit in order[:level] else bits[bit] for bit in (3, 2, 1, 0))
        return remote(ref.at[at], ref.at[at], sems, level, pairs[order[level]])

    in_rows = (w_in, in_gather, (3, 2, 1, 0))
    out_rows = (w_out, out_gather, (1, 3, 2, 0))
    conv_rows = (g_conv, conv_gather, (3, 2, 1, 0))

    def gather_next(group, level):
        gather_copy(group, level).wait()
        if level < 3:
            gather_copy(group, level + 1).start()

    gather_copy(in_rows, 0).start()
    gather_copy(out_rows, 0).start()
    own_conv.wait()
    gather_next(in_rows, 0)
    gather_copy(conv_rows, 0).start()
    gather_next(in_rows, 1)
    gather_next(in_rows, 2)
    gather_next(conv_rows, 0)
    gather_next(out_rows, 0)
    gather_next(in_rows, 3)

    def first_chunk(at, _):
        token_copy(at).wait_recv()

        def first(own, other, s1_block, h1_block, s2_block):
            base = pl.multiple_of((at * per + pl.program_id(0)) * BLOCK, BLOCK)
            x = jnp.concatenate(ordered(side, own[...], other[...]), axis=1)
            normed, _ = norm(x)
            act, slope = gelu_both(normed * wide[0:1, :] + wide[1:2, :])
            act = act.astype(jnp.bfloat16)
            a1v[pl.ds(base, BLOCK), :] = act
            s1_block[...] = slope
            value = dot(act, w_in[...].reshape(2 * half, inner)) + narrow[0:1, :]
            h1_block[...] = value
            normed, _ = norm(value)
            act, slope = gelu_both(normed * narrow[1:2, :] + narrow[2:3, :])
            keep = masks[pl.ds(base, BLOCK), KERNEL_TAPS : KERNEL_TAPS + 1].astype(jnp.float32)
            a2f[pl.ds(HALO + base, BLOCK), :] = (act * keep).astype(jnp.bfloat16)
            s2_block[...] = slope * keep

        pipeline(first, lambda i: at * per + i, [tokens.at[side], x_other], [s1, h1, s2], count=per)
        for level, (group, ready) in enumerate(((conv_rows, 1), (out_rows, 1), (out_rows, 2))):

            @pl.when(at == level)
            def _():
                gather_next(group, ready)

        return 0

    lax.fori_loop(0, CHUNKS, first_chunk, 0)
    halo_start(a2f, a2_sems)
    gather_next(conv_rows, 2)
    gather_next(out_rows, 3)
    gather_next(conv_rows, 3)

    height = inner // 16

    def conv_load(pair):
        return pltpu.make_async_copy(g_conv.at[pair // 2, pair % 2], stage.at[pair % 2], load_sems.at[2 + pair % 2])

    conv_load(0).start()
    conv_load(1).start()

    def relay(pair, _):
        conv_load(pair).wait()
        for low_bit in range(2):
            even = stage[pair % 2, low_bit, 0].astype(jnp.float32)
            odd = stage[pair % 2, low_bit, 1].astype(jnp.float32)
            at = pl.multiple_of((2 * pair + low_bit) * 2 * height, 2 * height)
            for tap in range(KERNEL_TAPS):
                top = tap * height
                w_conv[tap, pl.ds(at, 2 * height), :] = jnp.concatenate(
                    [even[top : top + height], odd[top : top + height]], axis=0
                ).astype(jnp.bfloat16)

        @pl.when(pair < 2)
        def _():
            conv_load(pair + 2).start()

        return 0

    lax.fori_loop(0, 4, relay, 0)

    def second(own, other, h3_block, s3_block, own_block):
        step = pl.program_id(0)
        at = middle_first(step)
        base = pl.multiple_of(at * BLOCK, BLOCK)

        @pl.when(step == blocks - 2)
        def _():
            halo_wait(a2f, a2_sems)

        taps = masks[pl.ds(base, BLOCK), :]
        weight = w_conv[...].reshape(KERNEL_TAPS * inner, inner)
        value = dot(windowed(a2f, taps, base, BLOCK), weight) + narrow[3:4, :]
        h3_block[...] = value
        normed, _ = norm(value)
        act, slope = gelu_both(normed * narrow[4:5, :] + narrow[5:6, :])
        act = act.astype(jnp.bfloat16)
        a3v[pl.ds(base, BLOCK), :] = act
        s3_block[...] = slope
        mixed = dot(act, w_out[...].reshape(2 * half, inner), ((1,), (1,))) + wide[2:3, :]
        left, right = mixed[:, :half], mixed[:, half:]
        own_block[...] = (own[...].astype(jnp.float32) + jnp.where(low, left, right)).astype(jnp.bfloat16)
        out_send[pl.ds(base, BLOCK), :] = (
            other[...].astype(jnp.float32) + jnp.where(low, right, left)
        ).astype(jnp.bfloat16)
        out_copy(at).start()

    pipeline(second, middle_first, [tokens.at[side], x_other], [h3, s3, out_own])

    def add_small(row, value):
        smalls[row : row + 1, :] += value

    def add_wide(row, value):
        smalls[row : row + 1, :] += value[:, :half]
        smalls[row + 1 : row + 2, :] += value[:, half:]

    def third(h3_block, s3_block):
        at = pl.program_id(0)
        base = pl.multiple_of(at * BLOCK, BLOCK)
        for later in range(CHUNKS):

            @pl.when(at == later * per)
            def _():
                gy_copy(later).wait_recv()

        gy = jnp.concatenate([gyv[0, pl.ds(base, BLOCK), :], gyv[1, pl.ds(base, BLOCK), :]], axis=1)
        add_wide(4, column_sums(gy.astype(jnp.float32)))
        dz3 = dot(gy, w_out[...].reshape(2 * half, inner)) * s3_block[...]
        normed, scale = norm(h3_block[...])
        dh3 = norm_back(dz3, normed, scale, narrow[4:5, :]).astype(jnp.bfloat16)
        dh3f[pl.ds(HALO + base, BLOCK), :] = dh3
        add_small(9, column_sums(dh3.astype(jnp.float32)))
        add_small(10, column_sums(dz3 * normed))
        add_small(11, column_sums(dz3))

    own_gy.wait()
    pipeline(third, in_order, [h3, s3], [])
    halo_start(dh3f, dh3_sems)

    def slot(pair, order):
        two = (pair % 4) if order[0] == 1 else (pair % 4) // 2 + 2 * (pair % 2)
        return pair // 4 * 4 + two

    def split(group, at, even, odd):
        keep_ref, send_ref = group[0], group[1]
        mine_first = bits[0] == 0
        keep_ref[at] = jnp.where(mine_first, even, odd)
        send_ref[at] = jnp.where(mine_first, odd, even).astype(jnp.bfloat16)

    def wide_grad(left_of, right_ref, group):
        tall_rows = group[0].shape[1]

        def tile(at, _):
            value = dot(left_of(at), right_ref[...], ((0,), (0,)))
            for pair in range(4):
                top = 2 * pair * tall_rows
                split(
                    group,
                    at * 4 + slot(pair, group[4]),
                    value[top : top + tall_rows],
                    value[top + tall_rows : top + 2 * tall_rows],
                )
            return 0

        lax.fori_loop(0, 2, tile, 0)
        sum_copy(group, 0).start()

    def conv_grad_of(taps, group):
        right = dh3f.at[pl.ds(HALO, rows)]
        values = []
        for tap in taps:
            left = a2f[tap * DILATION_STEP : tap * DILATION_STEP + rows, :] * masks[:, tap : tap + 1]
            values.append(dot(left, right[...], ((0,), (0,))))
        if len(values) == 1:
            tail = [jnp.zeros((CONV_PAD, inner), jnp.float32)]
        else:
            tail = []
        for pair in range(8):
            top = 2 * pair * height
            split(
                group,
                slot(pair, group[4]),
                jnp.concatenate([v[top : top + height] for v in values] + tail, axis=0),
                jnp.concatenate([v[top + height : top + 2 * height] for v in values] + tail, axis=0),
            )
        sum_copy(group, 0).start()

    y_first, z_first = (1, 2, 3), (2, 1, 3)
    in_set = (k_in, s_in, (r0_in, r1_in, r2_in, r3_in), in_sems, y_first)
    out_set = (k_out, s_out, (r0_out, r1_out, r2_out, r3_out), out_rs_sems, z_first)
    low_set = (k_low, s_low, (r0_low, r1_low, r2_low, r3_low), low_sems, y_first)
    mid_set = (k_mid, s_mid, (r0_mid, r1_mid, r2_mid, r3_mid), mid_sems, z_first)
    top_set = (k_top, s_top, (r0_top, r1_top, r2_top, r3_top), top_sems, y_first)
    starts = (0, 0, 4, 6)
    lengths = (8, 4, 2, 1)

    def sum_copy(group, level):
        _, send, received, sems, order = group
        bit = 0 if level == 0 else order[level - 1]
        return remote(
            send.at[pl.ds(starts[level], lengths[level])], received[level], sems, level, pairs[bit]
        )

    def sum_step(group, level):
        keep, send, received, _, order = group
        sum_copy(group, level).wait()
        came = received[level]
        fixed = 0
        for at in range(level):
            fixed = fixed + bits[order[at]] * (1 << at)
        if level == 3:
            keep[fixed] = keep[fixed] + came[0].astype(jnp.float32)
            return
        mine = bits[order[level]]

        def one(item, _):
            other = 2 * item + 1 - mine
            same = 2 * item + mine
            send[starts[level + 1] + item] = (
                keep[other * (1 << level) + fixed] + came[other].astype(jnp.float32)
            ).astype(jnp.bfloat16)
            at = same * (1 << level) + fixed
            keep[at] = keep[at] + came[same].astype(jnp.float32)
            return 0

        lax.fori_loop(0, lengths[level + 1], one, 0)
        sum_copy(group, level + 1).start()

    def at_step(step, when, *steps):
        @pl.when(step == when)
        def _():
            for group, level in steps:
                sum_step(group, level)

    conv_grad_of((0, 1), low_set)
    conv_grad_of((2, 3), mid_set)
    conv_grad_of((4,), top_set)
    wide_grad(lambda at: gyv[at], a3v, out_set)

    def fourth(h1_block, s2_block):
        step = pl.program_id(0)
        base = pl.multiple_of(step * BLOCK, BLOCK)
        taps = masks[pl.ds(base, BLOCK), :]
        da2 = jnp.zeros((BLOCK, inner), jnp.float32)
        for tap in range(KERNEL_TAPS):
            window = dh3f[pl.ds(base + tap * DILATION_STEP, BLOCK), :] * taps[:, tap : tap + 1]
            da2 = da2 + dot(window, w_conv[KERNEL_TAPS - 1 - tap], ((1,), (1,)))
        dz2 = da2 * s2_block[...]
        normed, scale = norm(h1_block[...])
        dh1 = norm_back(dz2, normed, scale, narrow[1:2, :]).astype(jnp.bfloat16)
        a3v[pl.ds(base, BLOCK), :] = dh1
        add_small(6, column_sums(dh1.astype(jnp.float32)))
        add_small(7, column_sums(dz2 * normed))
        add_small(8, column_sums(dz2))
        at_step(step, 0, (low_set, 0), (mid_set, 0), (top_set, 0))
        at_step(step, 1, (out_set, 0))
        at_step(step, 5, (low_set, 1))
        at_step(step, 6, (mid_set, 1))
        at_step(step, 7, (top_set, 1))

    halo_wait(dh3f, dh3_sems)
    pipeline(fourth, in_order, [h1, s2], [])
    wide_grad(lambda at: a1v[:, pl.ds(pl.multiple_of(at * half, 128), half)], a3v, in_set)
    sum_step(out_set, 1)
    sum_step(low_set, 2)

    def fifth(own, other, s1_block, own_block, tail_block, end_block):
        step = pl.program_id(0)
        base = pl.multiple_of(step * BLOCK, BLOCK)
        dh1 = a3v[pl.ds(base, BLOCK), :]
        dz1 = dot(dh1, w_in[...].reshape(2 * half, inner), ((1,), (1,))) * s1_block[...]
        x = jnp.concatenate(ordered(side, own[...], other[...]), axis=1)
        normed, scale = norm(x)
        dx = norm_back(dz1, normed, scale, wide[0:1, :])
        add_wide(0, column_sums(dz1 * normed))
        add_wide(2, column_sums(dz1))
        left, right = dx[:, :half], dx[:, half:]
        own_block[...] = jnp.where(low, left, right) + gyv[side, pl.ds(base, BLOCK), :].astype(jnp.float32)
        sent = jnp.where(low, right, left).astype(jnp.bfloat16)
        gyv[1 - side, pl.ds(base, BLOCK), :] = sent
        end_block[...] = sent

        @pl.when(step < blocks - 1)
        def _():
            tail_block[...] = sent

        @pl.when(step < HEAD - 1)
        def _():
            dx_copy(step).start()

        at_step(step, 0, (mid_set, 2), (in_set, 0))
        at_step(step, 2, (out_set, 2), (top_set, 2))
        at_step(step, 4, (low_set, 3))
        at_step(step, 5, (mid_set, 3))
        at_step(step, 6, (in_set, 1))
        at_step(step, 7, (top_set, 3), (out_set, 3))

    pipeline(fifth, in_order, [tokens.at[side], x_other, s1], [dx_own], (dx_tail, dx_end))


    def small_copy(level):
        device = pairs[level] if level < 4 else across
        return remote(small_send.at[level], small_recv.at[level], small_sems, level, device)

    def small_start(level):
        small_send[level] = smalls[...]
        small_copy(level).start()

    def small_step(level):
        small_copy(level).wait()
        smalls[...] += small_recv[level]

    small_start(0)
    sum_step(in_set, 2)
    small_step(0)
    small_start(1)
    small_step(1)
    small_start(2)
    small_step(2)
    small_start(3)
    sum_step(in_set, 3)
    small_step(3)
    small_start(4)

    row = 0
    for keep, _, _, _, order in (in_set, out_set, low_set, mid_set, top_set):
        mine = bits[order[0]] + 2 * bits[order[1]] + 4 * bits[order[2]]
        height = keep.shape[1]
        value = keep[mine]
        left, right = value[:, :wanted], value[:, inner - wanted :]
        grads[row : row + height, :] = jnp.where(low, left, right)
        cross_send[row : row + height, :] = jnp.where(low, right, left).astype(jnp.bfloat16)
        row += height
    cross = remote(cross_send, cross_recv, cross_sems, 0, across)
    cross.start()
    dx_copy(HEAD - 1).start()
    for at in range(CHUNKS):
        token_copy(at).wait_send()
        gy_copy(at).wait_send()
    for at in range(blocks):
        out_copy(at).wait()
    small_step(4)
    for index in range(3):
        both = smalls[2 * index : 2 * index + 2, :]
        sums_out[:, index * half : (index + 1) * half] = jnp.where(low, both[0:1], both[1:2])
    for index in range(6):
        both = smalls[6 + index : 7 + index, :]
        at = 3 * half + index * wanted
        sums_out[:, at : at + quarter] = jnp.where(low, both[:, :quarter], both[:, quarter:])
    cross.wait()
    total = grads[...] + cross_recv[...].astype(jnp.float32)
    grads_out[...] = jnp.where(low, total[:, :quarter], total[:, wanted - quarter :])
    for at in range(HEAD):
        dx_copy(at).wait()


def fast_call(tokens, cot, own_weights, own_vectors, masks, part_in, part_conv):
    _, rows, half = tokens.shape
    model = 2 * half
    inner = 2 * own_weights.shape[1]
    f32, bf16 = jnp.float32, jnp.bfloat16
    tall = KERNEL_TAPS * part_conv + CONV_PAD
    any_spec = pl.BlockSpec(memory_space=pl.ANY)
    vmem_spec = pl.BlockSpec(memory_space=pltpu.VMEM)
    total = 2 * part_in + tall
    wanted = half // 2 + 64

    def sums(height):
        return [pltpu.VMEM((8, height, inner), f32), pltpu.VMEM((8, height, inner), bf16)] + [
            pltpu.VMEM((length, height, inner), bf16) for length in (8, 4, 2, 1)
        ]

    def sems(count):
        return pltpu.SemaphoreType.DMA((2, count))

    shapes = [
        ((rows, half), bf16),
        ((rows, half), bf16),
        ((rows, half), f32),
        ((rows, half), bf16),
        ((rows - (HEAD + 1) * BLOCK, half), bf16),
        ((BLOCK, half), bf16),
        ((total, half // 2), f32),
        ((1, 3 * half + 6 * wanted), f32),
        ((rows, half), bf16),
        ((2, 2, 2, 2, tall, inner), bf16),
        ((rows, model), f32),
        ((rows, inner), f32),
        ((rows, inner), f32),
        ((rows, inner), f32),
        ((rows, inner), f32),
    ]
    flops = 6 * rows * (2 * model * inner + KERNEL_TAPS * inner * inner)
    results = pl.pallas_call(
        fast_kernel,
        out_shape=[jax.ShapeDtypeStruct(shape, dtype) for shape, dtype in shapes],
        in_specs=[any_spec] * 2 + [vmem_spec] * 3,
        out_specs=[any_spec] * 6 + [vmem_spec] * 2 + [any_spec] * 7,
        scratch_shapes=[
            pltpu.VMEM(own_vectors.shape, f32),
            pltpu.VMEM(own_weights.shape, bf16),
            pltpu.VMEM((8, model), f32),
            pltpu.VMEM((8, inner), f32),
            pltpu.VMEM((2, 2, 2, tall, inner), bf16),
            pltpu.VMEM((rows, model), bf16),
            pltpu.VMEM((rows + 2 * HALO, inner), bf16),
            pltpu.VMEM((rows, inner), bf16),
            pltpu.VMEM((2, rows, half), bf16),
            pltpu.VMEM((rows + 2 * HALO, inner), bf16),
            pltpu.VMEM((rows, half), bf16),
            pltpu.VMEM((2, 2, 2, 2, part_in, inner), bf16),
            pltpu.VMEM((2, 2, 2, 2, part_in, inner), bf16),
            pltpu.VMEM((KERNEL_TAPS, inner, inner), bf16),
        ]
        + sums(part_in) * 4
        + sums(tall - 2 * part_in)
        + [
            pltpu.VMEM((16, inner), f32),
            pltpu.VMEM((total, wanted), f32),
            pltpu.VMEM((total, wanted), bf16),
            pltpu.VMEM((total, wanted), bf16),
            pltpu.VMEM((5, 16, inner), f32),
            pltpu.VMEM((5, 16, inner), f32),
            pltpu.SemaphoreType.DMA((4,)),
            sems(2),
            sems(CHUNKS),
            sems(4),
            sems(4),
            sems(4),
            sems(CHUNKS),
            sems(rows // BLOCK),
            sems(HEAD),
            sems(2),
            sems(2),
            sems(4),
            sems(4),
            sems(4),
            sems(4),
            sems(4),
            sems(1),
            sems(5),
        ],
        compiler_params=pltpu.CompilerParams(
            collective_id=0, has_side_effects=True, vmem_limit_bytes=65280 * 2**10
        ),
        cost_estimate=pl.CostEstimate(flops=flops, bytes_accessed=120 * 2**20, transcendentals=0),
    )(tokens, cot, own_weights, own_vectors, masks)
    return results[:8]


def finish_kernel(side_ref, tail_ref, cot_ref, whole_ref, out_ref):
    out_ref[0] = tail_ref[...].astype(jnp.float32) + cot_ref[0].astype(jnp.float32)


def assemble_kernel(side_ref, out_own, out_back, dx_own, dx_back, cot, block_out, grad_tokens):
    side = side_ref[0]
    block_out[side] = out_own[...]
    block_out[1 - side] = out_back[...]
    grad_tokens[side] = dx_own[...]
    grad_tokens[1 - side] = dx_back[...].astype(jnp.float32) + cot[0].astype(jnp.float32)


def assemble_call(side, out_own, out_back, dx_own, dx_back, cot):
    rows, half = out_own.shape
    tile = 2 * BLOCK
    by_tile = pl.BlockSpec((tile, half), lambda i, side_ref: (i, 0))
    pair = pl.BlockSpec((2, tile, half), lambda i, side_ref: (0, i, 0))
    return pl.pallas_call(
        assemble_kernel,
        grid_spec=pltpu.PrefetchScalarGridSpec(
            num_scalar_prefetch=1,
            grid=(rows // tile,),
            in_specs=[by_tile] * 4
            + [pl.BlockSpec((1, tile, half), lambda i, side_ref: (1 - side_ref[0], i, 0))],
            out_specs=[pair, pair],
        ),
        out_shape=[
            jax.ShapeDtypeStruct((2, rows, half), jnp.bfloat16),
            jax.ShapeDtypeStruct((2, rows, half), jnp.float32),
        ],
        compiler_params=pltpu.CompilerParams(
            dimension_semantics=("arbitrary",), vmem_limit_bytes=56 * 2**20
        ),
        cost_estimate=pl.CostEstimate(flops=rows * half, bytes_accessed=24 * rows * half, transcendentals=0),
    )(side, out_own, out_back, dx_own, dx_back, cot)


def finish_call(side, tail, cot, grad_tokens, first):
    half = tail.shape[1]

    def theirs(i, side_ref):
        return (1 - side_ref[0], first + i, 0)

    return pl.pallas_call(
        finish_kernel,
        grid_spec=pltpu.PrefetchScalarGridSpec(
            num_scalar_prefetch=1,
            grid=(tail.shape[0] // BLOCK,),
            in_specs=[
                pl.BlockSpec((BLOCK, half), lambda i, side_ref: (i, 0)),
                pl.BlockSpec((1, BLOCK, half), theirs),
                pl.BlockSpec(memory_space=pl.ANY),
            ],
            out_specs=pl.BlockSpec((1, BLOCK, half), theirs),
        ),
        out_shape=jax.ShapeDtypeStruct(grad_tokens.shape, grad_tokens.dtype),
        input_output_aliases={3: 0},
        compiler_params=pltpu.CompilerParams(
            dimension_semantics=("arbitrary",), vmem_limit_bytes=63 * 2**20
        ),
        cost_estimate=pl.CostEstimate(flops=tail.size, bytes_accessed=8 * tail.size, transcendentals=0),
    )(side, tail, cot, grad_tokens)


def fast_body(
    tokens,
    cotangent,
    seq_lengths,
    residue_mask,
    first_gain,
    first_shift,
    proj_in,
    in_bias,
    mid_gain,
    mid_shift,
    conv_weight,
    conv_bias,
    last_gain,
    last_shift,
    proj_out,
    out_bias,
):
    micro, rows, half = tokens.shape
    inner_half = in_bias.shape[0]
    inner = 2 * inner_half
    model = 2 * half
    seq_count = lax.axis_size("seq")
    side = lax.axis_index("ch")
    low_side = side == 0
    f32, bf16 = jnp.float32, jnp.bfloat16

    def swap(value):
        return lax.ppermute(value, "ch", SWAP)

    def own_of(value):
        return lax.dynamic_index_in_dim(value, side, 0, keepdims=False)

    def other_of(value):
        return lax.dynamic_index_in_dim(value, 1 - side, 0, keepdims=False)

    gap = jnp.zeros((64,), f32)
    pieces = [first_gain, first_shift, out_bias]
    for piece in (in_bias, mid_gain, mid_shift, conv_bias, last_gain, last_shift):
        pieces += [piece, gap]
    own_vectors = lax.optimization_barrier(jnp.concatenate(pieces))[None]
    part_in = proj_in.shape[0]
    part_conv = conv_weight.shape[1]
    own_weights = jnp.concatenate(
        [
            proj_in,
            proj_out.T,
            conv_weight.reshape(KERNEL_TAPS * part_conv, inner_half),
            jnp.zeros((CONV_PAD, inner_half), bf16),
        ],
        axis=0,
    )

    places = lax.axis_index("seq") * rows + jnp.arange(rows + 2 * HALO, dtype=jnp.int32) - HALO
    inside = (places >= 0) & (places < rows * seq_count)
    bounds = jnp.cumsum(own_of(seq_lengths))[:-1]
    segment = jnp.sum((places[:, None] >= bounds[None, :]).astype(jnp.int32), axis=1)
    segment = jnp.where(inside, segment, -1)
    middle = segment[HALO : HALO + rows]
    columns = [
        (segment[tap * DILATION_STEP : tap * DILATION_STEP + rows] == middle).astype(bf16)
        for tap in range(KERNEL_TAPS)
    ]
    zero = jnp.zeros((rows,), bf16)
    masks = jnp.stack(columns + [own_of(residue_mask).astype(bf16), zero, zero], axis=1)

    out_own, out_back, dx_own, dx_back, dx_tail, dx_end, grads, sums = fast_call(
        tokens, cotangent, own_weights, own_vectors, masks, part_in, part_conv
    )

    side_array = side.astype(jnp.int32).reshape(1)
    tail_back, end_back = swap(dx_tail), swap(dx_end)
    block_out, grad_tokens = assemble_call(side_array, out_own, out_back, dx_own, dx_back, cotangent)
    grad_tokens = finish_call(side_array, tail_back, cotangent, grad_tokens, HEAD)
    grad_tokens = finish_call(side_array, end_back, cotangent, grad_tokens, rows // BLOCK - 1)
    wanted = inner_half + 64

    def narrow_part(index):
        at = 3 * half + index * wanted
        return sums[0, at : at + inner_half]

    return (
        block_out,
        grad_tokens,
        sums[0, :half],
        sums[0, half : 2 * half],
        grads[:part_in],
        narrow_part(0),
        narrow_part(1),
        narrow_part(2),
        grads[2 * part_in : 2 * part_in + KERNEL_TAPS * part_conv].reshape(KERNEL_TAPS, part_conv, inner_half),
        narrow_part(3),
        narrow_part(4),
        narrow_part(5),
        grads[part_in : 2 * part_in].T,
        sums[0, 2 * half : 3 * half],
    )


def solution(mesh):
    placed = (
        P(None, "seq", "ch"),
        P(None, "seq", "ch"),
        P(),
        P(None, "seq"),
        P("ch"),
        P("ch"),
        P("seq", "ch"),
        P("ch"),
        P("ch"),
        P("ch"),
        P(None, "seq", "ch"),
        P("ch"),
        P("ch"),
        P("ch"),
        P("ch", "seq"),
        P("ch"),
    )
    run = fast_body if mesh.shape["seq"] == 16 else body
    return jax.shard_map(
        run,
        mesh=mesh,
        in_specs=placed,
        out_specs=(
            P(None, "seq", "ch"),
            P(None, "seq", "ch"),
            P("ch"),
            P("ch"),
            P("seq", "ch"),
            P("ch"),
            P("ch"),
            P("ch"),
            P(None, "seq", "ch"),
            P("ch"),
            P("ch"),
            P("ch"),
            P("ch", "seq"),
            P("ch"),
        ),
        check_vma=False,
    )
```

```python
import jax
import jax.numpy as jnp
from jax import lax
from jax.experimental import pallas as pl
from jax.experimental.pallas import tpu as pltpu
from jax.sharding import PartitionSpec as P

KERNEL_TAPS = 5
DILATION_STEP = 32
HALO = 64

EPSILON = 1e-05
ROOT_HALF = 0.7071067811865476
ROOT_TAU = 0.3989422804014327
SWAP = [(0, 1), (1, 0)]


def gelu_both(value):
    half = 0.5 * (1.0 + lax.erf(value * ROOT_HALF))
    return value * half, half + value * jnp.exp(-0.5 * value * value) * ROOT_TAU


def norm(value):
    middle = jnp.mean(value, axis=1, keepdims=True)
    centred = value - middle
    scale = lax.rsqrt(jnp.mean(centred * centred, axis=1, keepdims=True) + EPSILON)
    return centred * scale, scale


def norm_back(grad_zed, normed, scale, gain):
    grad_normed = grad_zed * gain
    first = jnp.mean(grad_normed, axis=1, keepdims=True)
    second = jnp.mean(grad_normed * normed, axis=1, keepdims=True)
    return scale * (grad_normed - first - normed * second)


def dot(left, right, over=((1,), (0,))):
    return lax.dot_general(left, right, (over, ((), ())), preferred_element_type=jnp.float32)


def column_sums(value):
    return jnp.sum(value, axis=0, keepdims=True)


def ordered(side, own, other):
    low = side == 0
    own, other = own.astype(jnp.float32), other.astype(jnp.float32)
    return jnp.where(low, own, other), jnp.where(low, other, own)


def windowed(framed_ref, taps, base, count):
    return jnp.concatenate(
        [
            framed_ref[pl.ds(base + tap * DILATION_STEP, count), :] * taps[:, tap : tap + 1]
            for tap in range(KERNEL_TAPS)
        ],
        axis=1,
    )


def first_kernel(side_ref, own_ref, other_ref, keep_ref, weight_ref, wide_ref, narrow_ref, a1_ref, s1_ref, h1_ref, a2_ref, s2_ref):
    x = jnp.concatenate(ordered(side_ref[0], own_ref[...], other_ref[...]), axis=1)
    normed, _ = norm(x)
    act, slope = gelu_both(normed * wide_ref[0:1, :] + wide_ref[1:2, :])
    act = act.astype(jnp.bfloat16)
    a1_ref[...] = act
    s1_ref[...] = slope
    h1 = dot(act, weight_ref[...]) + narrow_ref[0:1, :]
    h1_ref[...] = h1
    normed, _ = norm(h1)
    act, slope = gelu_both(normed * narrow_ref[1:2, :] + narrow_ref[2:3, :])
    keep = keep_ref[...]
    a2_ref[...] = (act * keep).astype(jnp.bfloat16)
    s2_ref[...] = slope * keep


def second_kernel(side_ref, own_ref, other_ref, taps_ref, framed_ref, conv_ref, weight_ref, wide_ref, narrow_ref, h3_ref, a3_ref, s3_ref, out_own_ref, out_other_ref):
    count = own_ref.shape[0]
    half = own_ref.shape[1]
    base = pl.multiple_of(pl.program_id(0) * count, count)
    h3 = dot(windowed(framed_ref, taps_ref[...], base, count), conv_ref[...]) + narrow_ref[3:4, :]
    h3_ref[...] = h3
    normed, _ = norm(h3)
    act, slope = gelu_both(normed * narrow_ref[4:5, :] + narrow_ref[5:6, :])
    act = act.astype(jnp.bfloat16)
    a3_ref[...] = act
    s3_ref[...] = slope
    mixed = dot(act, weight_ref[...], ((1,), (1,))) + wide_ref[2:3, :]
    left, right = mixed[:, :half], mixed[:, half:]
    low = side_ref[0] == 0
    out_own_ref[...] = (own_ref[...].astype(jnp.float32) + jnp.where(low, left, right)).astype(jnp.bfloat16)
    out_other_ref[...] = (other_ref[...].astype(jnp.float32) + jnp.where(low, right, left)).astype(jnp.bfloat16)


def third_kernel(side_ref, own_ref, other_ref, h3_ref, s3_ref, weight_ref, narrow_ref, dh3_ref, gy_ref, wide_sum_ref, sum_ref):
    @pl.when(pl.program_id(0) == 0)
    def _():
        wide_sum_ref[...] = jnp.zeros_like(wide_sum_ref)
        sum_ref[...] = jnp.zeros_like(sum_ref)

    gy = jnp.concatenate(ordered(side_ref[0], own_ref[...], other_ref[...]), axis=1)
    wide_sum_ref[0:1, :] += column_sums(gy)
    gy = gy.astype(jnp.bfloat16)
    gy_ref[...] = gy
    dz3 = dot(gy, weight_ref[...]) * s3_ref[...]
    normed, scale = norm(h3_ref[...])
    dh3 = norm_back(dz3, normed, scale, narrow_ref[4:5, :]).astype(jnp.bfloat16)
    dh3_ref[...] = dh3
    sum_ref[0:1, :] += column_sums(dh3.astype(jnp.float32))
    sum_ref[1:2, :] += column_sums(dz3 * normed)
    sum_ref[2:3, :] += column_sums(dz3)


def fourth_kernel(side_ref, own_ref, other_ref, gy_own_ref, taps_ref, framed_ref, conv_ref, h1_ref, s2_ref, s1_ref, weight_ref, wide_ref, narrow_ref, dh1_ref, dx_own_ref, dx_other_ref, wide_sum_ref, sum_ref):
    @pl.when(pl.program_id(0) == 0)
    def _():
        wide_sum_ref[...] = jnp.zeros_like(wide_sum_ref)
        sum_ref[...] = jnp.zeros_like(sum_ref)

    count = own_ref.shape[0]
    half = own_ref.shape[1]
    base = pl.multiple_of(pl.program_id(0) * count, count)
    dz2 = dot(windowed(framed_ref, taps_ref[...], base, count), conv_ref[...]) * s2_ref[...]
    normed, scale = norm(h1_ref[...])
    dh1 = norm_back(dz2, normed, scale, narrow_ref[1:2, :]).astype(jnp.bfloat16)
    dh1_ref[...] = dh1
    sum_ref[0:1, :] += column_sums(dh1.astype(jnp.float32))
    sum_ref[1:2, :] += column_sums(dz2 * normed)
    sum_ref[2:3, :] += column_sums(dz2)
    dz1 = dot(dh1, weight_ref[...], ((1,), (1,))) * s1_ref[...]
    x = jnp.concatenate(ordered(side_ref[0], own_ref[...], other_ref[...]), axis=1)
    normed, scale = norm(x)
    dx = norm_back(dz1, normed, scale, wide_ref[0:1, :])
    wide_sum_ref[0:1, :] += column_sums(dz1 * normed)
    wide_sum_ref[1:2, :] += column_sums(dz1)
    low = side_ref[0] == 0
    left, right = dx[:, :half], dx[:, half:]
    dx_own_ref[...] = jnp.where(low, left, right) + gy_own_ref[...].astype(jnp.float32)
    dx_other_ref[...] = jnp.where(low, right, left).astype(jnp.bfloat16)


def grad_kernel(left_ref, right_ref, out_ref):
    out_ref[...] = dot(left_ref[...], right_ref[...], ((0,), (0,)))


def conv_grad_kernel(framed_ref, taps_ref, right_ref, out_ref):
    tap = pl.program_id(0)
    count = right_ref.shape[0]
    base = pl.multiple_of(tap * DILATION_STEP, DILATION_STEP)
    left = framed_ref[pl.ds(base, count), :] * taps_ref[0]
    out_ref[0] = dot(left, right_ref[...], ((0,), (0,)))


VMEM_LIMIT = 56 * 2**20


def once(shape):
    return pl.BlockSpec(shape, lambda *_: (0,) * len(shape), pipeline_mode=pl.Buffered(1))


def by_rows(count, width):
    return pl.BlockSpec((count, width), lambda i, *_: (i, 0))


def row_call(kernel, side, rows, count, operands, outs, flops):
    in_specs = [by_rows(count, a.shape[1]) if how == "rows" else once(a.shape) for a, how in operands]
    out_specs = [
        by_rows(count, width) if how == "rows" else pl.BlockSpec((8, width), lambda i, *_: (0, 0))
        for width, _, how in outs
    ]
    out_shape = [
        jax.ShapeDtypeStruct((rows if how == "rows" else 8, width), dtype) for width, dtype, how in outs
    ]
    moved = sum(a.size * a.dtype.itemsize for a, _ in operands)
    moved += sum(o.size * o.dtype.itemsize for o in out_shape)
    return pl.pallas_call(
        kernel,
        grid_spec=pltpu.PrefetchScalarGridSpec(
            num_scalar_prefetch=1, grid=(rows // count,), in_specs=in_specs, out_specs=out_specs
        ),
        out_shape=out_shape,
        compiler_params=pltpu.CompilerParams(
            dimension_semantics=("arbitrary",), vmem_limit_bytes=VMEM_LIMIT
        ),
        cost_estimate=pl.CostEstimate(flops=flops // 32, bytes_accessed=moved // 32, transcendentals=0),
    )(side, *[a for a, _ in operands])


def matrix_grad(left, right, tiles):
    rows, height = left.shape
    width = right.shape[1]
    return pl.pallas_call(
        grad_kernel,
        grid=(tiles,),
        in_specs=[pl.BlockSpec((rows, height // tiles), lambda i: (0, i)), once((rows, width))],
        out_specs=pl.BlockSpec((height // tiles, width), lambda i: (i, 0)),
        out_shape=jax.ShapeDtypeStruct((height, width), jnp.float32),
        compiler_params=pltpu.CompilerParams(
            dimension_semantics=("arbitrary",), vmem_limit_bytes=VMEM_LIMIT
        ),
        cost_estimate=pl.CostEstimate(
            flops=rows * height * width // 16, bytes_accessed=rows * (height + width) // 16, transcendentals=0
        ),
    )(left, right)


def conv_grad(framed_rows, taps, right):
    rows, width = right.shape
    return pl.pallas_call(
        conv_grad_kernel,
        grid=(KERNEL_TAPS,),
        in_specs=[
            once(framed_rows.shape),
            pl.BlockSpec((1, rows, 1), lambda i: (i, 0, 0)),
            once((rows, width)),
        ],
        out_specs=pl.BlockSpec((1, width, width), lambda i: (i, 0, 0)),
        out_shape=jax.ShapeDtypeStruct((KERNEL_TAPS, width, width), jnp.float32),
        compiler_params=pltpu.CompilerParams(
            dimension_semantics=("arbitrary",), vmem_limit_bytes=VMEM_LIMIT
        ),
        cost_estimate=pl.CostEstimate(
            flops=KERNEL_TAPS * rows * width * width // 16, bytes_accessed=rows * width // 8, transcendentals=0
        ),
    )(framed_rows, taps, right)


def framed(block, width):
    count = lax.axis_size("seq")
    forward = [(i, i + 1) for i in range(count - 1)]
    backward = [(i + 1, i) for i in range(count - 1)]
    low = lax.ppermute(block[block.shape[0] - width :], "seq", forward)
    high = lax.ppermute(block[:width], "seq", backward)
    return jnp.concatenate([low, block, high], axis=0)


def scattered(value, order):
    count = lax.axis_size("seq")
    place = lax.axis_index("seq")
    bits = count.bit_length() - 1
    value = value.reshape((2,) * bits + value.shape[1:])
    left = list(range(bits))
    for bit in order:
        dim = left.index(bits - 1 - bit)
        left.remove(bits - 1 - bit)
        mine = (place >> bit) & 1
        keep = lax.dynamic_index_in_dim(value, mine, dim, keepdims=False)
        send = lax.dynamic_index_in_dim(value, 1 - mine, dim, keepdims=False).astype(jnp.bfloat16)
        came = lax.ppermute(send, "seq", [(i, i ^ (1 << bit)) for i in range(count)])
        value = keep + came.astype(jnp.float32)
    return value


def body(
    tokens,
    cotangent,
    seq_lengths,
    residue_mask,
    first_gain,
    first_shift,
    proj_in,
    in_bias,
    mid_gain,
    mid_shift,
    conv_weight,
    conv_bias,
    last_gain,
    last_shift,
    proj_out,
    out_bias,
):
    micro, rows, half = tokens.shape
    inner_half = in_bias.shape[0]
    inner = 2 * inner_half
    model = 2 * half
    seq_count = lax.axis_size("seq")
    count = 256
    side = lax.axis_index("ch")
    side_array = side.astype(jnp.int32).reshape(1)
    low_side = side == 0

    def swap(value):
        return lax.ppermute(value, "ch", SWAP)

    def whole(own, other, axis):
        return jnp.where(
            low_side,
            jnp.concatenate([own, other], axis=axis),
            jnp.concatenate([other, own], axis=axis),
        )

    def own_of(value):
        return lax.dynamic_index_in_dim(value, side, 0, keepdims=False)

    def other_of(value):
        return lax.dynamic_index_in_dim(value, 1 - side, 0, keepdims=False)

    own_vectors = jnp.concatenate(
        [first_gain, first_shift, out_bias, in_bias, mid_gain, mid_shift, conv_bias, last_gain, last_shift]
    )
    part_in = proj_in.shape[0]
    part_conv = conv_weight.shape[1]
    own_weights = jnp.concatenate(
        [proj_in, proj_out.T, conv_weight.reshape(KERNEL_TAPS * part_conv, inner_half)], axis=0
    )
    own_vectors, own_weights = lax.optimization_barrier((own_vectors, own_weights))
    other_vectors, other_weights = swap(own_vectors), swap(own_weights)
    tokens_tied, other_vectors, other_weights = lax.optimization_barrier(
        (other_of(tokens), other_vectors, other_weights)
    )
    both = whole(own_weights, other_weights, 1)
    vectors = jnp.where(
        low_side, jnp.stack([own_vectors, other_vectors]), jnp.stack([other_vectors, own_vectors])
    )
    x_own = own_of(tokens)
    x_other = swap(tokens_tied)
    gy_own = own_of(cotangent)
    gy_tied, _ = lax.optimization_barrier((other_of(cotangent), x_other))
    gy_other = swap(gy_tied)

    gathered = lax.all_gather(both, "seq", axis=0)
    weight_in = gathered[:, :part_in].reshape(model, inner)
    weight_out = gathered[:, part_in : 2 * part_in].reshape(model, inner)
    weight_conv = (
        gathered[:, 2 * part_in :]
        .reshape(seq_count, KERNEL_TAPS, part_conv, inner)
        .transpose(1, 0, 2, 3)
        .reshape(KERNEL_TAPS, inner, inner)
    )
    wide = jnp.stack([vectors[:, i * half : (i + 1) * half].reshape(-1) for i in range(3)])
    narrow = jnp.stack(
        [
            vectors[:, 3 * half + i * inner_half : 3 * half + (i + 1) * inner_half].reshape(-1)
            for i in range(6)
        ]
    )

    places = lax.axis_index("seq") * rows + jnp.arange(rows + 2 * HALO, dtype=jnp.int32) - HALO
    inside = (places >= 0) & (places < rows * seq_count)
    bounds = jnp.cumsum(own_of(seq_lengths))[:-1]
    segment = jnp.sum((places[:, None] >= bounds[None, :]).astype(jnp.int32), axis=1)
    segment = jnp.where(inside, segment, -1)
    middle = segment[HALO : HALO + rows]
    tap_list = [
        (segment[tap * DILATION_STEP : tap * DILATION_STEP + rows] == middle).astype(jnp.bfloat16)
        for tap in range(KERNEL_TAPS)
    ]
    taps = jnp.stack(tap_list, axis=1)
    keep = own_of(residue_mask).astype(jnp.float32)[:, None]
    f32, bf16 = jnp.float32, jnp.bfloat16
    product = 2 * rows * model * inner

    a1, s1, h1, a2, s2 = row_call(
        first_kernel,
        side_array,
        rows,
        count,
        [(x_own, "rows"), (x_other, "rows"), (keep, "rows"), (weight_in, "once"), (wide, "once"), (narrow, "once")],
        [(model, bf16, "rows"), (model, f32, "rows"), (inner, f32, "rows"), (inner, bf16, "rows"), (inner, f32, "rows")],
        product,
    )
    a2 = framed(a2, HALO)
    h3, a3, s3, out_own, out_other = row_call(
        second_kernel,
        side_array,
        rows,
        count,
        [
            (x_own, "rows"),
            (x_other, "rows"),
            (taps, "rows"),
            (a2, "once"),
            (weight_conv.reshape(KERNEL_TAPS * inner, inner), "once"),
            (weight_out, "once"),
            (wide, "once"),
            (narrow, "once"),
        ],
        [(inner, f32, "rows"), (inner, bf16, "rows"), (inner, f32, "rows"), (half, bf16, "rows"), (half, bf16, "rows")],
        4 * product,
    )
    out_back = swap(out_other)

    dh3, gy, wide_sum_3, sum_3 = row_call(
        third_kernel,
        side_array,
        rows,
        count,
        [(gy_own, "rows"), (gy_other, "rows"), (h3, "rows"), (s3, "rows"), (weight_out, "once"), (narrow, "once")],
        [(inner, bf16, "rows"), (model, bf16, "rows"), (model, f32, "sum"), (inner, f32, "sum")],
        product,
    )
    dh3_framed = framed(dh3, HALO)
    grad_out = matrix_grad(gy, a3, 2)
    grad_conv = conv_grad(a2, jnp.stack(tap_list, axis=0)[:, :, None], dh3)
    dh3_framed, out_back = lax.optimization_barrier((dh3_framed, out_back))
    flipped = jnp.flip(weight_conv, 0).transpose(0, 2, 1).reshape(KERNEL_TAPS * inner, inner)
    dh1, dx_own, dx_other, wide_sum_1, sum_1 = row_call(
        fourth_kernel,
        side_array,
        rows,
        count,
        [
            (x_own, "rows"),
            (x_other, "rows"),
            (gy_own, "rows"),
            (taps, "rows"),
            (dh3_framed, "once"),
            (flipped, "once"),
            (h1, "rows"),
            (s2, "rows"),
            (s1, "rows"),
            (weight_in, "once"),
            (wide, "once"),
            (narrow, "once"),
        ],
        [(inner, bf16, "rows"), (half, f32, "rows"), (half, bf16, "rows"), (model, f32, "sum"), (inner, f32, "sum")],
        4 * product,
    )
    dx_back = swap(dx_other)
    grad_in = matrix_grad(a1, dh1, 2)

    def placed(own, back):
        return jnp.where(low_side, jnp.stack([own, back], 0), jnp.stack([back, own], 0))

    block_out = placed(out_own, out_back)
    grad_tokens = placed(
        dx_own, dx_back.astype(f32) + other_of(cotangent).astype(f32)
    )

    bits = list(range(seq_count.bit_length() - 1))
    swapped_bits = [bits[0]] + bits[2:] + [bits[1]]
    part = jnp.concatenate(
        [
            scattered(grad_in.reshape(seq_count, part_in, inner), bits),
            scattered(grad_out.reshape(seq_count, part_in, inner), swapped_bits),
            scattered(
                grad_conv.reshape(KERNEL_TAPS, seq_count, part_conv, inner).transpose(1, 0, 2, 3), bits
            ).reshape(KERNEL_TAPS * part_conv, inner),
        ],
        axis=0,
    )
    left, right = part[:, :inner_half], part[:, inner_half:]
    part_other = swap(jnp.where(low_side, right, left).astype(bf16))
    part = jnp.where(low_side, left, right) + part_other.astype(f32)

    smalls = jnp.concatenate(
        [
            small.reshape(2, -1)
            for small in (wide_sum_1[0], wide_sum_1[1], wide_sum_3[0], sum_1[0], sum_1[1], sum_1[2], sum_3[0], sum_3[1], sum_3[2])
        ],
        axis=1,
    )
    totals = smalls
    for bit in bits:
        totals = totals + lax.ppermute(totals, "seq", [(i, i ^ (1 << bit)) for i in range(seq_count)])
    totals = own_of(totals) + swap(other_of(totals))
    sizes = [half] * 3 + [inner_half] * 6
    parts = []
    at = 0
    for size in sizes:
        parts.append(totals[at : at + size])
        at += size
    return (
        block_out,
        grad_tokens,
        parts[0],
        parts[1],
        part[:part_in],
        parts[3],
        parts[4],
        parts[5],
        part[2 * part_in :].reshape(KERNEL_TAPS, part_conv, inner_half),
        parts[6],
        parts[7],
        parts[8],
        part[part_in : 2 * part_in].T,
        parts[2],
    )


BLOCK = 256
CHUNKS = 4
CONV_PAD = 8
HEAD = 5
LEAD = 128


def fast_kernel(
    tokens, cot, lengths, residues, proj_in, proj_out, conv_own, *rest,
) -> None:
    vectors, refs = rest[:9], rest[9:]
    fast_steps(tokens, cot, lengths, residues, proj_in, proj_out, conv_own, vectors, *refs)


def fast_steps(
    tokens, cot, lengths, residues, proj_in, proj_out, conv_own, vectors,
    out_own, out_back, dx_own, dx_back, dx_tail, dx_end, grads_out, sums_out,
    x_other, g_conv, s1, h1, s2, h3, s3,
    masks, own_vectors, other_vectors, wide, narrow, stage,
    a1v, a2f, a3v, gyv, dh3f, out_send, w_in, w_out, w_conv,
    k_in, s_in, r0_in, r1_in, r2_in, r3_in,
    k_out, s_out, r0_out, r1_out, r2_out, r3_out,
    k_low, s_low, r0_low, r1_low, r2_low, r3_low,
    k_mid, s_mid, r0_mid, r1_mid, r2_mid, r3_mid,
    k_top, s_top, r0_top, r1_top, r2_top, r3_top,
    smalls, cross_send, cross_recv, small_send, small_recv, load_sems,
    swap_sems, token_sems, in_gather, out_gather, conv_gather, gy_sems, out_sems, dx_sems, a2_sems, dh3_sems, in_sems, out_rs_sems, low_sems, mid_sems, top_sems, cross_sems, small_sems,
):
    rows = a1v.shape[0]
    half = tokens.shape[2]
    inner = narrow.shape[1]
    part = rows // CHUNKS
    side = lax.axis_index("ch")
    place = lax.axis_index("seq")
    last = lax.axis_size("seq") - 1
    low = side == 0
    bits = [lax.rem(place // (1 << bit), 2) for bit in range(4)]
    across = {"ch": 1 - side}
    pairs = [{"seq": place + (1 << bit) * (1 - 2 * bits[bit])} for bit in range(4)]
    before, after = {"seq": place - 1}, {"seq": place + 1}

    def remote(src, dst, sems, at, device):
        return pltpu.make_async_remote_copy(
            src_ref=src,
            dst_ref=dst,
            send_sem=sems.at[0, at],
            recv_sem=sems.at[1, at],
            device_id=device,
            device_id_type=pl.DeviceIdType.MESH,
        )

    def block(ref, at):
        return ref.at[pl.ds(pl.multiple_of(at * BLOCK, BLOCK), BLOCK)]


    def gy_copy(at):
        piece = pl.ds(at * part, part)
        return remote(cot.at[1 - side, piece], gyv.at[side, piece], gy_sems, at, across)

    token_part = (rows - LEAD) // CHUNKS

    def token_copy(at):
        piece = pl.ds(pl.multiple_of(LEAD + at * token_part, 16), token_part)
        return remote(tokens.at[1 - side, piece], x_other.at[piece], token_sems, at, across)

    lead = pl.ds(0, LEAD)
    lead_copy = remote(tokens.at[1 - side, lead], x_other.at[lead], token_sems, CHUNKS, across)

    tail_rows = k_top.shape[1]
    own_gy = pltpu.make_async_copy(cot.at[side], gyv.at[side], load_sems.at[0])
    def out_copy(at):
        return remote(block(out_send, at), block(out_back, at), out_sems, at, across)

    def dx_copy(at):
        return remote(block(gyv.at[1 - side], at), block(dx_back, at), dx_sems, at, across)

    def halo_low(framed_rows, sems):
        return remote(framed_rows.at[pl.ds(HALO, HALO)], framed_rows.at[pl.ds(HALO + rows, HALO)], sems, 0, before)

    def halo_high(framed_rows, sems):
        return remote(framed_rows.at[pl.ds(rows, HALO)], framed_rows.at[pl.ds(0, HALO)], sems, 1, after)

    def halo_start(framed_rows, sems):
        @pl.when(place > 0)
        def _():
            halo_low(framed_rows, sems).start()

        @pl.when(place < last)
        def _():
            halo_high(framed_rows, sems).start()

    def halo_wait(framed_rows, sems):
        @pl.when(place > 0)
        def _():
            halo_low(framed_rows, sems).wait_send()
            halo_high(framed_rows, sems).wait_recv()

        @pl.when(place < last)
        def _():
            halo_high(framed_rows, sems).wait_send()
            halo_low(framed_rows, sems).wait_recv()

    blocks = rows // BLOCK
    per = part // BLOCK

    def middle_first(step):
        late = step // (blocks - 2)
        return (step + 1) * (1 - late) + late * (step - (blocks - 2)) * (blocks - 1)

    def in_order(step):
        return step

    def pipeline(step, order, ins, outs, tail=None, count=None):
        def spec(ref):
            return pl.BlockSpec((BLOCK, ref.shape[-1]), lambda i: (order(i), 0))

        out_specs = [spec(r) for r in outs]
        if tail is not None:
            ahead, end = tail
            most = blocks - 2 - HEAD
            outs = outs + [ahead, end]
            out_specs.append(
                pl.BlockSpec((BLOCK, half), lambda i: (jnp.minimum(jnp.maximum(i - HEAD, 0), most), 0))
            )
            out_specs.append(pl.BlockSpec((BLOCK, half), lambda i: (0, 0)))
        pltpu.emit_pipeline(step, grid=(count or blocks,), in_specs=[spec(r) for r in ins], out_specs=out_specs)(*ins, *outs)

    barrier = pltpu.get_barrier_semaphore()
    ring = [{"seq": lax.rem(place + last, last + 1)}, {"seq": lax.rem(place + 1, last + 1)}]
    for device in [across] + pairs + ring:
        pl.semaphore_signal(barrier, inc=1, device_id=device, device_id_type=pl.DeviceIdType.MESH)
    pl.semaphore_wait(barrier, 7)

    lead_copy.start()
    height = inner // 16
    part_in = proj_in.shape[0]
    quarter = half // 2
    wanted = quarter + 64
    cross_send[0:part_in, 0:quarter] = proj_in[...]
    cross_send[part_in : 2 * part_in, 0:quarter] = proj_out[...]
    cross_send[2 * part_in :, 0:quarter] = jnp.concatenate(
        [conv_own[tap].astype(jnp.float32) for tap in range(KERNEL_TAPS)]
        + [jnp.zeros((CONV_PAD, quarter), jnp.float32)],
        axis=0,
    ).astype(jnp.bfloat16)
    cross_send[:, quarter:] = jnp.zeros((cross_send.shape[0], wanted - quarter), jnp.bfloat16)
    own_vectors[...] = jnp.zeros_like(own_vectors)
    at = 0
    for vector in vectors:
        width = vector.shape[0]
        own_vectors[:, at : at + width] = vector[...].reshape(1, width)
        at += width + width % 128
    swaps = [
        remote(cross_send, cross_recv, swap_sems, 0, across),
        remote(own_vectors, other_vectors, swap_sems, 1, across),
    ]
    for swap in swaps:
        swap.start()
    for at in range(CHUNKS):
        token_copy(at).start()
    for at in range(CHUNKS):
        gy_copy(at).start()
    own_gy.start()

    ends = jnp.where(low, lengths[0:1, :], lengths[1:2, :]).astype(jnp.float32)
    count = ends.shape[1]
    upper = lax.broadcasted_iota(jnp.int32, (count, count), 0) <= lax.broadcasted_iota(jnp.int32, (count, count), 1)
    ends = lax.dot_general(
        jnp.broadcast_to(ends, (8, count)),
        upper.astype(jnp.float32),
        (((1,), (0,)), ((), ())),
        precision=lax.Precision.HIGHEST,
        preferred_element_type=jnp.float32,
    )[0:1, :]

    def mask_block(at, _):
        base = pl.multiple_of(at * BLOCK, BLOCK)
        span = BLOCK + 2 * HALO
        spot = lax.broadcasted_iota(jnp.int32, (span, count), 0) + (place * rows + base - HALO)
        inside = (spot >= 0) & (spot < rows * (last + 1))
        reached = jnp.where(ends <= spot.astype(jnp.float32), 1.0, 0.0)
        segment = jnp.sum(jnp.where(inside, reached, -1.0 / count), axis=1, keepdims=True)
        own_segment = segment[HALO : HALO + BLOCK]
        lane = lax.broadcasted_iota(jnp.int32, (BLOCK, 8), 1)
        columns = jnp.zeros((BLOCK, 8), jnp.float32)
        for tap in range(KERNEL_TAPS):
            same = segment[tap * DILATION_STEP : tap * DILATION_STEP + BLOCK] == own_segment
            columns = jnp.where((lane == tap) & same, 1.0, columns)
        kept = residues[:, pl.ds(base, BLOCK)]
        kept = jnp.where(low, kept[0:1, :], kept[1:2, :]).astype(jnp.float32)
        square = (BLOCK, BLOCK)
        diagonal = lax.broadcasted_iota(jnp.int32, square, 0) == lax.broadcasted_iota(jnp.int32, square, 1)
        keep = jnp.sum(jnp.where(diagonal, kept, 0.0), axis=1, keepdims=True)
        columns = jnp.where(lane == KERNEL_TAPS, keep, columns)
        masks[pl.ds(base, BLOCK), :] = columns.astype(jnp.bfloat16)
        return 0

    lax.fori_loop(0, rows // BLOCK, mask_block, 0)
    smalls[...] = jnp.zeros_like(smalls)

    @pl.when(place == 0)
    def _():
        a2f[0:HALO, :] = jnp.zeros((HALO, inner), jnp.bfloat16)
        dh3f[0:HALO, :] = jnp.zeros((HALO, inner), jnp.bfloat16)

    @pl.when(place == last)
    def _():
        a2f[HALO + rows :, :] = jnp.zeros((HALO, inner), jnp.bfloat16)
        dh3f[HALO + rows :, :] = jnp.zeros((HALO, inner), jnp.bfloat16)

    def both(own, other):
        left, right = ordered(side, own, other)
        return jnp.concatenate([left, right], axis=1)

    for swap in swaps:
        swap.wait()
    rows_here = both(cross_send[:, 0:quarter], cross_recv[:, 0:quarter]).astype(jnp.bfloat16)
    here = (bits[3], bits[2], bits[1], bits[0])
    w_in[here] = rows_here[:part_in]
    w_out[here] = rows_here[part_in : 2 * part_in]
    stage[0, 0] = rows_here[2 * part_in :]
    own_conv = pltpu.make_async_copy(stage.at[0, 0], g_conv.at[here], load_sems.at[1])
    own_conv.start()
    for index in range(3):
        lanes = slice(index * half, (index + 1) * half)
        wide[index : index + 1, :] = both(own_vectors[:, lanes], other_vectors[:, lanes])
    for index in range(6):
        lanes = slice(3 * half + index * wanted, 3 * half + index * wanted + quarter)
        narrow[index : index + 1, :] = both(own_vectors[:, lanes], other_vectors[:, lanes])

    def gather_copy(group, level):
        ref, sems, order = group
        every = slice(None)
        at = tuple(every if bit in order[:level] else bits[bit] for bit in (3, 2, 1, 0))
        return remote(ref.at[at], ref.at[at], sems, level, pairs[order[level]])

    in_rows = (w_in, in_gather, (3, 2, 1, 0))
    out_rows = (w_out, out_gather, (1, 3, 2, 0))
    conv_rows = (g_conv, conv_gather, (3, 2, 1, 0))

    def gather_next(group, level):
        gather_copy(group, level).wait()
        if level < 3:
            gather_copy(group, level + 1).start()

    gather_copy(in_rows, 0).start()
    gather_copy(out_rows, 0).start()
    own_conv.wait()
    gather_next(in_rows, 0)
    gather_copy(conv_rows, 0).start()
    gather_next(in_rows, 1)
    gather_next(in_rows, 2)
    gather_next(conv_rows, 0)
    gather_next(out_rows, 0)
    gather_next(in_rows, 3)

    def first_chunk(at, _):
        token_copy(at).wait_recv()

        def first(own, other, s1_block, h1_block, s2_block):
            base = pl.multiple_of((at * per + pl.program_id(0)) * BLOCK, BLOCK)
            x = jnp.concatenate(ordered(side, own[...], other[...]), axis=1)
            normed, _ = norm(x)
            act, slope = gelu_both(normed * wide[0:1, :] + wide[1:2, :])
            act = act.astype(jnp.bfloat16)
            a1v[pl.ds(base, BLOCK), :] = act
            s1_block[...] = slope
            value = dot(act, w_in[...].reshape(2 * half, inner)) + narrow[0:1, :]
            h1_block[...] = value
            normed, _ = norm(value)
            act, slope = gelu_both(normed * narrow[1:2, :] + narrow[2:3, :])
            keep = masks[pl.ds(base, BLOCK), KERNEL_TAPS : KERNEL_TAPS + 1].astype(jnp.float32)
            a2f[pl.ds(HALO + base, BLOCK), :] = (act * keep).astype(jnp.bfloat16)
            s2_block[...] = slope * keep

        pipeline(first, lambda i: at * per + i, [tokens.at[side], x_other], [s1, h1, s2], count=per)
        for level, (group, ready) in enumerate(((conv_rows, 1), (out_rows, 1), (out_rows, 2))):

            @pl.when(at == level)
            def _():
                gather_next(group, ready)

        return 0

    lead_copy.wait_recv()
    lax.fori_loop(0, CHUNKS, first_chunk, 0)
    halo_start(a2f, a2_sems)
    gather_next(conv_rows, 2)
    gather_next(out_rows, 3)
    gather_next(conv_rows, 3)

    def conv_load(pair):
        return pltpu.make_async_copy(g_conv.at[pair // 2, pair % 2], stage, load_sems.at[2])

    def relay(pair, _):
        conv_load(pair).start()
        conv_load(pair).wait()
        for low_bit in range(2):
            even = stage[low_bit, 0].astype(jnp.float32)
            odd = stage[low_bit, 1].astype(jnp.float32)
            at = pl.multiple_of((2 * pair + low_bit) * 2 * height, 2 * height)
            for tap in range(KERNEL_TAPS):
                top = tap * height
                w_conv[tap, pl.ds(at, 2 * height), :] = jnp.concatenate(
                    [even[top : top + height], odd[top : top + height]], axis=0
                ).astype(jnp.bfloat16)

        return 0

    lax.fori_loop(0, 4, relay, 0)

    def second(own, other, h3_block, s3_block, own_block):
        step = pl.program_id(0)
        at = middle_first(step)
        base = pl.multiple_of(at * BLOCK, BLOCK)

        @pl.when(step == blocks - 2)
        def _():
            halo_wait(a2f, a2_sems)

        taps = masks[pl.ds(base, BLOCK), :]
        weight = w_conv[...].reshape(KERNEL_TAPS * inner, inner)
        value = dot(windowed(a2f, taps, base, BLOCK), weight) + narrow[3:4, :]
        h3_block[...] = value
        normed, _ = norm(value)
        act, slope = gelu_both(normed * narrow[4:5, :] + narrow[5:6, :])
        act = act.astype(jnp.bfloat16)
        a3v[pl.ds(base, BLOCK), :] = act
        s3_block[...] = slope
        mixed = dot(act, w_out[...].reshape(2 * half, inner), ((1,), (1,))) + wide[2:3, :]
        left, right = mixed[:, :half], mixed[:, half:]
        own_block[...] = (own[...].astype(jnp.float32) + jnp.where(low, left, right)).astype(jnp.bfloat16)
        out_send[pl.ds(base, BLOCK), :] = (
            other[...].astype(jnp.float32) + jnp.where(low, right, left)
        ).astype(jnp.bfloat16)
        out_copy(at).start()

    pipeline(second, middle_first, [tokens.at[side], x_other], [h3, s3, out_own])

    def add_small(row, value):
        smalls[row : row + 1, :] += value

    def add_wide(row, value):
        smalls[row : row + 1, :] += value[:, :half]
        smalls[row + 1 : row + 2, :] += value[:, half:]

    def third(h3_block, s3_block):
        at = pl.program_id(0)
        base = pl.multiple_of(at * BLOCK, BLOCK)
        for later in range(CHUNKS):

            @pl.when(at == later * per)
            def _():
                gy_copy(later).wait_recv()

        gy = jnp.concatenate([gyv[0, pl.ds(base, BLOCK), :], gyv[1, pl.ds(base, BLOCK), :]], axis=1)
        add_wide(4, column_sums(gy.astype(jnp.float32)))
        dz3 = dot(gy, w_out[...].reshape(2 * half, inner)) * s3_block[...]
        normed, scale = norm(h3_block[...])
        dh3 = norm_back(dz3, normed, scale, narrow[4:5, :]).astype(jnp.bfloat16)
        dh3f[pl.ds(HALO + base, BLOCK), :] = dh3
        add_small(9, column_sums(dh3.astype(jnp.float32)))
        add_small(10, column_sums(dz3 * normed))
        add_small(11, column_sums(dz3))

    own_gy.wait()
    pipeline(third, in_order, [h3, s3], [])
    halo_start(dh3f, dh3_sems)

    def slot(pair, order):
        two = (pair % 4) if order[0] == 1 else (pair % 4) // 2 + 2 * (pair % 2)
        return pair // 4 * 4 + two

    def split(group, at, even, odd):
        keep_ref, send_ref = group[0], group[1]
        mine_first = bits[0] == 0
        keep_ref[at] = jnp.where(mine_first, even, odd)
        send_ref[at] = jnp.where(mine_first, odd, even).astype(jnp.bfloat16)

    def wide_grad(left_of, right_ref, group):
        tall_rows = group[0].shape[1]

        def tile(at, _):
            value = dot(left_of(at), right_ref[...], ((0,), (0,)))
            for pair in range(4):
                top = 2 * pair * tall_rows
                split(
                    group,
                    at * 4 + slot(pair, group[4]),
                    value[top : top + tall_rows],
                    value[top + tall_rows : top + 2 * tall_rows],
                )
            return 0

        lax.fori_loop(0, 2, tile, 0)
        sum_copy(group, 0).start()

    def conv_grad_of(taps, group):
        right = dh3f.at[pl.ds(HALO, rows)]
        values = []
        for tap in taps:
            left = a2f[tap * DILATION_STEP : tap * DILATION_STEP + rows, :] * masks[:, tap : tap + 1]
            values.append(dot(left, right[...], ((0,), (0,))))
        if len(values) == 1:
            tail = [jnp.zeros((CONV_PAD, inner), jnp.float32)]
        else:
            tail = []
        for pair in range(8):
            top = 2 * pair * height
            split(
                group,
                slot(pair, group[4]),
                jnp.concatenate([v[top : top + height] for v in values] + tail, axis=0),
                jnp.concatenate([v[top + height : top + 2 * height] for v in values] + tail, axis=0),
            )
        sum_copy(group, 0).start()

    y_first, z_first = (1, 2, 3), (2, 1, 3)
    in_set = (k_in, s_in, (r0_in, r1_in, r2_in, r3_in), in_sems, y_first)
    out_set = (k_out, s_out, (r0_out, r1_out, r2_out, r3_out), out_rs_sems, z_first)
    low_set = (k_low, s_low, (r0_low, r1_low, r2_low, r3_low), low_sems, y_first)
    mid_set = (k_mid, s_mid, (r0_mid, r1_mid, r2_mid, r3_mid), mid_sems, z_first)
    top_set = (k_top, s_top, (r0_top, r1_top, r2_top, r3_top), top_sems, y_first)
    starts = (0, 0, 4, 6)
    lengths = (8, 4, 2, 1)

    def sum_copy(group, level):
        _, send, received, sems, order = group
        bit = 0 if level == 0 else order[level - 1]
        return remote(
            send.at[pl.ds(starts[level], lengths[level])], received[level], sems, level, pairs[bit]
        )

    def sum_step(group, level):
        keep, send, received, _, order = group
        sum_copy(group, level).wait()
        came = received[level]
        fixed = 0
        for at in range(level):
            fixed = fixed + bits[order[at]] * (1 << at)
        if level == 3:
            keep[fixed] = keep[fixed] + came[0].astype(jnp.float32)
            return
        mine = bits[order[level]]

        def one(item, _):
            other = 2 * item + 1 - mine
            same = 2 * item + mine
            send[starts[level + 1] + item] = (
                keep[other * (1 << level) + fixed] + came[other].astype(jnp.float32)
            ).astype(jnp.bfloat16)
            at = same * (1 << level) + fixed
            keep[at] = keep[at] + came[same].astype(jnp.float32)
            return 0

        lax.fori_loop(0, lengths[level + 1], one, 0)
        sum_copy(group, level + 1).start()

    def at_step(step, when, *steps):
        @pl.when(step == when)
        def _():
            for group, level in steps:
                sum_step(group, level)

    conv_grad_of((0, 1), low_set)
    conv_grad_of((2, 3), mid_set)
    conv_grad_of((4,), top_set)
    wide_grad(lambda at: gyv[at], a3v, out_set)

    def fourth(h1_block, s2_block):
        step = pl.program_id(0)
        base = pl.multiple_of(step * BLOCK, BLOCK)
        taps = masks[pl.ds(base, BLOCK), :]
        da2 = jnp.zeros((BLOCK, inner), jnp.float32)
        for tap in range(KERNEL_TAPS):
            window = dh3f[pl.ds(base + tap * DILATION_STEP, BLOCK), :] * taps[:, tap : tap + 1]
            da2 = da2 + dot(window, w_conv[KERNEL_TAPS - 1 - tap], ((1,), (1,)))
        dz2 = da2 * s2_block[...]
        normed, scale = norm(h1_block[...])
        dh1 = norm_back(dz2, normed, scale, narrow[1:2, :]).astype(jnp.bfloat16)
        a3v[pl.ds(base, BLOCK), :] = dh1
        add_small(6, column_sums(dh1.astype(jnp.float32)))
        add_small(7, column_sums(dz2 * normed))
        add_small(8, column_sums(dz2))
        at_step(step, 0, (low_set, 0), (mid_set, 0), (top_set, 0))
        at_step(step, 1, (out_set, 0))
        at_step(step, 5, (low_set, 1))
        at_step(step, 6, (mid_set, 1))
        at_step(step, 7, (top_set, 1))

    halo_wait(dh3f, dh3_sems)
    pipeline(fourth, in_order, [h1, s2], [])
    wide_grad(lambda at: a1v[:, pl.ds(pl.multiple_of(at * half, 128), half)], a3v, in_set)
    sum_step(out_set, 1)
    sum_step(low_set, 2)

    def fifth(own, other, s1_block, own_block, tail_block, end_block):
        step = pl.program_id(0)
        base = pl.multiple_of(step * BLOCK, BLOCK)
        dh1 = a3v[pl.ds(base, BLOCK), :]
        dz1 = dot(dh1, w_in[...].reshape(2 * half, inner), ((1,), (1,))) * s1_block[...]
        x = jnp.concatenate(ordered(side, own[...], other[...]), axis=1)
        normed, scale = norm(x)
        dx = norm_back(dz1, normed, scale, wide[0:1, :])
        add_wide(0, column_sums(dz1 * normed))
        add_wide(2, column_sums(dz1))
        left, right = dx[:, :half], dx[:, half:]
        own_block[...] = jnp.where(low, left, right) + gyv[side, pl.ds(base, BLOCK), :].astype(jnp.float32)
        sent = jnp.where(low, right, left).astype(jnp.bfloat16)
        gyv[1 - side, pl.ds(base, BLOCK), :] = sent
        end_block[...] = sent

        @pl.when(step < blocks - 1)
        def _():
            tail_block[...] = sent

        @pl.when(step < HEAD - 1)
        def _():
            dx_copy(step).start()

        at_step(step, 0, (mid_set, 2), (in_set, 0))
        at_step(step, 2, (out_set, 2), (top_set, 2))
        at_step(step, 4, (low_set, 3))
        at_step(step, 5, (mid_set, 3))
        at_step(step, 6, (in_set, 1))
        at_step(step, 7, (top_set, 3), (out_set, 3))

    pipeline(fifth, in_order, [tokens.at[side], x_other, s1], [dx_own], (dx_tail, dx_end))


    def small_copy(level):
        device = pairs[level] if level < 4 else across
        return remote(small_send.at[level], small_recv.at[level], small_sems, level, device)

    def small_start(level):
        small_send[level] = smalls[...]
        small_copy(level).start()

    def small_step(level):
        small_copy(level).wait()
        smalls[...] += small_recv[level]

    small_start(0)
    sum_step(in_set, 2)
    small_step(0)
    small_start(1)
    small_step(1)
    small_start(2)
    small_step(2)
    small_start(3)
    sum_step(in_set, 3)
    small_step(3)
    small_start(4)

    row = 0
    for keep, _, _, _, order in (in_set, out_set, low_set, mid_set, top_set):
        mine = bits[order[0]] + 2 * bits[order[1]] + 4 * bits[order[2]]
        height = keep.shape[1]
        value = keep[mine]
        left, right = value[:, :wanted], value[:, inner - wanted :]
        cross_send[row : row + height, :] = jnp.where(low, right, left).astype(jnp.bfloat16)
        row += height
    for at in range(blocks):
        out_copy(at).wait()
    cross = remote(cross_send, cross_recv, cross_sems, 0, across)
    cross.start()
    dx_copy(HEAD - 1).start()
    lead_copy.wait_send()
    for at in range(CHUNKS):
        token_copy(at).wait_send()
        gy_copy(at).wait_send()
    small_step(4)
    for index in range(3):
        both = smalls[2 * index : 2 * index + 2, :]
        sums_out[:, index * half : (index + 1) * half] = jnp.where(low, both[0:1], both[1:2])
    for index in range(6):
        both = smalls[6 + index : 7 + index, :]
        at = 3 * half + index * wanted
        sums_out[:, at : at + quarter] = jnp.where(low, both[:, :quarter], both[:, quarter:])
    cross.wait()
    row = 0
    for keep, _, _, _, order in (in_set, out_set, low_set, mid_set, top_set):
        height = keep.shape[1]
        value = keep[bits[order[0]] + 2 * bits[order[1]] + 4 * bits[order[2]]]
        came = cross_recv[row : row + height, :].astype(jnp.float32)
        grads_out[row : row + height, :] = jnp.where(
            low, value[:, :quarter] + came[:, :quarter], value[:, quarter:] + came[:, wanted - quarter :]
        )
        row += height
    for at in range(HEAD):
        dx_copy(at).wait()


def fast_call(tokens, cot, lengths, residues, proj_in, proj_out, conv_own, vectors):
    _, rows, half = tokens.shape
    model = 2 * half
    inner = 2 * proj_in.shape[1]
    part_in = proj_in.shape[0]
    part_conv = conv_own.shape[1]
    f32, bf16 = jnp.float32, jnp.bfloat16
    tall = KERNEL_TAPS * part_conv + CONV_PAD
    any_spec = pl.BlockSpec(memory_space=pl.ANY)
    vmem_spec = pl.BlockSpec(memory_space=pltpu.VMEM)
    total = 2 * part_in + tall
    wanted = half // 2 + 64

    def sums(height):
        return [pltpu.VMEM((8, height, inner), f32), pltpu.VMEM((8, height, inner), bf16)] + [
            pltpu.VMEM((length, height, inner), bf16) for length in (8, 4, 2, 1)
        ]

    def sems(count):
        return pltpu.SemaphoreType.DMA((2, count))

    shapes = [
        ((rows, half), bf16),
        ((rows, half), bf16),
        ((rows, half), f32),
        ((rows, half), bf16),
        ((rows - (HEAD + 1) * BLOCK, half), bf16),
        ((BLOCK, half), bf16),
        ((total, half // 2), f32),
        ((1, 3 * half + 6 * wanted), f32),
        ((rows, half), bf16),
        ((2, 2, 2, 2, tall, inner), bf16),
        ((rows, model), f32),
        ((rows, inner), f32),
        ((rows, inner), f32),
        ((rows, inner), f32),
        ((rows, inner), f32),
    ]
    flops = 6 * rows * (2 * model * inner + KERNEL_TAPS * inner * inner)
    results = pl.pallas_call(
        fast_kernel,
        out_shape=[jax.ShapeDtypeStruct(shape, dtype) for shape, dtype in shapes],
        in_specs=[any_spec] * 2 + [vmem_spec] * 14,
        out_specs=[any_spec] * 6 + [vmem_spec] * 2 + [any_spec] * 7,
        scratch_shapes=[
            pltpu.VMEM((rows, 8), bf16),
            pltpu.VMEM((1, 3 * half + 6 * wanted), f32),
            pltpu.VMEM((1, 3 * half + 6 * wanted), f32),
            pltpu.VMEM((8, model), f32),
            pltpu.VMEM((8, inner), f32),
            pltpu.VMEM((2, 2, tall, inner), bf16),
            pltpu.VMEM((rows, model), bf16),
            pltpu.VMEM((rows + 2 * HALO, inner), bf16),
            pltpu.VMEM((rows, inner), bf16),
            pltpu.VMEM((2, rows, half), bf16),
            pltpu.VMEM((rows + 2 * HALO, inner), bf16),
            pltpu.VMEM((rows, half), bf16),
            pltpu.VMEM((2, 2, 2, 2, part_in, inner), bf16),
            pltpu.VMEM((2, 2, 2, 2, part_in, inner), bf16),
            pltpu.VMEM((KERNEL_TAPS, inner, inner), bf16),
        ]
        + sums(part_in) * 4
        + sums(tall - 2 * part_in)
        + [
            pltpu.VMEM((16, inner), f32),
            pltpu.VMEM((total, wanted), bf16),
            pltpu.VMEM((total, wanted), bf16),
            pltpu.VMEM((5, 16, inner), f32),
            pltpu.VMEM((5, 16, inner), f32),
            pltpu.SemaphoreType.DMA((3,)),
            sems(2),
            sems(CHUNKS + 1),
            sems(4),
            sems(4),
            sems(4),
            sems(CHUNKS),
            sems(rows // BLOCK),
            sems(HEAD),
            sems(2),
            sems(2),
            sems(4),
            sems(4),
            sems(4),
            sems(4),
            sems(4),
            sems(1),
            sems(5),
        ],
        compiler_params=pltpu.CompilerParams(
            collective_id=0, has_side_effects=True, vmem_limit_bytes=65280 * 2**10
        ),
        cost_estimate=pl.CostEstimate(flops=flops, bytes_accessed=120 * 2**20, transcendentals=0),
    )(tokens, cot, lengths, residues, proj_in, proj_out, conv_own, *vectors)
    return results[:8]


def finish_kernel(side_ref, tail_ref, cot_ref, whole_ref, out_ref):
    at = pl.ds(pl.multiple_of(pl.program_id(0) * BLOCK, BLOCK), BLOCK)
    out_ref[0] = tail_ref[at, :].astype(jnp.float32) + cot_ref[0].astype(jnp.float32)


def assemble_kernel(side_ref, out_own, out_back, dx_own, dx_back, cot, block_out, grad_tokens):
    side = side_ref[0]
    block_out[side] = out_own[...]
    block_out[1 - side] = out_back[...]
    grad_tokens[side] = dx_own[...]
    grad_tokens[1 - side] = dx_back[...].astype(jnp.float32) + cot[0].astype(jnp.float32)


def assemble_call(side, out_own, out_back, dx_own, dx_back, cot):
    rows, half = out_own.shape
    tile = 2 * BLOCK
    by_tile = pl.BlockSpec((tile, half), lambda i, side_ref: (i, 0))
    pair = pl.BlockSpec((2, tile, half), lambda i, side_ref: (0, i, 0))
    return pl.pallas_call(
        assemble_kernel,
        grid_spec=pltpu.PrefetchScalarGridSpec(
            num_scalar_prefetch=1,
            grid=(rows // tile,),
            in_specs=[by_tile] * 4
            + [pl.BlockSpec((1, tile, half), lambda i, side_ref: (1 - side_ref[0], i, 0))],
            out_specs=[pair, pair],
        ),
        out_shape=[
            jax.ShapeDtypeStruct((2, rows, half), jnp.bfloat16),
            jax.ShapeDtypeStruct((2, rows, half), jnp.float32),
        ],
        compiler_params=pltpu.CompilerParams(
            dimension_semantics=("arbitrary",), vmem_limit_bytes=56 * 2**20
        ),
        cost_estimate=pl.CostEstimate(flops=rows * half, bytes_accessed=24 * rows * half, transcendentals=0),
    )(side, out_own, out_back, dx_own, dx_back, cot)


def finish_call(side, tail, cot, grad_tokens, first):
    half = tail.shape[1]

    def theirs(i, side_ref):
        return (1 - side_ref[0], first + i, 0)

    return pl.pallas_call(
        finish_kernel,
        grid_spec=pltpu.PrefetchScalarGridSpec(
            num_scalar_prefetch=1,
            grid=(tail.shape[0] // BLOCK,),
            in_specs=[
                pl.BlockSpec(memory_space=pltpu.VMEM),
                pl.BlockSpec((1, BLOCK, half), theirs),
                pl.BlockSpec(memory_space=pl.ANY),
            ],
            out_specs=pl.BlockSpec((1, BLOCK, half), theirs),
        ),
        out_shape=jax.ShapeDtypeStruct(grad_tokens.shape, grad_tokens.dtype),
        input_output_aliases={3: 0},
        compiler_params=pltpu.CompilerParams(
            dimension_semantics=("arbitrary",), vmem_limit_bytes=63 * 2**20
        ),
        cost_estimate=pl.CostEstimate(flops=tail.size, bytes_accessed=8 * tail.size, transcendentals=0),
    )(side, tail, cot, grad_tokens)


def fast_body(
    tokens,
    cotangent,
    seq_lengths,
    residue_mask,
    first_gain,
    first_shift,
    proj_in,
    in_bias,
    mid_gain,
    mid_shift,
    conv_weight,
    conv_bias,
    last_gain,
    last_shift,
    proj_out,
    out_bias,
):
    micro, rows, half = tokens.shape
    inner_half = in_bias.shape[0]
    side = lax.axis_index("ch")

    def swap(value):
        return lax.ppermute(value, "ch", SWAP)

    part_in = proj_in.shape[0]
    part_conv = conv_weight.shape[1]
    vectors = (
        first_gain, first_shift, out_bias, in_bias, mid_gain, mid_shift, conv_bias, last_gain, last_shift
    )
    out_own, out_back, dx_own, dx_back, dx_tail, dx_end, grads, sums = fast_call(
        tokens, cotangent, seq_lengths, residue_mask, proj_in, proj_out.T, conv_weight, vectors
    )
    conv_part = grads[2 * part_in : 2 * part_in + KERNEL_TAPS * part_conv]

    side_array = side.astype(jnp.int32).reshape(1)
    tail_back = swap(dx_tail)
    block_out, grad_tokens = assemble_call(side_array, out_own, out_back, dx_own, dx_back, cotangent)
    dx_end, grad_tokens = lax.optimization_barrier((dx_end, grad_tokens))
    end_back = swap(dx_end)
    grad_tokens = finish_call(side_array, tail_back, cotangent, grad_tokens, HEAD)
    grad_tokens = finish_call(side_array, end_back, cotangent, grad_tokens, rows // BLOCK - 1)
    wanted = inner_half + 64

    def narrow_part(index):
        at = 3 * half + index * wanted
        return sums[0, at : at + inner_half]

    return (
        block_out,
        grad_tokens,
        sums[0, :half],
        sums[0, half : 2 * half],
        grads[:part_in],
        narrow_part(0),
        narrow_part(1),
        narrow_part(2),
        conv_part.reshape(KERNEL_TAPS, part_conv, inner_half),
        narrow_part(3),
        narrow_part(4),
        narrow_part(5),
        grads[part_in : 2 * part_in].T,
        sums[0, 2 * half : 3 * half],
    )


def solution(mesh):
    placed = (
        P(None, "seq", "ch"),
        P(None, "seq", "ch"),
        P(),
        P(None, "seq"),
        P("ch"),
        P("ch"),
        P("seq", "ch"),
        P("ch"),
        P("ch"),
        P("ch"),
        P(None, "seq", "ch"),
        P("ch"),
        P("ch"),
        P("ch"),
        P("ch", "seq"),
        P("ch"),
    )
    run = fast_body if mesh.shape["seq"] == 16 else body
    return jax.shard_map(
        run,
        mesh=mesh,
        in_specs=placed,
        out_specs=(
            P(None, "seq", "ch"),
            P(None, "seq", "ch"),
            P("ch"),
            P("ch"),
            P("seq", "ch"),
            P("ch"),
            P("ch"),
            P("ch"),
            P(None, "seq", "ch"),
            P("ch"),
            P("ch"),
            P("ch"),
            P("ch", "seq"),
            P("ch"),
        ),
        check_vma=False,
    )
```

```python
import jax
import jax.numpy as jnp
from jax import lax
from jax.experimental import pallas as pl
from jax.experimental.pallas import tpu as pltpu
from jax.sharding import PartitionSpec as P

KERNEL_TAPS = 5
DILATION_STEP = 32
HALO = 64

EPSILON = 1e-05
ROOT_HALF = 0.7071067811865476
ROOT_TAU = 0.3989422804014327
SWAP = [(0, 1), (1, 0)]


def gelu_both(value):
    half = 0.5 * (1.0 + lax.erf(value * ROOT_HALF))
    return value * half, half + value * jnp.exp(-0.5 * value * value) * ROOT_TAU


def norm(value):
    middle = jnp.mean(value, axis=1, keepdims=True)
    centred = value - middle
    scale = lax.rsqrt(jnp.mean(centred * centred, axis=1, keepdims=True) + EPSILON)
    return centred * scale, scale


def norm_back(grad_zed, normed, scale, gain):
    grad_normed = grad_zed * gain
    first = jnp.mean(grad_normed, axis=1, keepdims=True)
    second = jnp.mean(grad_normed * normed, axis=1, keepdims=True)
    return scale * (grad_normed - first - normed * second)


def dot(left, right, over=((1,), (0,))):
    return lax.dot_general(left, right, (over, ((), ())), preferred_element_type=jnp.float32)


def column_sums(value):
    return jnp.sum(value, axis=0, keepdims=True)


def ordered(side, own, other):
    low = side == 0
    own, other = own.astype(jnp.float32), other.astype(jnp.float32)
    return jnp.where(low, own, other), jnp.where(low, other, own)


def windowed(framed_ref, taps, base, count):
    return jnp.concatenate(
        [
            framed_ref[pl.ds(base + tap * DILATION_STEP, count), :] * taps[:, tap : tap + 1]
            for tap in range(KERNEL_TAPS)
        ],
        axis=1,
    )


def first_kernel(side_ref, own_ref, other_ref, keep_ref, weight_ref, wide_ref, narrow_ref, a1_ref, s1_ref, h1_ref, a2_ref, s2_ref):
    x = jnp.concatenate(ordered(side_ref[0], own_ref[...], other_ref[...]), axis=1)
    normed, _ = norm(x)
    act, slope = gelu_both(normed * wide_ref[0:1, :] + wide_ref[1:2, :])
    act = act.astype(jnp.bfloat16)
    a1_ref[...] = act
    s1_ref[...] = slope
    h1 = dot(act, weight_ref[...]) + narrow_ref[0:1, :]
    h1_ref[...] = h1
    normed, _ = norm(h1)
    act, slope = gelu_both(normed * narrow_ref[1:2, :] + narrow_ref[2:3, :])
    keep = keep_ref[...]
    a2_ref[...] = (act * keep).astype(jnp.bfloat16)
    s2_ref[...] = slope * keep


def second_kernel(side_ref, own_ref, other_ref, taps_ref, framed_ref, conv_ref, weight_ref, wide_ref, narrow_ref, h3_ref, a3_ref, s3_ref, out_own_ref, out_other_ref):
    count = own_ref.shape[0]
    half = own_ref.shape[1]
    base = pl.multiple_of(pl.program_id(0) * count, count)
    h3 = dot(windowed(framed_ref, taps_ref[...], base, count), conv_ref[...]) + narrow_ref[3:4, :]
    h3_ref[...] = h3
    normed, _ = norm(h3)
    act, slope = gelu_both(normed * narrow_ref[4:5, :] + narrow_ref[5:6, :])
    act = act.astype(jnp.bfloat16)
    a3_ref[...] = act
    s3_ref[...] = slope
    mixed = dot(act, weight_ref[...], ((1,), (1,))) + wide_ref[2:3, :]
    left, right = mixed[:, :half], mixed[:, half:]
    low = side_ref[0] == 0
    out_own_ref[...] = (own_ref[...].astype(jnp.float32) + jnp.where(low, left, right)).astype(jnp.bfloat16)
    out_other_ref[...] = (other_ref[...].astype(jnp.float32) + jnp.where(low, right, left)).astype(jnp.bfloat16)


def third_kernel(side_ref, own_ref, other_ref, h3_ref, s3_ref, weight_ref, narrow_ref, dh3_ref, gy_ref, wide_sum_ref, sum_ref):
    @pl.when(pl.program_id(0) == 0)
    def _():
        wide_sum_ref[...] = jnp.zeros_like(wide_sum_ref)
        sum_ref[...] = jnp.zeros_like(sum_ref)

    gy = jnp.concatenate(ordered(side_ref[0], own_ref[...], other_ref[...]), axis=1)
    wide_sum_ref[0:1, :] += column_sums(gy)
    gy = gy.astype(jnp.bfloat16)
    gy_ref[...] = gy
    dz3 = dot(gy, weight_ref[...]) * s3_ref[...]
    normed, scale = norm(h3_ref[...])
    dh3 = norm_back(dz3, normed, scale, narrow_ref[4:5, :]).astype(jnp.bfloat16)
    dh3_ref[...] = dh3
    sum_ref[0:1, :] += column_sums(dh3.astype(jnp.float32))
    sum_ref[1:2, :] += column_sums(dz3 * normed)
    sum_ref[2:3, :] += column_sums(dz3)


def fourth_kernel(side_ref, own_ref, other_ref, gy_own_ref, taps_ref, framed_ref, conv_ref, h1_ref, s2_ref, s1_ref, weight_ref, wide_ref, narrow_ref, dh1_ref, dx_own_ref, dx_other_ref, wide_sum_ref, sum_ref):
    @pl.when(pl.program_id(0) == 0)
    def _():
        wide_sum_ref[...] = jnp.zeros_like(wide_sum_ref)
        sum_ref[...] = jnp.zeros_like(sum_ref)

    count = own_ref.shape[0]
    half = own_ref.shape[1]
    base = pl.multiple_of(pl.program_id(0) * count, count)
    dz2 = dot(windowed(framed_ref, taps_ref[...], base, count), conv_ref[...]) * s2_ref[...]
    normed, scale = norm(h1_ref[...])
    dh1 = norm_back(dz2, normed, scale, narrow_ref[1:2, :]).astype(jnp.bfloat16)
    dh1_ref[...] = dh1
    sum_ref[0:1, :] += column_sums(dh1.astype(jnp.float32))
    sum_ref[1:2, :] += column_sums(dz2 * normed)
    sum_ref[2:3, :] += column_sums(dz2)
    dz1 = dot(dh1, weight_ref[...], ((1,), (1,))) * s1_ref[...]
    x = jnp.concatenate(ordered(side_ref[0], own_ref[...], other_ref[...]), axis=1)
    normed, scale = norm(x)
    dx = norm_back(dz1, normed, scale, wide_ref[0:1, :])
    wide_sum_ref[0:1, :] += column_sums(dz1 * normed)
    wide_sum_ref[1:2, :] += column_sums(dz1)
    low = side_ref[0] == 0
    left, right = dx[:, :half], dx[:, half:]
    dx_own_ref[...] = jnp.where(low, left, right) + gy_own_ref[...].astype(jnp.float32)
    dx_other_ref[...] = jnp.where(low, right, left).astype(jnp.bfloat16)


def grad_kernel(left_ref, right_ref, out_ref):
    out_ref[...] = dot(left_ref[...], right_ref[...], ((0,), (0,)))


def conv_grad_kernel(framed_ref, taps_ref, right_ref, out_ref):
    tap = pl.program_id(0)
    count = right_ref.shape[0]
    base = pl.multiple_of(tap * DILATION_STEP, DILATION_STEP)
    left = framed_ref[pl.ds(base, count), :] * taps_ref[0]
    out_ref[0] = dot(left, right_ref[...], ((0,), (0,)))


VMEM_LIMIT = 56 * 2**20


def once(shape):
    return pl.BlockSpec(shape, lambda *_: (0,) * len(shape), pipeline_mode=pl.Buffered(1))


def by_rows(count, width):
    return pl.BlockSpec((count, width), lambda i, *_: (i, 0))


def row_call(kernel, side, rows, count, operands, outs, flops):
    in_specs = [by_rows(count, a.shape[1]) if how == "rows" else once(a.shape) for a, how in operands]
    out_specs = [
        by_rows(count, width) if how == "rows" else pl.BlockSpec((8, width), lambda i, *_: (0, 0))
        for width, _, how in outs
    ]
    out_shape = [
        jax.ShapeDtypeStruct((rows if how == "rows" else 8, width), dtype) for width, dtype, how in outs
    ]
    moved = sum(a.size * a.dtype.itemsize for a, _ in operands)
    moved += sum(o.size * o.dtype.itemsize for o in out_shape)
    return pl.pallas_call(
        kernel,
        grid_spec=pltpu.PrefetchScalarGridSpec(
            num_scalar_prefetch=1, grid=(rows // count,), in_specs=in_specs, out_specs=out_specs
        ),
        out_shape=out_shape,
        compiler_params=pltpu.CompilerParams(
            dimension_semantics=("arbitrary",), vmem_limit_bytes=VMEM_LIMIT
        ),
        cost_estimate=pl.CostEstimate(flops=flops // 32, bytes_accessed=moved // 32, transcendentals=0),
    )(side, *[a for a, _ in operands])


def matrix_grad(left, right, tiles):
    rows, height = left.shape
    width = right.shape[1]
    return pl.pallas_call(
        grad_kernel,
        grid=(tiles,),
        in_specs=[pl.BlockSpec((rows, height // tiles), lambda i: (0, i)), once((rows, width))],
        out_specs=pl.BlockSpec((height // tiles, width), lambda i: (i, 0)),
        out_shape=jax.ShapeDtypeStruct((height, width), jnp.float32),
        compiler_params=pltpu.CompilerParams(
            dimension_semantics=("arbitrary",), vmem_limit_bytes=VMEM_LIMIT
        ),
        cost_estimate=pl.CostEstimate(
            flops=rows * height * width // 16, bytes_accessed=rows * (height + width) // 16, transcendentals=0
        ),
    )(left, right)


def conv_grad(framed_rows, taps, right):
    rows, width = right.shape
    return pl.pallas_call(
        conv_grad_kernel,
        grid=(KERNEL_TAPS,),
        in_specs=[
            once(framed_rows.shape),
            pl.BlockSpec((1, rows, 1), lambda i: (i, 0, 0)),
            once((rows, width)),
        ],
        out_specs=pl.BlockSpec((1, width, width), lambda i: (i, 0, 0)),
        out_shape=jax.ShapeDtypeStruct((KERNEL_TAPS, width, width), jnp.float32),
        compiler_params=pltpu.CompilerParams(
            dimension_semantics=("arbitrary",), vmem_limit_bytes=VMEM_LIMIT
        ),
        cost_estimate=pl.CostEstimate(
            flops=KERNEL_TAPS * rows * width * width // 16, bytes_accessed=rows * width // 8, transcendentals=0
        ),
    )(framed_rows, taps, right)


def framed(block, width):
    count = lax.axis_size("seq")
    forward = [(i, i + 1) for i in range(count - 1)]
    backward = [(i + 1, i) for i in range(count - 1)]
    low = lax.ppermute(block[block.shape[0] - width :], "seq", forward)
    high = lax.ppermute(block[:width], "seq", backward)
    return jnp.concatenate([low, block, high], axis=0)


def scattered(value, order):
    count = lax.axis_size("seq")
    place = lax.axis_index("seq")
    bits = count.bit_length() - 1
    value = value.reshape((2,) * bits + value.shape[1:])
    left = list(range(bits))
    for bit in order:
        dim = left.index(bits - 1 - bit)
        left.remove(bits - 1 - bit)
        mine = (place >> bit) & 1
        keep = lax.dynamic_index_in_dim(value, mine, dim, keepdims=False)
        send = lax.dynamic_index_in_dim(value, 1 - mine, dim, keepdims=False).astype(jnp.bfloat16)
        came = lax.ppermute(send, "seq", [(i, i ^ (1 << bit)) for i in range(count)])
        value = keep + came.astype(jnp.float32)
    return value


def body(
    tokens,
    cotangent,
    seq_lengths,
    residue_mask,
    first_gain,
    first_shift,
    proj_in,
    in_bias,
    mid_gain,
    mid_shift,
    conv_weight,
    conv_bias,
    last_gain,
    last_shift,
    proj_out,
    out_bias,
):
    micro, rows, half = tokens.shape
    inner_half = in_bias.shape[0]
    inner = 2 * inner_half
    model = 2 * half
    seq_count = lax.axis_size("seq")
    count = 256
    side = lax.axis_index("ch")
    side_array = side.astype(jnp.int32).reshape(1)
    low_side = side == 0

    def swap(value):
        return lax.ppermute(value, "ch", SWAP)

    def whole(own, other, axis):
        return jnp.where(
            low_side,
            jnp.concatenate([own, other], axis=axis),
            jnp.concatenate([other, own], axis=axis),
        )

    def own_of(value):
        return lax.dynamic_index_in_dim(value, side, 0, keepdims=False)

    def other_of(value):
        return lax.dynamic_index_in_dim(value, 1 - side, 0, keepdims=False)

    own_vectors = jnp.concatenate(
        [first_gain, first_shift, out_bias, in_bias, mid_gain, mid_shift, conv_bias, last_gain, last_shift]
    )
    part_in = proj_in.shape[0]
    part_conv = conv_weight.shape[1]
    own_weights = jnp.concatenate(
        [proj_in, proj_out.T, conv_weight.reshape(KERNEL_TAPS * part_conv, inner_half)], axis=0
    )
    own_vectors, own_weights = lax.optimization_barrier((own_vectors, own_weights))
    other_vectors, other_weights = swap(own_vectors), swap(own_weights)
    tokens_tied, other_vectors, other_weights = lax.optimization_barrier(
        (other_of(tokens), other_vectors, other_weights)
    )
    both = whole(own_weights, other_weights, 1)
    vectors = jnp.where(
        low_side, jnp.stack([own_vectors, other_vectors]), jnp.stack([other_vectors, own_vectors])
    )
    x_own = own_of(tokens)
    x_other = swap(tokens_tied)
    gy_own = own_of(cotangent)
    gy_tied, _ = lax.optimization_barrier((other_of(cotangent), x_other))
    gy_other = swap(gy_tied)

    gathered = lax.all_gather(both, "seq", axis=0)
    weight_in = gathered[:, :part_in].reshape(model, inner)
    weight_out = gathered[:, part_in : 2 * part_in].reshape(model, inner)
    weight_conv = (
        gathered[:, 2 * part_in :]
        .reshape(seq_count, KERNEL_TAPS, part_conv, inner)
        .transpose(1, 0, 2, 3)
        .reshape(KERNEL_TAPS, inner, inner)
    )
    wide = jnp.stack([vectors[:, i * half : (i + 1) * half].reshape(-1) for i in range(3)])
    narrow = jnp.stack(
        [
            vectors[:, 3 * half + i * inner_half : 3 * half + (i + 1) * inner_half].reshape(-1)
            for i in range(6)
        ]
    )

    places = lax.axis_index("seq") * rows + jnp.arange(rows + 2 * HALO, dtype=jnp.int32) - HALO
    inside = (places >= 0) & (places < rows * seq_count)
    bounds = jnp.cumsum(own_of(seq_lengths))[:-1]
    segment = jnp.sum((places[:, None] >= bounds[None, :]).astype(jnp.int32), axis=1)
    segment = jnp.where(inside, segment, -1)
    middle = segment[HALO : HALO + rows]
    tap_list = [
        (segment[tap * DILATION_STEP : tap * DILATION_STEP + rows] == middle).astype(jnp.bfloat16)
        for tap in range(KERNEL_TAPS)
    ]
    taps = jnp.stack(tap_list, axis=1)
    keep = own_of(residue_mask).astype(jnp.float32)[:, None]
    f32, bf16 = jnp.float32, jnp.bfloat16
    product = 2 * rows * model * inner

    a1, s1, h1, a2, s2 = row_call(
        first_kernel,
        side_array,
        rows,
        count,
        [(x_own, "rows"), (x_other, "rows"), (keep, "rows"), (weight_in, "once"), (wide, "once"), (narrow, "once")],
        [(model, bf16, "rows"), (model, f32, "rows"), (inner, f32, "rows"), (inner, bf16, "rows"), (inner, f32, "rows")],
        product,
    )
    a2 = framed(a2, HALO)
    h3, a3, s3, out_own, out_other = row_call(
        second_kernel,
        side_array,
        rows,
        count,
        [
            (x_own, "rows"),
            (x_other, "rows"),
            (taps, "rows"),
            (a2, "once"),
            (weight_conv.reshape(KERNEL_TAPS * inner, inner), "once"),
            (weight_out, "once"),
            (wide, "once"),
            (narrow, "once"),
        ],
        [(inner, f32, "rows"), (inner, bf16, "rows"), (inner, f32, "rows"), (half, bf16, "rows"), (half, bf16, "rows")],
        4 * product,
    )
    out_back = swap(out_other)

    dh3, gy, wide_sum_3, sum_3 = row_call(
        third_kernel,
        side_array,
        rows,
        count,
        [(gy_own, "rows"), (gy_other, "rows"), (h3, "rows"), (s3, "rows"), (weight_out, "once"), (narrow, "once")],
        [(inner, bf16, "rows"), (model, bf16, "rows"), (model, f32, "sum"), (inner, f32, "sum")],
        product,
    )
    dh3_framed = framed(dh3, HALO)
    grad_out = matrix_grad(gy, a3, 2)
    grad_conv = conv_grad(a2, jnp.stack(tap_list, axis=0)[:, :, None], dh3)
    dh3_framed, out_back = lax.optimization_barrier((dh3_framed, out_back))
    flipped = jnp.flip(weight_conv, 0).transpose(0, 2, 1).reshape(KERNEL_TAPS * inner, inner)
    dh1, dx_own, dx_other, wide_sum_1, sum_1 = row_call(
        fourth_kernel,
        side_array,
        rows,
        count,
        [
            (x_own, "rows"),
            (x_other, "rows"),
            (gy_own, "rows"),
            (taps, "rows"),
            (dh3_framed, "once"),
            (flipped, "once"),
            (h1, "rows"),
            (s2, "rows"),
            (s1, "rows"),
            (weight_in, "once"),
            (wide, "once"),
            (narrow, "once"),
        ],
        [(inner, bf16, "rows"), (half, f32, "rows"), (half, bf16, "rows"), (model, f32, "sum"), (inner, f32, "sum")],
        4 * product,
    )
    dx_back = swap(dx_other)
    grad_in = matrix_grad(a1, dh1, 2)

    def placed(own, back):
        return jnp.where(low_side, jnp.stack([own, back], 0), jnp.stack([back, own], 0))

    block_out = placed(out_own, out_back)
    grad_tokens = placed(
        dx_own, dx_back.astype(f32) + other_of(cotangent).astype(f32)
    )

    bits = list(range(seq_count.bit_length() - 1))
    swapped_bits = [bits[0]] + bits[2:] + [bits[1]]
    part = jnp.concatenate(
        [
            scattered(grad_in.reshape(seq_count, part_in, inner), bits),
            scattered(grad_out.reshape(seq_count, part_in, inner), swapped_bits),
            scattered(
                grad_conv.reshape(KERNEL_TAPS, seq_count, part_conv, inner).transpose(1, 0, 2, 3), bits
            ).reshape(KERNEL_TAPS * part_conv, inner),
        ],
        axis=0,
    )
    left, right = part[:, :inner_half], part[:, inner_half:]
    part_other = swap(jnp.where(low_side, right, left).astype(bf16))
    part = jnp.where(low_side, left, right) + part_other.astype(f32)

    smalls = jnp.concatenate(
        [
            small.reshape(2, -1)
            for small in (wide_sum_1[0], wide_sum_1[1], wide_sum_3[0], sum_1[0], sum_1[1], sum_1[2], sum_3[0], sum_3[1], sum_3[2])
        ],
        axis=1,
    )
    totals = smalls
    for bit in bits:
        totals = totals + lax.ppermute(totals, "seq", [(i, i ^ (1 << bit)) for i in range(seq_count)])
    totals = own_of(totals) + swap(other_of(totals))
    sizes = [half] * 3 + [inner_half] * 6
    parts = []
    at = 0
    for size in sizes:
        parts.append(totals[at : at + size])
        at += size
    return (
        block_out,
        grad_tokens,
        parts[0],
        parts[1],
        part[:part_in],
        parts[3],
        parts[4],
        parts[5],
        part[2 * part_in :].reshape(KERNEL_TAPS, part_conv, inner_half),
        parts[6],
        parts[7],
        parts[8],
        part[part_in : 2 * part_in].T,
        parts[2],
    )


BLOCK = 256
CHUNKS = 4
CONV_PAD = 8
HEAD = 5
LEAD = 128


def fast_kernel(
    tokens, cot, lengths, residues, proj_in, proj_out, conv_own, *rest,
) -> None:
    vectors, refs = rest[:9], rest[9:]
    fast_steps(tokens, cot, lengths, residues, proj_in, proj_out, conv_own, vectors, *refs)


def fast_steps(
    tokens, cot, lengths, residues, proj_in, proj_out, conv_own, vectors,
    out_own, out_back, dx_own, dx_back, dx_tail, dx_end, grads_out, sums_out,
    x_other, g_conv, s1, h1, s2, h3, s3,
    masks, own_vectors, other_vectors, wide, narrow, stage,
    a1v, a2f, a3v, gyv, dh3f, out_send, w_in, w_out, w_conv,
    k_in, s_in, r0_in, r1_in, r2_in, r3_in,
    k_out, s_out, r0_out, r1_out, r2_out, r3_out,
    k_low, s_low, r0_low, r1_low, r2_low, r3_low,
    k_mid, s_mid, r0_mid, r1_mid, r2_mid, r3_mid,
    k_top, s_top, r0_top, r1_top, r2_top, r3_top,
    smalls, cross_send, cross_recv, small_send, small_recv, load_sems,
    swap_sems, token_sems, in_gather, out_gather, conv_gather, gy_sems, out_sems, dx_sems, a2_sems, dh3_sems, in_sems, out_rs_sems, low_sems, mid_sems, top_sems, cross_sems, small_sems,
):
    rows = a1v.shape[0]
    half = tokens.shape[2]
    inner = narrow.shape[1]
    part = rows // CHUNKS
    side = lax.axis_index("ch")
    place = lax.axis_index("seq")
    last = lax.axis_size("seq") - 1
    low = side == 0
    bits = [lax.rem(place // (1 << bit), 2) for bit in range(4)]
    across = {"ch": 1 - side}
    pairs = [{"seq": place + (1 << bit) * (1 - 2 * bits[bit])} for bit in range(4)]
    before = {"seq": lax.rem(place + last, last + 1)}
    after = {"seq": lax.rem(place + 1, last + 1)}

    def remote(src, dst, sems, at, device):
        return pltpu.make_async_remote_copy(
            src_ref=src,
            dst_ref=dst,
            send_sem=sems.at[0, at],
            recv_sem=sems.at[1, at],
            device_id=device,
            device_id_type=pl.DeviceIdType.MESH,
        )

    def block(ref, at):
        return ref.at[pl.ds(pl.multiple_of(at * BLOCK, BLOCK), BLOCK)]


    def gy_copy(at):
        piece = pl.ds(at * part, part)
        return remote(cot.at[1 - side, piece], gyv.at[side, piece], gy_sems, at, across)

    token_part = (rows - LEAD) // CHUNKS

    def token_copy(at):
        piece = pl.ds(pl.multiple_of(LEAD + at * token_part, 16), token_part)
        return remote(tokens.at[1 - side, piece], x_other.at[piece], token_sems, at, across)

    lead = pl.ds(0, LEAD)
    lead_copy = remote(tokens.at[1 - side, lead], x_other.at[lead], token_sems, CHUNKS, across)

    tail_rows = k_top.shape[1]
    own_gy = pltpu.make_async_copy(cot.at[side], gyv.at[side], load_sems.at[0])
    def out_copy(at):
        return remote(block(out_send, at), block(out_back, at), out_sems, at, across)

    def dx_copy(at):
        return remote(block(gyv.at[1 - side], at), block(dx_back, at), dx_sems, at, across)

    def halo_low(framed_rows, sems):
        return remote(framed_rows.at[pl.ds(HALO, HALO)], framed_rows.at[pl.ds(HALO + rows, HALO)], sems, 0, before)

    def halo_high(framed_rows, sems):
        return remote(framed_rows.at[pl.ds(rows, HALO)], framed_rows.at[pl.ds(0, HALO)], sems, 1, after)

    def halo_start(framed_rows, sems):
        @pl.when(place > 0)
        def _():
            halo_low(framed_rows, sems).start()

        @pl.when(place < last)
        def _():
            halo_high(framed_rows, sems).start()

    def halo_wait(framed_rows, sems):
        @pl.when(place > 0)
        def _():
            halo_low(framed_rows, sems).wait_send()
            halo_high(framed_rows, sems).wait_recv()

        @pl.when(place < last)
        def _():
            halo_high(framed_rows, sems).wait_send()
            halo_low(framed_rows, sems).wait_recv()

    blocks = rows // BLOCK
    per = part // BLOCK

    def middle_first(step):
        late = step // (blocks - 2)
        return (step + 1) * (1 - late) + late * (step - (blocks - 2)) * (blocks - 1)

    def in_order(step):
        return step

    def pipeline(step, order, ins, outs, tail=None, count=None):
        def spec(ref):
            return pl.BlockSpec((BLOCK, ref.shape[-1]), lambda i: (order(i), 0))

        out_specs = [spec(r) for r in outs]
        if tail is not None:
            ahead, end = tail
            most = blocks - 2 - HEAD
            outs = outs + [ahead, end]
            out_specs.append(
                pl.BlockSpec((BLOCK, half), lambda i: (jnp.minimum(jnp.maximum(i - HEAD, 0), most), 0))
            )
            out_specs.append(pl.BlockSpec((BLOCK, half), lambda i: (0, 0)))
        pltpu.emit_pipeline(step, grid=(count or blocks,), in_specs=[spec(r) for r in ins], out_specs=out_specs)(*ins, *outs)

    barrier = pltpu.get_barrier_semaphore()
    for device in [across] + pairs + [before, after]:
        pl.semaphore_signal(barrier, inc=1, device_id=device, device_id_type=pl.DeviceIdType.MESH)
    pl.semaphore_wait(barrier, 7)

    lead_copy.start()
    height = inner // 16
    part_in = proj_in.shape[0]
    quarter = half // 2
    wanted = quarter + 64
    packed = cross_send.shape[0]

    def pack(pieces):
        pieces = [piece.astype(jnp.float32) for piece in pieces]
        short = 2 * packed - sum(piece.shape[0] for piece in pieces)
        value = jnp.concatenate(pieces + [jnp.zeros((short, quarter), jnp.float32)], axis=0)
        cross_send[...] = jnp.concatenate([value[:packed], value[packed:]], axis=1).astype(jnp.bfloat16)

    def unpack(ref):
        value = ref[...].astype(jnp.float32)
        return jnp.concatenate([value[:, :quarter], value[:, quarter:]], axis=0)

    pack([proj_in[...], proj_out[...]] + [conv_own[tap] for tap in range(KERNEL_TAPS)])
    own_vectors[...] = jnp.zeros_like(own_vectors)
    at = 0
    for vector in vectors:
        width = vector.shape[0]
        own_vectors[:, at : at + width] = vector[...].reshape(1, width)
        at += width + width % 128
    swaps = [
        remote(cross_send, cross_recv, swap_sems, 0, across),
        remote(own_vectors, other_vectors, swap_sems, 1, across),
    ]
    for swap in swaps:
        swap.start()
    for at in range(CHUNKS):
        token_copy(at).start()
    for at in range(CHUNKS):
        gy_copy(at).start()
    own_gy.start()

    ends = jnp.where(low, lengths[0:1, :], lengths[1:2, :]).astype(jnp.float32)
    count = ends.shape[1]
    upper = lax.broadcasted_iota(jnp.int32, (count, count), 0) <= lax.broadcasted_iota(jnp.int32, (count, count), 1)
    ends = lax.dot_general(
        jnp.broadcast_to(ends, (8, count)),
        upper.astype(jnp.float32),
        (((1,), (0,)), ((), ())),
        precision=lax.Precision.HIGHEST,
        preferred_element_type=jnp.float32,
    )[0:1, :]

    def mask_block(at, _):
        base = pl.multiple_of(at * BLOCK, BLOCK)
        span = BLOCK + 2 * HALO
        spot = lax.broadcasted_iota(jnp.int32, (span, count), 0) + (place * rows + base - HALO)
        inside = (spot >= 0) & (spot < rows * (last + 1))
        reached = jnp.where(ends <= spot.astype(jnp.float32), 1.0, 0.0)
        segment = jnp.sum(jnp.where(inside, reached, -1.0 / count), axis=1, keepdims=True)
        own_segment = segment[HALO : HALO + BLOCK]
        lane = lax.broadcasted_iota(jnp.int32, (BLOCK, 8), 1)
        columns = jnp.zeros((BLOCK, 8), jnp.float32)
        for tap in range(KERNEL_TAPS):
            same = segment[tap * DILATION_STEP : tap * DILATION_STEP + BLOCK] == own_segment
            columns = jnp.where((lane == tap) & same, 1.0, columns)
        kept = residues[:, pl.ds(base, BLOCK)]
        kept = jnp.where(low, kept[0:1, :], kept[1:2, :]).astype(jnp.float32)
        square = (BLOCK, BLOCK)
        diagonal = lax.broadcasted_iota(jnp.int32, square, 0) == lax.broadcasted_iota(jnp.int32, square, 1)
        keep = jnp.sum(jnp.where(diagonal, kept, 0.0), axis=1, keepdims=True)
        columns = jnp.where(lane == KERNEL_TAPS, keep, columns)
        masks[pl.ds(base, BLOCK), :] = columns.astype(jnp.bfloat16)
        return 0

    lax.fori_loop(0, rows // BLOCK, mask_block, 0)
    smalls[...] = jnp.zeros_like(smalls)

    @pl.when(place == 0)
    def _():
        a2f[0:HALO, :] = jnp.zeros((HALO, inner), jnp.bfloat16)
        dh3f[0:HALO, :] = jnp.zeros((HALO, inner), jnp.bfloat16)

    @pl.when(place == last)
    def _():
        a2f[HALO + rows :, :] = jnp.zeros((HALO, inner), jnp.bfloat16)
        dh3f[HALO + rows :, :] = jnp.zeros((HALO, inner), jnp.bfloat16)

    def both(own, other):
        left, right = ordered(side, own, other)
        return jnp.concatenate([left, right], axis=1)

    for swap in swaps:
        swap.wait()
    rows_here = both(unpack(cross_send), unpack(cross_recv)).astype(jnp.bfloat16)
    here = (bits[3], bits[2], bits[1], bits[0])
    w_in[here] = rows_here[:part_in]
    w_out[here] = rows_here[part_in : 2 * part_in]
    stage[0, 0] = rows_here[2 * part_in : 2 * part_in + stage.shape[2]]
    own_conv = pltpu.make_async_copy(stage.at[0, 0], g_conv.at[here], load_sems.at[1])
    own_conv.start()
    for index in range(3):
        lanes = slice(index * half, (index + 1) * half)
        wide[index : index + 1, :] = both(own_vectors[:, lanes], other_vectors[:, lanes])
    for index in range(6):
        lanes = slice(3 * half + index * wanted, 3 * half + index * wanted + quarter)
        narrow[index : index + 1, :] = both(own_vectors[:, lanes], other_vectors[:, lanes])

    def gather_copy(group, level):
        ref, sems, order = group
        every = slice(None)
        at = tuple(every if bit in order[:level] else bits[bit] for bit in (3, 2, 1, 0))
        return remote(ref.at[at], ref.at[at], sems, level, pairs[order[level]])

    in_rows = (w_in, in_gather, (3, 2, 1, 0))
    out_rows = (w_out, out_gather, (1, 3, 2, 0))
    conv_rows = (g_conv, conv_gather, (3, 2, 1, 0))

    def gather_next(group, level):
        gather_copy(group, level).wait()
        if level < 3:
            gather_copy(group, level + 1).start()

    gather_copy(in_rows, 0).start()
    gather_copy(out_rows, 0).start()
    own_conv.wait()
    gather_next(in_rows, 0)
    gather_copy(conv_rows, 0).start()
    gather_next(in_rows, 1)
    gather_next(in_rows, 2)
    gather_next(conv_rows, 0)
    gather_next(out_rows, 0)
    gather_next(in_rows, 3)

    def first_chunk(at, _):
        token_copy(at).wait_recv()

        def first(own, other, s1_block, h1_block, s2_block):
            base = pl.multiple_of((at * per + pl.program_id(0)) * BLOCK, BLOCK)
            x = jnp.concatenate(ordered(side, own[...], other[...]), axis=1)
            normed, _ = norm(x)
            act, slope = gelu_both(normed * wide[0:1, :] + wide[1:2, :])
            act = act.astype(jnp.bfloat16)
            a1v[pl.ds(base, BLOCK), :] = act
            s1_block[...] = slope
            value = dot(act, w_in[...].reshape(2 * half, inner)) + narrow[0:1, :]
            h1_block[...] = value
            normed, _ = norm(value)
            act, slope = gelu_both(normed * narrow[1:2, :] + narrow[2:3, :])
            keep = masks[pl.ds(base, BLOCK), KERNEL_TAPS : KERNEL_TAPS + 1].astype(jnp.float32)
            a2f[pl.ds(HALO + base, BLOCK), :] = (act * keep).astype(jnp.bfloat16)
            s2_block[...] = slope * keep

        pipeline(first, lambda i: at * per + i, [tokens.at[side], x_other], [s1, h1, s2], count=per)
        for level, (group, ready) in enumerate(((conv_rows, 1), (out_rows, 1), (out_rows, 2))):

            @pl.when(at == level)
            def _():
                gather_next(group, ready)

        return 0

    lead_copy.wait_recv()
    lax.fori_loop(0, CHUNKS, first_chunk, 0)
    halo_start(a2f, a2_sems)
    gather_next(conv_rows, 2)
    gather_next(out_rows, 3)
    gather_next(conv_rows, 3)

    def conv_load(pair):
        return pltpu.make_async_copy(g_conv.at[pair // 2, pair % 2], stage, load_sems.at[2])

    def relay(pair, _):
        conv_load(pair).start()
        conv_load(pair).wait()
        for low_bit in range(2):
            even = stage[low_bit, 0].astype(jnp.float32)
            odd = stage[low_bit, 1].astype(jnp.float32)
            at = pl.multiple_of((2 * pair + low_bit) * 2 * height, 2 * height)
            for tap in range(KERNEL_TAPS):
                top = tap * height
                w_conv[tap, pl.ds(at, 2 * height), :] = jnp.concatenate(
                    [even[top : top + height], odd[top : top + height]], axis=0
                ).astype(jnp.bfloat16)

        return 0

    lax.fori_loop(0, 4, relay, 0)

    def second(own, other, h3_block, s3_block, own_block):
        step = pl.program_id(0)
        at = middle_first(step)
        base = pl.multiple_of(at * BLOCK, BLOCK)

        @pl.when(step == blocks - 2)
        def _():
            halo_wait(a2f, a2_sems)

        taps = masks[pl.ds(base, BLOCK), :]
        weight = w_conv[...].reshape(KERNEL_TAPS * inner, inner)
        value = dot(windowed(a2f, taps, base, BLOCK), weight) + narrow[3:4, :]
        h3_block[...] = value
        normed, _ = norm(value)
        act, slope = gelu_both(normed * narrow[4:5, :] + narrow[5:6, :])
        act = act.astype(jnp.bfloat16)
        a3v[pl.ds(base, BLOCK), :] = act
        s3_block[...] = slope
        mixed = dot(act, w_out[...].reshape(2 * half, inner), ((1,), (1,))) + wide[2:3, :]
        left, right = mixed[:, :half], mixed[:, half:]
        own_block[...] = (own[...].astype(jnp.float32) + jnp.where(low, left, right)).astype(jnp.bfloat16)
        out_send[pl.ds(base, BLOCK), :] = (
            other[...].astype(jnp.float32) + jnp.where(low, right, left)
        ).astype(jnp.bfloat16)
        out_copy(at).start()

    pipeline(second, middle_first, [tokens.at[side], x_other], [h3, s3, out_own])

    def add_small(row, value):
        smalls[row : row + 1, :] += value

    def add_wide(row, value):
        smalls[row : row + 1, :] += value[:, :half]
        smalls[row + 1 : row + 2, :] += value[:, half:]

    def third(h3_block, s3_block):
        at = pl.program_id(0)
        base = pl.multiple_of(at * BLOCK, BLOCK)
        for later in range(CHUNKS):

            @pl.when(at == later * per)
            def _():
                gy_copy(later).wait_recv()

        gy = jnp.concatenate([gyv[0, pl.ds(base, BLOCK), :], gyv[1, pl.ds(base, BLOCK), :]], axis=1)
        add_wide(4, column_sums(gy.astype(jnp.float32)))
        dz3 = dot(gy, w_out[...].reshape(2 * half, inner)) * s3_block[...]
        normed, scale = norm(h3_block[...])
        dh3 = norm_back(dz3, normed, scale, narrow[4:5, :]).astype(jnp.bfloat16)
        dh3f[pl.ds(HALO + base, BLOCK), :] = dh3
        add_small(9, column_sums(dh3.astype(jnp.float32)))
        add_small(10, column_sums(dz3 * normed))
        add_small(11, column_sums(dz3))

    own_gy.wait()
    pipeline(third, in_order, [h3, s3], [])
    halo_start(dh3f, dh3_sems)

    def slot(pair, order):
        two = (pair % 4) if order[0] == 1 else (pair % 4) // 2 + 2 * (pair % 2)
        return pair // 4 * 4 + two

    def split(group, at, even, odd):
        keep_ref, send_ref = group[0], group[1]
        mine_first = bits[0] == 0
        keep_ref[at] = jnp.where(mine_first, even, odd)
        send_ref[at] = jnp.where(mine_first, odd, even).astype(jnp.bfloat16)

    def wide_grad(left_of, right_ref, group):
        tall_rows = group[0].shape[1]

        def tile(at, _):
            value = dot(left_of(at), right_ref[...], ((0,), (0,)))
            for pair in range(4):
                top = 2 * pair * tall_rows
                split(
                    group,
                    at * 4 + slot(pair, group[4]),
                    value[top : top + tall_rows],
                    value[top + tall_rows : top + 2 * tall_rows],
                )
            return 0

        lax.fori_loop(0, 2, tile, 0)
        sum_copy(group, 0).start()

    def conv_grad_of(taps, group):
        right = dh3f.at[pl.ds(HALO, rows)]
        values = []
        for tap in taps:
            left = a2f[tap * DILATION_STEP : tap * DILATION_STEP + rows, :] * masks[:, tap : tap + 1]
            values.append(dot(left, right[...], ((0,), (0,))))
        if len(values) == 1:
            tail = [jnp.zeros((CONV_PAD, inner), jnp.float32)]
        else:
            tail = []
        for pair in range(8):
            top = 2 * pair * height
            split(
                group,
                slot(pair, group[4]),
                jnp.concatenate([v[top : top + height] for v in values] + tail, axis=0),
                jnp.concatenate([v[top + height : top + 2 * height] for v in values] + tail, axis=0),
            )
        sum_copy(group, 0).start()

    y_first, z_first = (1, 2, 3), (2, 1, 3)
    in_set = (k_in, s_in, (r0_in, r1_in, r2_in, r3_in), in_sems, y_first)
    out_set = (k_out, s_out, (r0_out, r1_out, r2_out, r3_out), out_rs_sems, z_first)
    low_set = (k_low, s_low, (r0_low, r1_low, r2_low, r3_low), low_sems, y_first)
    mid_set = (k_mid, s_mid, (r0_mid, r1_mid, r2_mid, r3_mid), mid_sems, z_first)
    top_set = (k_top, s_top, (r0_top, r1_top, r2_top, r3_top), top_sems, y_first)
    starts = (0, 0, 4, 6)
    lengths = (8, 4, 2, 1)

    def sum_copy(group, level):
        _, send, received, sems, order = group
        bit = 0 if level == 0 else order[level - 1]
        return remote(
            send.at[pl.ds(starts[level], lengths[level])], received[level], sems, level, pairs[bit]
        )

    def sum_step(group, level):
        keep, send, received, _, order = group
        sum_copy(group, level).wait()
        came = received[level]
        fixed = 0
        for at in range(level):
            fixed = fixed + bits[order[at]] * (1 << at)
        if level == 3:
            keep[fixed] = keep[fixed] + came[0].astype(jnp.float32)
            return
        mine = bits[order[level]]

        def one(item, _):
            other = 2 * item + 1 - mine
            same = 2 * item + mine
            send[starts[level + 1] + item] = (
                keep[other * (1 << level) + fixed] + came[other].astype(jnp.float32)
            ).astype(jnp.bfloat16)
            at = same * (1 << level) + fixed
            keep[at] = keep[at] + came[same].astype(jnp.float32)
            return 0

        lax.fori_loop(0, lengths[level + 1], one, 0)
        sum_copy(group, level + 1).start()

    def at_step(step, when, *steps):
        @pl.when(step == when)
        def _():
            for group, level in steps:
                sum_step(group, level)

    conv_grad_of((0, 1), low_set)
    conv_grad_of((2, 3), mid_set)
    conv_grad_of((4,), top_set)
    wide_grad(lambda at: gyv[at], a3v, out_set)

    def fourth(h1_block, s2_block):
        step = pl.program_id(0)
        base = pl.multiple_of(step * BLOCK, BLOCK)
        taps = masks[pl.ds(base, BLOCK), :]
        da2 = jnp.zeros((BLOCK, inner), jnp.float32)
        for tap in range(KERNEL_TAPS):
            window = dh3f[pl.ds(base + tap * DILATION_STEP, BLOCK), :] * taps[:, tap : tap + 1]
            da2 = da2 + dot(window, w_conv[KERNEL_TAPS - 1 - tap], ((1,), (1,)))
        dz2 = da2 * s2_block[...]
        normed, scale = norm(h1_block[...])
        dh1 = norm_back(dz2, normed, scale, narrow[1:2, :]).astype(jnp.bfloat16)
        a3v[pl.ds(base, BLOCK), :] = dh1
        add_small(6, column_sums(dh1.astype(jnp.float32)))
        add_small(7, column_sums(dz2 * normed))
        add_small(8, column_sums(dz2))
        at_step(step, 0, (low_set, 0), (mid_set, 0), (top_set, 0))
        at_step(step, 1, (out_set, 0))
        at_step(step, 5, (low_set, 1))
        at_step(step, 6, (mid_set, 1))
        at_step(step, 7, (top_set, 1))

    halo_wait(dh3f, dh3_sems)
    pipeline(fourth, in_order, [h1, s2], [])
    wide_grad(lambda at: a1v[:, pl.ds(pl.multiple_of(at * half, 128), half)], a3v, in_set)
    sum_step(out_set, 1)
    sum_step(low_set, 2)

    def fifth(own, other, s1_block, own_block, tail_block, end_block):
        step = pl.program_id(0)
        base = pl.multiple_of(step * BLOCK, BLOCK)
        dh1 = a3v[pl.ds(base, BLOCK), :]
        dz1 = dot(dh1, w_in[...].reshape(2 * half, inner), ((1,), (1,))) * s1_block[...]
        x = jnp.concatenate(ordered(side, own[...], other[...]), axis=1)
        normed, scale = norm(x)
        dx = norm_back(dz1, normed, scale, wide[0:1, :])
        add_wide(0, column_sums(dz1 * normed))
        add_wide(2, column_sums(dz1))
        left, right = dx[:, :half], dx[:, half:]
        own_block[...] = jnp.where(low, left, right) + gyv[side, pl.ds(base, BLOCK), :].astype(jnp.float32)
        sent = jnp.where(low, right, left).astype(jnp.bfloat16)
        gyv[1 - side, pl.ds(base, BLOCK), :] = sent
        end_block[...] = sent

        @pl.when(step < blocks - 1)
        def _():
            tail_block[...] = sent

        @pl.when(step < HEAD - 1)
        def _():
            dx_copy(step).start()

        at_step(step, 0, (mid_set, 2), (in_set, 0))
        at_step(step, 2, (out_set, 2), (top_set, 2))
        at_step(step, 4, (low_set, 3))
        at_step(step, 5, (mid_set, 3))
        at_step(step, 6, (in_set, 1))
        at_step(step, 7, (top_set, 3), (out_set, 3))

    pipeline(fifth, in_order, [tokens.at[side], x_other, s1], [dx_own], (dx_tail, dx_end))


    def small_copy(level):
        device = pairs[level] if level < 4 else across
        return remote(small_send.at[level], small_recv.at[level], small_sems, level, device)

    def small_start(level):
        small_send[level] = smalls[...]
        small_copy(level).start()

    def small_step(level):
        small_copy(level).wait()
        smalls[...] += small_recv[level]

    small_start(0)
    sum_step(in_set, 2)
    small_step(0)
    small_start(1)
    small_step(1)
    small_start(2)
    small_step(2)
    small_start(3)
    sum_step(in_set, 3)
    small_step(3)
    small_start(4)

    def owned(group):
        keep, order = group[0], group[4]
        return keep[bits[order[0]] + 2 * bits[order[1]] + 4 * bits[order[2]]]

    groups = (in_set, out_set, low_set, mid_set, top_set)
    others = []
    for group in groups:
        value = owned(group)
        others.append(jnp.where(low, value[:, quarter:], value[:, :quarter]))
    pack(others)
    for at in range(blocks):
        out_copy(at).wait()
    cross = remote(cross_send, cross_recv, cross_sems, 0, across)
    cross.start()
    dx_copy(HEAD - 1).start()
    lead_copy.wait_send()
    for at in range(CHUNKS):
        token_copy(at).wait_send()
        gy_copy(at).wait_send()
    small_step(4)
    for index in range(3):
        both = smalls[2 * index : 2 * index + 2, :]
        sums_out[:, index * half : (index + 1) * half] = jnp.where(low, both[0:1], both[1:2])
    for index in range(6):
        both = smalls[6 + index : 7 + index, :]
        at = 3 * half + index * wanted
        sums_out[:, at : at + quarter] = jnp.where(low, both[:, :quarter], both[:, quarter:])
    cross.wait()
    came = unpack(cross_recv)
    row = 0
    for group in groups:
        value = owned(group)
        height = value.shape[0]
        grads_out[row : row + height, :] = (
            jnp.where(low, value[:, :quarter], value[:, quarter:]) + came[row : row + height]
        )
        row += height
    for at in range(HEAD):
        dx_copy(at).wait()


def fast_call(tokens, cot, lengths, residues, proj_in, proj_out, conv_own, vectors):
    _, rows, half = tokens.shape
    model = 2 * half
    inner = 2 * proj_in.shape[1]
    part_in = proj_in.shape[0]
    part_conv = conv_own.shape[1]
    f32, bf16 = jnp.float32, jnp.bfloat16
    tall = KERNEL_TAPS * part_conv + CONV_PAD
    any_spec = pl.BlockSpec(memory_space=pl.ANY)
    vmem_spec = pl.BlockSpec(memory_space=pltpu.VMEM)
    total = 2 * part_in + tall
    wanted = half // 2 + 64
    packed = (total + 31) // 32 * 16

    def sums(height):
        return [pltpu.VMEM((8, height, inner), f32), pltpu.VMEM((8, height, inner), bf16)] + [
            pltpu.VMEM((length, height, inner), bf16) for length in (8, 4, 2, 1)
        ]

    def sems(count):
        return pltpu.SemaphoreType.DMA((2, count))

    shapes = [
        ((rows, half), bf16),
        ((rows, half), bf16),
        ((rows, half), f32),
        ((rows, half), bf16),
        ((rows - (HEAD + 1) * BLOCK, half), bf16),
        ((BLOCK, half), bf16),
        ((total, half // 2), f32),
        ((1, 3 * half + 6 * wanted), f32),
        ((rows, half), bf16),
        ((2, 2, 2, 2, tall, inner), bf16),
        ((rows, model), f32),
        ((rows, inner), f32),
        ((rows, inner), f32),
        ((rows, inner), f32),
        ((rows, inner), f32),
    ]
    flops = 6 * rows * (2 * model * inner + KERNEL_TAPS * inner * inner)
    results = pl.pallas_call(
        fast_kernel,
        out_shape=[jax.ShapeDtypeStruct(shape, dtype) for shape, dtype in shapes],
        in_specs=[any_spec] * 2 + [vmem_spec] * 14,
        out_specs=[any_spec] * 6 + [vmem_spec] * 2 + [any_spec] * 7,
        scratch_shapes=[
            pltpu.VMEM((rows, 8), bf16),
            pltpu.VMEM((1, 3 * half + 6 * wanted), f32),
            pltpu.VMEM((1, 3 * half + 6 * wanted), f32),
            pltpu.VMEM((8, model), f32),
            pltpu.VMEM((8, inner), f32),
            pltpu.VMEM((2, 2, tall, inner), bf16),
            pltpu.VMEM((rows, model), bf16),
            pltpu.VMEM((rows + 2 * HALO, inner), bf16),
            pltpu.VMEM((rows, inner), bf16),
            pltpu.VMEM((2, rows, half), bf16),
            pltpu.VMEM((rows + 2 * HALO, inner), bf16),
            pltpu.VMEM((rows, half), bf16),
            pltpu.VMEM((2, 2, 2, 2, part_in, inner), bf16),
            pltpu.VMEM((2, 2, 2, 2, part_in, inner), bf16),
            pltpu.VMEM((KERNEL_TAPS, inner, inner), bf16),
        ]
        + sums(part_in) * 4
        + sums(tall - 2 * part_in)
        + [
            pltpu.VMEM((16, inner), f32),
            pltpu.VMEM((packed, inner), bf16),
            pltpu.VMEM((packed, inner), bf16),
            pltpu.VMEM((5, 16, inner), f32),
            pltpu.VMEM((5, 16, inner), f32),
            pltpu.SemaphoreType.DMA((3,)),
            sems(2),
            sems(CHUNKS + 1),
            sems(4),
            sems(4),
            sems(4),
            sems(CHUNKS),
            sems(rows // BLOCK),
            sems(HEAD),
            sems(2),
            sems(2),
            sems(4),
            sems(4),
            sems(4),
            sems(4),
            sems(4),
            sems(1),
            sems(5),
        ],
        compiler_params=pltpu.CompilerParams(
            collective_id=0, has_side_effects=True, vmem_limit_bytes=65280 * 2**10
        ),
        cost_estimate=pl.CostEstimate(flops=flops, bytes_accessed=120 * 2**20, transcendentals=0),
    )(tokens, cot, lengths, residues, proj_in, proj_out, conv_own, *vectors)
    return results[:8]


def finish_kernel(side_ref, tail_ref, cot_ref, whole_ref, out_ref):
    at = pl.ds(pl.multiple_of(pl.program_id(0) * BLOCK, BLOCK), BLOCK)
    out_ref[0] = tail_ref[at, :].astype(jnp.float32) + cot_ref[0].astype(jnp.float32)


def assemble_kernel(side_ref, out_own, out_back, dx_own, dx_back, cot, block_out, grad_tokens):
    side = side_ref[0]
    block_out[side] = out_own[...]
    block_out[1 - side] = out_back[...]
    grad_tokens[side] = dx_own[...]
    grad_tokens[1 - side] = dx_back[...].astype(jnp.float32) + cot[0].astype(jnp.float32)


def assemble_call(side, out_own, out_back, dx_own, dx_back, cot):
    rows, half = out_own.shape
    tile = 2 * BLOCK
    by_tile = pl.BlockSpec((tile, half), lambda i, side_ref: (i, 0))
    pair = pl.BlockSpec((2, tile, half), lambda i, side_ref: (0, i, 0))
    return pl.pallas_call(
        assemble_kernel,
        grid_spec=pltpu.PrefetchScalarGridSpec(
            num_scalar_prefetch=1,
            grid=(rows // tile,),
            in_specs=[by_tile] * 4
            + [pl.BlockSpec((1, tile, half), lambda i, side_ref: (1 - side_ref[0], i, 0))],
            out_specs=[pair, pair],
        ),
        out_shape=[
            jax.ShapeDtypeStruct((2, rows, half), jnp.bfloat16),
            jax.ShapeDtypeStruct((2, rows, half), jnp.float32),
        ],
        compiler_params=pltpu.CompilerParams(
            dimension_semantics=("arbitrary",), vmem_limit_bytes=56 * 2**20
        ),
        cost_estimate=pl.CostEstimate(flops=rows * half, bytes_accessed=24 * rows * half, transcendentals=0),
    )(side, out_own, out_back, dx_own, dx_back, cot)


def finish_call(side, tail, cot, grad_tokens, first):
    half = tail.shape[1]

    def theirs(i, side_ref):
        return (1 - side_ref[0], first + i, 0)

    return pl.pallas_call(
        finish_kernel,
        grid_spec=pltpu.PrefetchScalarGridSpec(
            num_scalar_prefetch=1,
            grid=(tail.shape[0] // BLOCK,),
            in_specs=[
                pl.BlockSpec(memory_space=pltpu.VMEM),
                pl.BlockSpec((1, BLOCK, half), theirs),
                pl.BlockSpec(memory_space=pl.ANY),
            ],
            out_specs=pl.BlockSpec((1, BLOCK, half), theirs),
        ),
        out_shape=jax.ShapeDtypeStruct(grad_tokens.shape, grad_tokens.dtype),
        input_output_aliases={3: 0},
        compiler_params=pltpu.CompilerParams(
            dimension_semantics=("arbitrary",), vmem_limit_bytes=63 * 2**20
        ),
        cost_estimate=pl.CostEstimate(flops=tail.size, bytes_accessed=8 * tail.size, transcendentals=0),
    )(side, tail, cot, grad_tokens)


def fast_body(
    tokens,
    cotangent,
    seq_lengths,
    residue_mask,
    first_gain,
    first_shift,
    proj_in,
    in_bias,
    mid_gain,
    mid_shift,
    conv_weight,
    conv_bias,
    last_gain,
    last_shift,
    proj_out,
    out_bias,
):
    micro, rows, half = tokens.shape
    inner_half = in_bias.shape[0]
    side = lax.axis_index("ch")

    def swap(value):
        return lax.ppermute(value, "ch", SWAP)

    part_in = proj_in.shape[0]
    part_conv = conv_weight.shape[1]
    vectors = (
        first_gain, first_shift, out_bias, in_bias, mid_gain, mid_shift, conv_bias, last_gain, last_shift
    )
    out_own, out_back, dx_own, dx_back, dx_tail, dx_end, grads, sums = fast_call(
        tokens, cotangent, seq_lengths, residue_mask, proj_in, proj_out.T, conv_weight, vectors
    )
    conv_part = grads[2 * part_in : 2 * part_in + KERNEL_TAPS * part_conv]

    side_array = side.astype(jnp.int32).reshape(1)
    tail_back = swap(dx_tail)
    block_out, grad_tokens = assemble_call(side_array, out_own, out_back, dx_own, dx_back, cotangent)
    dx_end, grad_tokens = lax.optimization_barrier((dx_end, grad_tokens))
    end_back = swap(dx_end)
    grad_tokens = finish_call(side_array, tail_back, cotangent, grad_tokens, HEAD)
    grad_tokens = finish_call(side_array, end_back, cotangent, grad_tokens, rows // BLOCK - 1)
    wanted = inner_half + 64

    def narrow_part(index):
        at = 3 * half + index * wanted
        return sums[0, at : at + inner_half]

    return (
        block_out,
        grad_tokens,
        sums[0, :half],
        sums[0, half : 2 * half],
        grads[:part_in],
        narrow_part(0),
        narrow_part(1),
        narrow_part(2),
        conv_part.reshape(KERNEL_TAPS, part_conv, inner_half),
        narrow_part(3),
        narrow_part(4),
        narrow_part(5),
        grads[part_in : 2 * part_in].T,
        sums[0, 2 * half : 3 * half],
    )


def solution(mesh):
    placed = (
        P(None, "seq", "ch"),
        P(None, "seq", "ch"),
        P(),
        P(None, "seq"),
        P("ch"),
        P("ch"),
        P("seq", "ch"),
        P("ch"),
        P("ch"),
        P("ch"),
        P(None, "seq", "ch"),
        P("ch"),
        P("ch"),
        P("ch"),
        P("ch", "seq"),
        P("ch"),
    )
    run = fast_body if mesh.shape["seq"] == 16 else body
    return jax.shard_map(
        run,
        mesh=mesh,
        in_specs=placed,
        out_specs=(
            P(None, "seq", "ch"),
            P(None, "seq", "ch"),
            P("ch"),
            P("ch"),
            P("seq", "ch"),
            P("ch"),
            P("ch"),
            P("ch"),
            P(None, "seq", "ch"),
            P("ch"),
            P("ch"),
            P("ch"),
            P("ch", "seq"),
            P("ch"),
        ),
        check_vma=False,
    )
```

```python
import jax
import jax.numpy as jnp
from jax import lax
from jax.experimental import pallas as pl
from jax.experimental.pallas import tpu as pltpu
from jax.sharding import PartitionSpec as P

KERNEL_TAPS = 5
DILATION_STEP = 32
HALO = 64

EPSILON = 1e-05
ROOT_HALF = 0.7071067811865476
ROOT_TAU = 0.3989422804014327
SWAP = [(0, 1), (1, 0)]


def gelu_both(value):
    half = 0.5 * (1.0 + lax.erf(value * ROOT_HALF))
    return value * half, half + value * jnp.exp(-0.5 * value * value) * ROOT_TAU


def norm(value):
    middle = jnp.mean(value, axis=1, keepdims=True)
    centred = value - middle
    scale = lax.rsqrt(jnp.mean(centred * centred, axis=1, keepdims=True) + EPSILON)
    return centred * scale, scale


def norm_back(grad_zed, normed, scale, gain):
    grad_normed = grad_zed * gain
    first = jnp.mean(grad_normed, axis=1, keepdims=True)
    second = jnp.mean(grad_normed * normed, axis=1, keepdims=True)
    return scale * (grad_normed - first - normed * second)


def dot(left, right, over=((1,), (0,))):
    return lax.dot_general(left, right, (over, ((), ())), preferred_element_type=jnp.float32)


def column_sums(value):
    return jnp.sum(value, axis=0, keepdims=True)


def ordered(side, own, other):
    low = side == 0
    own, other = own.astype(jnp.float32), other.astype(jnp.float32)
    return jnp.where(low, own, other), jnp.where(low, other, own)


def windowed(framed_ref, taps, base, count):
    return jnp.concatenate(
        [
            framed_ref[pl.ds(base + tap * DILATION_STEP, count), :] * taps[:, tap : tap + 1]
            for tap in range(KERNEL_TAPS)
        ],
        axis=1,
    )


def first_kernel(side_ref, own_ref, other_ref, keep_ref, weight_ref, wide_ref, narrow_ref, a1_ref, s1_ref, h1_ref, a2_ref, s2_ref):
    x = jnp.concatenate(ordered(side_ref[0], own_ref[...], other_ref[...]), axis=1)
    normed, _ = norm(x)
    act, slope = gelu_both(normed * wide_ref[0:1, :] + wide_ref[1:2, :])
    act = act.astype(jnp.bfloat16)
    a1_ref[...] = act
    s1_ref[...] = slope
    h1 = dot(act, weight_ref[...]) + narrow_ref[0:1, :]
    h1_ref[...] = h1
    normed, _ = norm(h1)
    act, slope = gelu_both(normed * narrow_ref[1:2, :] + narrow_ref[2:3, :])
    keep = keep_ref[...]
    a2_ref[...] = (act * keep).astype(jnp.bfloat16)
    s2_ref[...] = slope * keep


def second_kernel(side_ref, own_ref, other_ref, taps_ref, framed_ref, conv_ref, weight_ref, wide_ref, narrow_ref, h3_ref, a3_ref, s3_ref, out_own_ref, out_other_ref):
    count = own_ref.shape[0]
    half = own_ref.shape[1]
    base = pl.multiple_of(pl.program_id(0) * count, count)
    h3 = dot(windowed(framed_ref, taps_ref[...], base, count), conv_ref[...]) + narrow_ref[3:4, :]
    h3_ref[...] = h3
    normed, _ = norm(h3)
    act, slope = gelu_both(normed * narrow_ref[4:5, :] + narrow_ref[5:6, :])
    act = act.astype(jnp.bfloat16)
    a3_ref[...] = act
    s3_ref[...] = slope
    mixed = dot(act, weight_ref[...], ((1,), (1,))) + wide_ref[2:3, :]
    left, right = mixed[:, :half], mixed[:, half:]
    low = side_ref[0] == 0
    out_own_ref[...] = (own_ref[...].astype(jnp.float32) + jnp.where(low, left, right)).astype(jnp.bfloat16)
    out_other_ref[...] = (other_ref[...].astype(jnp.float32) + jnp.where(low, right, left)).astype(jnp.bfloat16)


def third_kernel(side_ref, own_ref, other_ref, h3_ref, s3_ref, weight_ref, narrow_ref, dh3_ref, gy_ref, wide_sum_ref, sum_ref):
    @pl.when(pl.program_id(0) == 0)
    def _():
        wide_sum_ref[...] = jnp.zeros_like(wide_sum_ref)
        sum_ref[...] = jnp.zeros_like(sum_ref)

    gy = jnp.concatenate(ordered(side_ref[0], own_ref[...], other_ref[...]), axis=1)
    wide_sum_ref[0:1, :] += column_sums(gy)
    gy = gy.astype(jnp.bfloat16)
    gy_ref[...] = gy
    dz3 = dot(gy, weight_ref[...]) * s3_ref[...]
    normed, scale = norm(h3_ref[...])
    dh3 = norm_back(dz3, normed, scale, narrow_ref[4:5, :]).astype(jnp.bfloat16)
    dh3_ref[...] = dh3
    sum_ref[0:1, :] += column_sums(dh3.astype(jnp.float32))
    sum_ref[1:2, :] += column_sums(dz3 * normed)
    sum_ref[2:3, :] += column_sums(dz3)


def fourth_kernel(side_ref, own_ref, other_ref, gy_own_ref, taps_ref, framed_ref, conv_ref, h1_ref, s2_ref, s1_ref, weight_ref, wide_ref, narrow_ref, dh1_ref, dx_own_ref, dx_other_ref, wide_sum_ref, sum_ref):
    @pl.when(pl.program_id(0) == 0)
    def _():
        wide_sum_ref[...] = jnp.zeros_like(wide_sum_ref)
        sum_ref[...] = jnp.zeros_like(sum_ref)

    count = own_ref.shape[0]
    half = own_ref.shape[1]
    base = pl.multiple_of(pl.program_id(0) * count, count)
    dz2 = dot(windowed(framed_ref, taps_ref[...], base, count), conv_ref[...]) * s2_ref[...]
    normed, scale = norm(h1_ref[...])
    dh1 = norm_back(dz2, normed, scale, narrow_ref[1:2, :]).astype(jnp.bfloat16)
    dh1_ref[...] = dh1
    sum_ref[0:1, :] += column_sums(dh1.astype(jnp.float32))
    sum_ref[1:2, :] += column_sums(dz2 * normed)
    sum_ref[2:3, :] += column_sums(dz2)
    dz1 = dot(dh1, weight_ref[...], ((1,), (1,))) * s1_ref[...]
    x = jnp.concatenate(ordered(side_ref[0], own_ref[...], other_ref[...]), axis=1)
    normed, scale = norm(x)
    dx = norm_back(dz1, normed, scale, wide_ref[0:1, :])
    wide_sum_ref[0:1, :] += column_sums(dz1 * normed)
    wide_sum_ref[1:2, :] += column_sums(dz1)
    low = side_ref[0] == 0
    left, right = dx[:, :half], dx[:, half:]
    dx_own_ref[...] = jnp.where(low, left, right) + gy_own_ref[...].astype(jnp.float32)
    dx_other_ref[...] = jnp.where(low, right, left).astype(jnp.bfloat16)


def grad_kernel(left_ref, right_ref, out_ref):
    out_ref[...] = dot(left_ref[...], right_ref[...], ((0,), (0,)))


def conv_grad_kernel(framed_ref, taps_ref, right_ref, out_ref):
    tap = pl.program_id(0)
    count = right_ref.shape[0]
    base = pl.multiple_of(tap * DILATION_STEP, DILATION_STEP)
    left = framed_ref[pl.ds(base, count), :] * taps_ref[0]
    out_ref[0] = dot(left, right_ref[...], ((0,), (0,)))


VMEM_LIMIT = 56 * 2**20


def once(shape):
    return pl.BlockSpec(shape, lambda *_: (0,) * len(shape), pipeline_mode=pl.Buffered(1))


def by_rows(count, width):
    return pl.BlockSpec((count, width), lambda i, *_: (i, 0))


def row_call(kernel, side, rows, count, operands, outs, flops):
    in_specs = [by_rows(count, a.shape[1]) if how == "rows" else once(a.shape) for a, how in operands]
    out_specs = [
        by_rows(count, width) if how == "rows" else pl.BlockSpec((8, width), lambda i, *_: (0, 0))
        for width, _, how in outs
    ]
    out_shape = [
        jax.ShapeDtypeStruct((rows if how == "rows" else 8, width), dtype) for width, dtype, how in outs
    ]
    moved = sum(a.size * a.dtype.itemsize for a, _ in operands)
    moved += sum(o.size * o.dtype.itemsize for o in out_shape)
    return pl.pallas_call(
        kernel,
        grid_spec=pltpu.PrefetchScalarGridSpec(
            num_scalar_prefetch=1, grid=(rows // count,), in_specs=in_specs, out_specs=out_specs
        ),
        out_shape=out_shape,
        compiler_params=pltpu.CompilerParams(
            dimension_semantics=("arbitrary",), vmem_limit_bytes=VMEM_LIMIT
        ),
        cost_estimate=pl.CostEstimate(flops=flops // 32, bytes_accessed=moved // 32, transcendentals=0),
    )(side, *[a for a, _ in operands])


def matrix_grad(left, right, tiles):
    rows, height = left.shape
    width = right.shape[1]
    return pl.pallas_call(
        grad_kernel,
        grid=(tiles,),
        in_specs=[pl.BlockSpec((rows, height // tiles), lambda i: (0, i)), once((rows, width))],
        out_specs=pl.BlockSpec((height // tiles, width), lambda i: (i, 0)),
        out_shape=jax.ShapeDtypeStruct((height, width), jnp.float32),
        compiler_params=pltpu.CompilerParams(
            dimension_semantics=("arbitrary",), vmem_limit_bytes=VMEM_LIMIT
        ),
        cost_estimate=pl.CostEstimate(
            flops=rows * height * width // 16, bytes_accessed=rows * (height + width) // 16, transcendentals=0
        ),
    )(left, right)


def conv_grad(framed_rows, taps, right):
    rows, width = right.shape
    return pl.pallas_call(
        conv_grad_kernel,
        grid=(KERNEL_TAPS,),
        in_specs=[
            once(framed_rows.shape),
            pl.BlockSpec((1, rows, 1), lambda i: (i, 0, 0)),
            once((rows, width)),
        ],
        out_specs=pl.BlockSpec((1, width, width), lambda i: (i, 0, 0)),
        out_shape=jax.ShapeDtypeStruct((KERNEL_TAPS, width, width), jnp.float32),
        compiler_params=pltpu.CompilerParams(
            dimension_semantics=("arbitrary",), vmem_limit_bytes=VMEM_LIMIT
        ),
        cost_estimate=pl.CostEstimate(
            flops=KERNEL_TAPS * rows * width * width // 16, bytes_accessed=rows * width // 8, transcendentals=0
        ),
    )(framed_rows, taps, right)


def framed(block, width):
    count = lax.axis_size("seq")
    forward = [(i, i + 1) for i in range(count - 1)]
    backward = [(i + 1, i) for i in range(count - 1)]
    low = lax.ppermute(block[block.shape[0] - width :], "seq", forward)
    high = lax.ppermute(block[:width], "seq", backward)
    return jnp.concatenate([low, block, high], axis=0)


def scattered(value, order):
    count = lax.axis_size("seq")
    place = lax.axis_index("seq")
    bits = count.bit_length() - 1
    value = value.reshape((2,) * bits + value.shape[1:])
    left = list(range(bits))
    for bit in order:
        dim = left.index(bits - 1 - bit)
        left.remove(bits - 1 - bit)
        mine = (place >> bit) & 1
        keep = lax.dynamic_index_in_dim(value, mine, dim, keepdims=False)
        send = lax.dynamic_index_in_dim(value, 1 - mine, dim, keepdims=False).astype(jnp.bfloat16)
        came = lax.ppermute(send, "seq", [(i, i ^ (1 << bit)) for i in range(count)])
        value = keep + came.astype(jnp.float32)
    return value


def body(
    tokens,
    cotangent,
    seq_lengths,
    residue_mask,
    first_gain,
    first_shift,
    proj_in,
    in_bias,
    mid_gain,
    mid_shift,
    conv_weight,
    conv_bias,
    last_gain,
    last_shift,
    proj_out,
    out_bias,
):
    micro, rows, half = tokens.shape
    inner_half = in_bias.shape[0]
    inner = 2 * inner_half
    model = 2 * half
    seq_count = lax.axis_size("seq")
    count = 256
    side = lax.axis_index("ch")
    side_array = side.astype(jnp.int32).reshape(1)
    low_side = side == 0

    def swap(value):
        return lax.ppermute(value, "ch", SWAP)

    def whole(own, other, axis):
        return jnp.where(
            low_side,
            jnp.concatenate([own, other], axis=axis),
            jnp.concatenate([other, own], axis=axis),
        )

    def own_of(value):
        return lax.dynamic_index_in_dim(value, side, 0, keepdims=False)

    def other_of(value):
        return lax.dynamic_index_in_dim(value, 1 - side, 0, keepdims=False)

    own_vectors = jnp.concatenate(
        [first_gain, first_shift, out_bias, in_bias, mid_gain, mid_shift, conv_bias, last_gain, last_shift]
    )
    part_in = proj_in.shape[0]
    part_conv = conv_weight.shape[1]
    own_weights = jnp.concatenate(
        [proj_in, proj_out.T, conv_weight.reshape(KERNEL_TAPS * part_conv, inner_half)], axis=0
    )
    own_vectors, own_weights = lax.optimization_barrier((own_vectors, own_weights))
    other_vectors, other_weights = swap(own_vectors), swap(own_weights)
    tokens_tied, other_vectors, other_weights = lax.optimization_barrier(
        (other_of(tokens), other_vectors, other_weights)
    )
    both = whole(own_weights, other_weights, 1)
    vectors = jnp.where(
        low_side, jnp.stack([own_vectors, other_vectors]), jnp.stack([other_vectors, own_vectors])
    )
    x_own = own_of(tokens)
    x_other = swap(tokens_tied)
    gy_own = own_of(cotangent)
    gy_tied, _ = lax.optimization_barrier((other_of(cotangent), x_other))
    gy_other = swap(gy_tied)

    gathered = lax.all_gather(both, "seq", axis=0)
    weight_in = gathered[:, :part_in].reshape(model, inner)
    weight_out = gathered[:, part_in : 2 * part_in].reshape(model, inner)
    weight_conv = (
        gathered[:, 2 * part_in :]
        .reshape(seq_count, KERNEL_TAPS, part_conv, inner)
        .transpose(1, 0, 2, 3)
        .reshape(KERNEL_TAPS, inner, inner)
    )
    wide = jnp.stack([vectors[:, i * half : (i + 1) * half].reshape(-1) for i in range(3)])
    narrow = jnp.stack(
        [
            vectors[:, 3 * half + i * inner_half : 3 * half + (i + 1) * inner_half].reshape(-1)
            for i in range(6)
        ]
    )

    places = lax.axis_index("seq") * rows + jnp.arange(rows + 2 * HALO, dtype=jnp.int32) - HALO
    inside = (places >= 0) & (places < rows * seq_count)
    bounds = jnp.cumsum(own_of(seq_lengths))[:-1]
    segment = jnp.sum((places[:, None] >= bounds[None, :]).astype(jnp.int32), axis=1)
    segment = jnp.where(inside, segment, -1)
    middle = segment[HALO : HALO + rows]
    tap_list = [
        (segment[tap * DILATION_STEP : tap * DILATION_STEP + rows] == middle).astype(jnp.bfloat16)
        for tap in range(KERNEL_TAPS)
    ]
    taps = jnp.stack(tap_list, axis=1)
    keep = own_of(residue_mask).astype(jnp.float32)[:, None]
    f32, bf16 = jnp.float32, jnp.bfloat16
    product = 2 * rows * model * inner

    a1, s1, h1, a2, s2 = row_call(
        first_kernel,
        side_array,
        rows,
        count,
        [(x_own, "rows"), (x_other, "rows"), (keep, "rows"), (weight_in, "once"), (wide, "once"), (narrow, "once")],
        [(model, bf16, "rows"), (model, f32, "rows"), (inner, f32, "rows"), (inner, bf16, "rows"), (inner, f32, "rows")],
        product,
    )
    a2 = framed(a2, HALO)
    h3, a3, s3, out_own, out_other = row_call(
        second_kernel,
        side_array,
        rows,
        count,
        [
            (x_own, "rows"),
            (x_other, "rows"),
            (taps, "rows"),
            (a2, "once"),
            (weight_conv.reshape(KERNEL_TAPS * inner, inner), "once"),
            (weight_out, "once"),
            (wide, "once"),
            (narrow, "once"),
        ],
        [(inner, f32, "rows"), (inner, bf16, "rows"), (inner, f32, "rows"), (half, bf16, "rows"), (half, bf16, "rows")],
        4 * product,
    )
    out_back = swap(out_other)

    dh3, gy, wide_sum_3, sum_3 = row_call(
        third_kernel,
        side_array,
        rows,
        count,
        [(gy_own, "rows"), (gy_other, "rows"), (h3, "rows"), (s3, "rows"), (weight_out, "once"), (narrow, "once")],
        [(inner, bf16, "rows"), (model, bf16, "rows"), (model, f32, "sum"), (inner, f32, "sum")],
        product,
    )
    dh3_framed = framed(dh3, HALO)
    grad_out = matrix_grad(gy, a3, 2)
    grad_conv = conv_grad(a2, jnp.stack(tap_list, axis=0)[:, :, None], dh3)
    dh3_framed, out_back = lax.optimization_barrier((dh3_framed, out_back))
    flipped = jnp.flip(weight_conv, 0).transpose(0, 2, 1).reshape(KERNEL_TAPS * inner, inner)
    dh1, dx_own, dx_other, wide_sum_1, sum_1 = row_call(
        fourth_kernel,
        side_array,
        rows,
        count,
        [
            (x_own, "rows"),
            (x_other, "rows"),
            (gy_own, "rows"),
            (taps, "rows"),
            (dh3_framed, "once"),
            (flipped, "once"),
            (h1, "rows"),
            (s2, "rows"),
            (s1, "rows"),
            (weight_in, "once"),
            (wide, "once"),
            (narrow, "once"),
        ],
        [(inner, bf16, "rows"), (half, f32, "rows"), (half, bf16, "rows"), (model, f32, "sum"), (inner, f32, "sum")],
        4 * product,
    )
    dx_back = swap(dx_other)
    grad_in = matrix_grad(a1, dh1, 2)

    def placed(own, back):
        return jnp.where(low_side, jnp.stack([own, back], 0), jnp.stack([back, own], 0))

    block_out = placed(out_own, out_back)
    grad_tokens = placed(
        dx_own, dx_back.astype(f32) + other_of(cotangent).astype(f32)
    )

    bits = list(range(seq_count.bit_length() - 1))
    swapped_bits = [bits[0]] + bits[2:] + [bits[1]]
    part = jnp.concatenate(
        [
            scattered(grad_in.reshape(seq_count, part_in, inner), bits),
            scattered(grad_out.reshape(seq_count, part_in, inner), swapped_bits),
            scattered(
                grad_conv.reshape(KERNEL_TAPS, seq_count, part_conv, inner).transpose(1, 0, 2, 3), bits
            ).reshape(KERNEL_TAPS * part_conv, inner),
        ],
        axis=0,
    )
    left, right = part[:, :inner_half], part[:, inner_half:]
    part_other = swap(jnp.where(low_side, right, left).astype(bf16))
    part = jnp.where(low_side, left, right) + part_other.astype(f32)

    smalls = jnp.concatenate(
        [
            small.reshape(2, -1)
            for small in (wide_sum_1[0], wide_sum_1[1], wide_sum_3[0], sum_1[0], sum_1[1], sum_1[2], sum_3[0], sum_3[1], sum_3[2])
        ],
        axis=1,
    )
    totals = smalls
    for bit in bits:
        totals = totals + lax.ppermute(totals, "seq", [(i, i ^ (1 << bit)) for i in range(seq_count)])
    totals = own_of(totals) + swap(other_of(totals))
    sizes = [half] * 3 + [inner_half] * 6
    parts = []
    at = 0
    for size in sizes:
        parts.append(totals[at : at + size])
        at += size
    return (
        block_out,
        grad_tokens,
        parts[0],
        parts[1],
        part[:part_in],
        parts[3],
        parts[4],
        parts[5],
        part[2 * part_in :].reshape(KERNEL_TAPS, part_conv, inner_half),
        parts[6],
        parts[7],
        parts[8],
        part[part_in : 2 * part_in].T,
        parts[2],
    )


BLOCK = 256
CHUNKS = 4
CONV_PAD = 8
HEAD = 5
LEAD = 128


def fast_kernel(
    tokens, cot, lengths, residues, proj_in, proj_out, conv_own, *rest,
) -> None:
    vectors, refs = rest[:9], rest[9:]
    fast_steps(tokens, cot, lengths, residues, proj_in, proj_out, conv_own, vectors, *refs)


def fast_steps(
    tokens, cot, lengths, residues, proj_in, proj_out, conv_own, vectors,
    out_own, out_back, dx_own, dx_back, dx_tail, dx_end, grads_out, sums_out,
    x_other, g_conv, s1, h1, s2, h3, s3,
    masks, own_vectors, other_vectors, wide, narrow, stage,
    a1v, a2f, a3v, gyv, dh3f, out_send, w_in, w_out, w_conv,
    k_in, s_in, r0_in, r1_in, r2_in, r3_in,
    k_out, s_out, r0_out, r1_out, r2_out, r3_out,
    k_low, s_low, r0_low, r1_low, r2_low, r3_low,
    k_mid, s_mid, r0_mid, r1_mid, r2_mid, r3_mid,
    k_top, s_top, r0_top, r1_top, r2_top, r3_top,
    smalls, cross_send, cross_recv, small_send, small_recv, load_sems,
    swap_sems, token_sems, in_gather, out_gather, conv_gather, gy_sems, out_sems, dx_sems, a2_sems, dh3_sems, in_sems, out_rs_sems, low_sems, mid_sems, top_sems, cross_sems, small_sems,
):
    rows = a1v.shape[0]
    half = tokens.shape[2]
    inner = narrow.shape[1]
    part = rows // CHUNKS
    side = lax.axis_index("ch")
    place = lax.axis_index("seq")
    last = lax.axis_size("seq") - 1
    low = side == 0
    bits = [lax.rem(place // (1 << bit), 2) for bit in range(4)]
    across = {"ch": 1 - side}
    pairs = [{"seq": place + (1 << bit) * (1 - 2 * bits[bit])} for bit in range(4)]
    before = {"seq": lax.rem(place + last, last + 1)}
    after = {"seq": lax.rem(place + 1, last + 1)}

    def remote(src, dst, sems, at, device):
        return pltpu.make_async_remote_copy(
            src_ref=src,
            dst_ref=dst,
            send_sem=sems.at[0, at],
            recv_sem=sems.at[1, at],
            device_id=device,
            device_id_type=pl.DeviceIdType.MESH,
        )

    def block(ref, at):
        return ref.at[pl.ds(pl.multiple_of(at * BLOCK, BLOCK), BLOCK)]


    def gy_copy(at):
        piece = pl.ds(at * part, part)
        return remote(cot.at[1 - side, piece], gyv.at[side, piece], gy_sems, at, across)

    token_part = (rows - LEAD) // CHUNKS

    def token_copy(at):
        piece = pl.ds(pl.multiple_of(LEAD + at * token_part, 16), token_part)
        return remote(tokens.at[1 - side, piece], x_other.at[piece], token_sems, at, across)

    lead = pl.ds(0, LEAD)
    lead_copy = remote(tokens.at[1 - side, lead], x_other.at[lead], token_sems, CHUNKS, across)

    tail_rows = k_top.shape[1]
    own_gy = pltpu.make_async_copy(cot.at[side], gyv.at[side], load_sems.at[0])
    def out_copy(at):
        return remote(block(out_send, at), block(out_back, at), out_sems, at, across)

    def dx_copy(at):
        return remote(block(gyv.at[1 - side], at), block(dx_back, at), dx_sems, at, across)

    def halo_low(framed_rows, sems):
        return remote(framed_rows.at[pl.ds(HALO, HALO)], framed_rows.at[pl.ds(HALO + rows, HALO)], sems, 0, before)

    def halo_high(framed_rows, sems):
        return remote(framed_rows.at[pl.ds(rows, HALO)], framed_rows.at[pl.ds(0, HALO)], sems, 1, after)

    def halo_start(framed_rows, sems):
        @pl.when(place > 0)
        def _():
            halo_low(framed_rows, sems).start()

        @pl.when(place < last)
        def _():
            halo_high(framed_rows, sems).start()

    def halo_wait(framed_rows, sems):
        @pl.when(place > 0)
        def _():
            halo_low(framed_rows, sems).wait_send()
            halo_high(framed_rows, sems).wait_recv()

        @pl.when(place < last)
        def _():
            halo_high(framed_rows, sems).wait_send()
            halo_low(framed_rows, sems).wait_recv()

    blocks = rows // BLOCK
    per = part // BLOCK

    def middle_first(step):
        late = step // (blocks - 2)
        return (step + 1) * (1 - late) + late * (step - (blocks - 2)) * (blocks - 1)

    def in_order(step):
        return step

    def pipeline(step, order, ins, outs, tail=None, count=None):
        def spec(ref):
            return pl.BlockSpec((BLOCK, ref.shape[-1]), lambda i: (order(i), 0))

        out_specs = [spec(r) for r in outs]
        if tail is not None:
            ahead, end = tail
            most = blocks - 2 - HEAD
            outs = outs + [ahead, end]
            out_specs.append(
                pl.BlockSpec((BLOCK, half), lambda i: (jnp.minimum(jnp.maximum(i - HEAD, 0), most), 0))
            )
            out_specs.append(pl.BlockSpec((BLOCK, half), lambda i: (0, 0)))
        pltpu.emit_pipeline(step, grid=(count or blocks,), in_specs=[spec(r) for r in ins], out_specs=out_specs)(*ins, *outs)

    barrier = pltpu.get_barrier_semaphore()
    for device in [across] + pairs + [before, after]:
        pl.semaphore_signal(barrier, inc=1, device_id=device, device_id_type=pl.DeviceIdType.MESH)
    pl.semaphore_wait(barrier, 7)

    lead_copy.start()
    height = inner // 16
    part_in = proj_in.shape[0]
    quarter = half // 2
    wanted = quarter + 64
    packed = cross_send.shape[0]

    def pack(pieces):
        pieces = [piece.astype(jnp.float32) for piece in pieces]
        short = 2 * packed - sum(piece.shape[0] for piece in pieces)
        value = jnp.concatenate(pieces + [jnp.zeros((short, quarter), jnp.float32)], axis=0)
        cross_send[...] = jnp.concatenate([value[:packed], value[packed:]], axis=1).astype(jnp.bfloat16)

    def unpack(ref):
        value = ref[...].astype(jnp.float32)
        return jnp.concatenate([value[:, :quarter], value[:, quarter:]], axis=0)

    pack([proj_in[...], proj_out[...]] + [conv_own[tap] for tap in range(KERNEL_TAPS)])
    own_vectors[...] = jnp.zeros_like(own_vectors)
    at = 0
    for vector in vectors:
        width = vector.shape[0]
        own_vectors[:, at : at + width] = vector[...].reshape(1, width)
        at += width + width % 128
    swaps = [
        remote(cross_send, cross_recv, swap_sems, 0, across),
        remote(own_vectors, other_vectors, swap_sems, 1, across),
    ]
    for swap in swaps:
        swap.start()
    for at in range(CHUNKS):
        token_copy(at).start()
    for at in range(CHUNKS):
        gy_copy(at).start()
    own_gy.start()

    ends = jnp.where(low, lengths[0:1, :], lengths[1:2, :]).astype(jnp.float32)
    count = ends.shape[1]
    upper = lax.broadcasted_iota(jnp.int32, (count, count), 0) <= lax.broadcasted_iota(jnp.int32, (count, count), 1)
    ends = lax.dot_general(
        jnp.broadcast_to(ends, (8, count)),
        upper.astype(jnp.float32),
        (((1,), (0,)), ((), ())),
        precision=lax.Precision.HIGHEST,
        preferred_element_type=jnp.float32,
    )[0:1, :]

    def mask_block(at, _):
        base = pl.multiple_of(at * BLOCK, BLOCK)
        span = BLOCK + 2 * HALO
        spot = lax.broadcasted_iota(jnp.int32, (span, count), 0) + (place * rows + base - HALO)
        inside = (spot >= 0) & (spot < rows * (last + 1))
        reached = jnp.where(ends <= spot.astype(jnp.float32), 1.0, 0.0)
        segment = jnp.sum(jnp.where(inside, reached, -1.0 / count), axis=1, keepdims=True)
        own_segment = segment[HALO : HALO + BLOCK]
        lane = lax.broadcasted_iota(jnp.int32, (BLOCK, 8), 1)
        columns = jnp.zeros((BLOCK, 8), jnp.float32)
        for tap in range(KERNEL_TAPS):
            same = segment[tap * DILATION_STEP : tap * DILATION_STEP + BLOCK] == own_segment
            columns = jnp.where((lane == tap) & same, 1.0, columns)
        kept = residues[:, pl.ds(base, BLOCK)]
        kept = jnp.where(low, kept[0:1, :], kept[1:2, :]).astype(jnp.float32)
        square = (BLOCK, BLOCK)
        diagonal = lax.broadcasted_iota(jnp.int32, square, 0) == lax.broadcasted_iota(jnp.int32, square, 1)
        keep = jnp.sum(jnp.where(diagonal, kept, 0.0), axis=1, keepdims=True)
        columns = jnp.where(lane == KERNEL_TAPS, keep, columns)
        masks[pl.ds(base, BLOCK), :] = columns.astype(jnp.bfloat16)
        return 0

    lax.fori_loop(0, rows // BLOCK, mask_block, 0)
    smalls[...] = jnp.zeros_like(smalls)

    @pl.when(place == 0)
    def _():
        a2f[0:HALO, :] = jnp.zeros((HALO, inner), jnp.bfloat16)
        dh3f[0:HALO, :] = jnp.zeros((HALO, inner), jnp.bfloat16)

    @pl.when(place == last)
    def _():
        a2f[HALO + rows :, :] = jnp.zeros((HALO, inner), jnp.bfloat16)
        dh3f[HALO + rows :, :] = jnp.zeros((HALO, inner), jnp.bfloat16)

    def both(own, other):
        left, right = ordered(side, own, other)
        return jnp.concatenate([left, right], axis=1)

    for swap in swaps:
        swap.wait()
    rows_here = both(unpack(cross_send), unpack(cross_recv)).astype(jnp.bfloat16)
    here = (bits[3], bits[2], bits[1], bits[0])
    w_in[here] = rows_here[:part_in]
    w_out[here] = rows_here[part_in : 2 * part_in]
    stage[0, 0] = rows_here[2 * part_in : 2 * part_in + stage.shape[2]]
    own_conv = pltpu.make_async_copy(stage.at[0, 0], g_conv.at[here], load_sems.at[1])
    own_conv.start()
    for index in range(3):
        lanes = slice(index * half, (index + 1) * half)
        wide[index : index + 1, :] = both(own_vectors[:, lanes], other_vectors[:, lanes])
    for index in range(6):
        lanes = slice(3 * half + index * wanted, 3 * half + index * wanted + quarter)
        narrow[index : index + 1, :] = both(own_vectors[:, lanes], other_vectors[:, lanes])

    def gather_copy(group, level):
        ref, sems, order = group
        every = slice(None)
        at = tuple(every if bit in order[:level] else bits[bit] for bit in (3, 2, 1, 0))
        return remote(ref.at[at], ref.at[at], sems, level, pairs[order[level]])

    in_rows = (w_in, in_gather, (3, 2, 1, 0))
    out_rows = (w_out, out_gather, (1, 3, 2, 0))
    conv_rows = (g_conv, conv_gather, (3, 2, 1, 0))

    def gather_next(group, level):
        gather_copy(group, level).wait()
        if level < 3:
            gather_copy(group, level + 1).start()

    gather_copy(in_rows, 0).start()
    gather_copy(out_rows, 0).start()
    own_conv.wait()
    gather_next(in_rows, 0)
    gather_copy(conv_rows, 0).start()
    gather_next(in_rows, 1)
    gather_next(in_rows, 2)
    gather_next(conv_rows, 0)
    gather_next(out_rows, 0)
    gather_next(in_rows, 3)

    def first_chunk(at, _):
        token_copy(at).wait_recv()

        def first(own, other, s1_block, h1_block, s2_block):
            base = pl.multiple_of((at * per + pl.program_id(0)) * BLOCK, BLOCK)
            x = jnp.concatenate(ordered(side, own[...], other[...]), axis=1)
            normed, _ = norm(x)
            act, slope = gelu_both(normed * wide[0:1, :] + wide[1:2, :])
            act = act.astype(jnp.bfloat16)
            a1v[pl.ds(base, BLOCK), :] = act
            s1_block[...] = slope
            value = dot(act, w_in[...].reshape(2 * half, inner)) + narrow[0:1, :]
            h1_block[...] = value
            normed, _ = norm(value)
            act, slope = gelu_both(normed * narrow[1:2, :] + narrow[2:3, :])
            keep = masks[pl.ds(base, BLOCK), KERNEL_TAPS : KERNEL_TAPS + 1].astype(jnp.float32)
            a2f[pl.ds(HALO + base, BLOCK), :] = (act * keep).astype(jnp.bfloat16)
            s2_block[...] = slope * keep

        pipeline(first, lambda i: at * per + i, [tokens.at[side], x_other], [s1, h1, s2], count=per)
        for level, (group, ready) in enumerate(((conv_rows, 1), (out_rows, 1), (out_rows, 2))):

            @pl.when(at == level)
            def _():
                gather_next(group, ready)

        return 0

    lead_copy.wait_recv()
    lax.fori_loop(0, CHUNKS, first_chunk, 0)
    halo_start(a2f, a2_sems)
    gather_next(conv_rows, 2)
    gather_next(out_rows, 3)
    gather_next(conv_rows, 3)

    def conv_load(pair):
        return pltpu.make_async_copy(g_conv.at[pair // 2, pair % 2], stage, load_sems.at[2])

    def relay(pair, _):
        conv_load(pair).start()
        conv_load(pair).wait()
        for low_bit in range(2):
            even = stage[low_bit, 0].astype(jnp.float32)
            odd = stage[low_bit, 1].astype(jnp.float32)
            at = pl.multiple_of((2 * pair + low_bit) * 2 * height, 2 * height)
            for tap in range(KERNEL_TAPS):
                top = tap * height
                w_conv[tap, pl.ds(at, 2 * height), :] = jnp.concatenate(
                    [even[top : top + height], odd[top : top + height]], axis=0
                ).astype(jnp.bfloat16)

        return 0

    lax.fori_loop(0, 4, relay, 0)

    def second(own, other, h3_block, s3_block, own_block):
        step = pl.program_id(0)
        at = middle_first(step)
        base = pl.multiple_of(at * BLOCK, BLOCK)

        @pl.when(step == blocks - 2)
        def _():
            halo_wait(a2f, a2_sems)

        taps = masks[pl.ds(base, BLOCK), :]
        weight = w_conv[...].reshape(KERNEL_TAPS * inner, inner)
        value = dot(windowed(a2f, taps, base, BLOCK), weight) + narrow[3:4, :]
        h3_block[...] = value
        normed, _ = norm(value)
        act, slope = gelu_both(normed * narrow[4:5, :] + narrow[5:6, :])
        act = act.astype(jnp.bfloat16)
        a3v[pl.ds(base, BLOCK), :] = act
        s3_block[...] = slope
        mixed = dot(act, w_out[...].reshape(2 * half, inner), ((1,), (1,))) + wide[2:3, :]
        left, right = mixed[:, :half], mixed[:, half:]
        own_block[...] = (own[...].astype(jnp.float32) + jnp.where(low, left, right)).astype(jnp.bfloat16)
        out_send[pl.ds(base, BLOCK), :] = (
            other[...].astype(jnp.float32) + jnp.where(low, right, left)
        ).astype(jnp.bfloat16)
        out_copy(at).start()

    pipeline(second, middle_first, [tokens.at[side], x_other], [h3, s3, out_own])

    def add_small(row, value):
        smalls[row : row + 1, :] += value

    def add_wide(row, value):
        smalls[row : row + 1, :] += value[:, :half]
        smalls[row + 1 : row + 2, :] += value[:, half:]

    def third(h3_block, s3_block):
        at = pl.program_id(0)
        base = pl.multiple_of(at * BLOCK, BLOCK)
        for later in range(CHUNKS):

            @pl.when(at == later * per)
            def _():
                gy_copy(later).wait_recv()

        gy = jnp.concatenate([gyv[0, pl.ds(base, BLOCK), :], gyv[1, pl.ds(base, BLOCK), :]], axis=1)
        add_wide(4, column_sums(gy.astype(jnp.float32)))
        dz3 = dot(gy, w_out[...].reshape(2 * half, inner)) * s3_block[...]
        normed, scale = norm(h3_block[...])
        dh3 = norm_back(dz3, normed, scale, narrow[4:5, :]).astype(jnp.bfloat16)
        dh3f[pl.ds(HALO + base, BLOCK), :] = dh3
        add_small(9, column_sums(dh3.astype(jnp.float32)))
        add_small(10, column_sums(dz3 * normed))
        add_small(11, column_sums(dz3))

    own_gy.wait()
    pipeline(third, in_order, [h3, s3], [])
    halo_start(dh3f, dh3_sems)

    def slot(pair, order):
        two = (pair % 4) if order[0] == 1 else (pair % 4) // 2 + 2 * (pair % 2)
        return pair // 4 * 4 + two

    def split(group, at, even, odd):
        keep_ref, send_ref = group[0], group[1]
        mine_first = bits[0] == 0
        keep_ref[at] = jnp.where(mine_first, even, odd)
        send_ref[at] = jnp.where(mine_first, odd, even).astype(jnp.bfloat16)

    def wide_grad(left_of, right_ref, group):
        tall_rows = group[0].shape[1]

        def tile(at, _):
            value = dot(left_of(at), right_ref[...], ((0,), (0,)))
            for pair in range(4):
                top = 2 * pair * tall_rows
                split(
                    group,
                    at * 4 + slot(pair, group[4]),
                    value[top : top + tall_rows],
                    value[top + tall_rows : top + 2 * tall_rows],
                )
            return 0

        lax.fori_loop(0, 2, tile, 0)
        sum_copy(group, 0).start()

    def conv_grad_of(taps, group):
        right = dh3f.at[pl.ds(HALO, rows)]
        values = []
        for tap in taps:
            left = a2f[tap * DILATION_STEP : tap * DILATION_STEP + rows, :] * masks[:, tap : tap + 1]
            values.append(dot(left, right[...], ((0,), (0,))))
        if len(values) == 1:
            tail = [jnp.zeros((CONV_PAD, inner), jnp.float32)]
        else:
            tail = []
        for pair in range(8):
            top = 2 * pair * height
            split(
                group,
                slot(pair, group[4]),
                jnp.concatenate([v[top : top + height] for v in values] + tail, axis=0),
                jnp.concatenate([v[top + height : top + 2 * height] for v in values] + tail, axis=0),
            )
        sum_copy(group, 0).start()

    y_first, z_first = (1, 2, 3), (2, 1, 3)
    in_set = (k_in, s_in, (r0_in, r1_in, r2_in, r3_in), in_sems, y_first)
    out_set = (k_out, s_out, (r0_out, r1_out, r2_out, r3_out), out_rs_sems, z_first)
    low_set = (k_low, s_low, (r0_low, r1_low, r2_low, r3_low), low_sems, y_first)
    mid_set = (k_mid, s_mid, (r0_mid, r1_mid, r2_mid, r3_mid), mid_sems, z_first)
    top_set = (k_top, s_top, (r0_top, r1_top, r2_top, r3_top), top_sems, y_first)
    starts = (0, 0, 4, 6)
    lengths = (8, 4, 2, 1)

    def sum_copy(group, level):
        _, send, received, sems, order = group
        bit = 0 if level == 0 else order[level - 1]
        return remote(
            send.at[pl.ds(starts[level], lengths[level])], received[level], sems, level, pairs[bit]
        )

    def sum_step(group, level):
        keep, send, received, _, order = group
        sum_copy(group, level).wait()
        came = received[level]
        fixed = 0
        for at in range(level):
            fixed = fixed + bits[order[at]] * (1 << at)
        if level == 3:
            keep[fixed] = keep[fixed] + came[0].astype(jnp.float32)
            return
        mine = bits[order[level]]

        def one(item, _):
            other = 2 * item + 1 - mine
            same = 2 * item + mine
            send[starts[level + 1] + item] = (
                keep[other * (1 << level) + fixed] + came[other].astype(jnp.float32)
            ).astype(jnp.bfloat16)
            at = same * (1 << level) + fixed
            keep[at] = keep[at] + came[same].astype(jnp.float32)
            return 0

        lax.fori_loop(0, lengths[level + 1], one, 0)
        sum_copy(group, level + 1).start()

    def at_step(step, when, *steps):
        @pl.when(step == when)
        def _():
            for group, level in steps:
                sum_step(group, level)

    conv_grad_of((0, 1), low_set)
    conv_grad_of((2, 3), mid_set)
    conv_grad_of((4,), top_set)
    wide_grad(lambda at: gyv[at], a3v, out_set)

    def fourth(h1_block, s2_block):
        step = pl.program_id(0)
        base = pl.multiple_of(step * BLOCK, BLOCK)
        taps = masks[pl.ds(base, BLOCK), :]
        da2 = jnp.zeros((BLOCK, inner), jnp.float32)
        for tap in range(KERNEL_TAPS):
            window = dh3f[pl.ds(base + tap * DILATION_STEP, BLOCK), :] * taps[:, tap : tap + 1]
            da2 = da2 + dot(window, w_conv[KERNEL_TAPS - 1 - tap], ((1,), (1,)))
        dz2 = da2 * s2_block[...]
        normed, scale = norm(h1_block[...])
        dh1 = norm_back(dz2, normed, scale, narrow[1:2, :]).astype(jnp.bfloat16)
        a3v[pl.ds(base, BLOCK), :] = dh1
        add_small(6, column_sums(dh1.astype(jnp.float32)))
        add_small(7, column_sums(dz2 * normed))
        add_small(8, column_sums(dz2))
        at_step(step, 0, (low_set, 0), (mid_set, 0), (top_set, 0))
        at_step(step, 1, (out_set, 0))
        at_step(step, 5, (low_set, 1))
        at_step(step, 6, (mid_set, 1))
        at_step(step, 7, (top_set, 1))

    halo_wait(dh3f, dh3_sems)
    pipeline(fourth, in_order, [h1, s2], [])
    wide_grad(lambda at: a1v[:, pl.ds(pl.multiple_of(at * half, 128), half)], a3v, in_set)
    sum_step(out_set, 1)
    sum_step(low_set, 2)

    def fifth(own, other, s1_block, own_block, tail_block, end_block):
        step = pl.program_id(0)
        base = pl.multiple_of(step * BLOCK, BLOCK)
        dh1 = a3v[pl.ds(base, BLOCK), :]
        dz1 = dot(dh1, w_in[...].reshape(2 * half, inner), ((1,), (1,))) * s1_block[...]
        x = jnp.concatenate(ordered(side, own[...], other[...]), axis=1)
        normed, scale = norm(x)
        dx = norm_back(dz1, normed, scale, wide[0:1, :])
        add_wide(0, column_sums(dz1 * normed))
        add_wide(2, column_sums(dz1))
        left, right = dx[:, :half], dx[:, half:]
        own_block[...] = jnp.where(low, left, right) + gyv[side, pl.ds(base, BLOCK), :].astype(jnp.float32)
        sent = jnp.where(low, right, left).astype(jnp.bfloat16)
        gyv[1 - side, pl.ds(base, BLOCK), :] = sent
        end_block[...] = sent

        @pl.when(step < blocks - 1)
        def _():
            tail_block[...] = sent

        @pl.when(step < HEAD - 1)
        def _():
            dx_copy(step).start()

        at_step(step, 0, (mid_set, 2), (in_set, 0))
        at_step(step, 2, (out_set, 2), (top_set, 2))
        at_step(step, 4, (low_set, 3))
        at_step(step, 5, (mid_set, 3))
        at_step(step, 6, (in_set, 1))
        at_step(step, 7, (top_set, 3), (out_set, 3))

    pipeline(fifth, in_order, [tokens.at[side], x_other, s1], [dx_own], (dx_tail, dx_end))


    def small_copy(level):
        device = pairs[level] if level < 4 else across
        return remote(small_send.at[level], small_recv.at[level], small_sems, level, device)

    def small_start(level):
        small_send[level] = smalls[...]
        small_copy(level).start()

    def small_step(level):
        small_copy(level).wait()
        smalls[...] += small_recv[level]

    small_start(0)
    sum_step(in_set, 2)
    small_step(0)
    small_start(1)
    small_step(1)
    small_start(2)
    small_step(2)
    small_start(3)
    sum_step(in_set, 3)
    small_step(3)
    small_start(4)

    def owned(group):
        keep, order = group[0], group[4]
        return keep[bits[order[0]] + 2 * bits[order[1]] + 4 * bits[order[2]]]

    groups = (in_set, out_set, low_set, mid_set, top_set)
    others = []
    for group in groups:
        value = owned(group)
        others.append(jnp.where(low, value[:, quarter:], value[:, :quarter]))
    pack(others)
    for at in range(blocks):
        out_copy(at).wait()
    cross = remote(cross_send, cross_recv, cross_sems, 0, across)
    cross.start()
    dx_copy(HEAD - 1).start()
    lead_copy.wait_send()
    for at in range(CHUNKS):
        token_copy(at).wait_send()
        gy_copy(at).wait_send()
    small_step(4)
    for index in range(3):
        both = smalls[2 * index : 2 * index + 2, :]
        sums_out[:, index * half : (index + 1) * half] = jnp.where(low, both[0:1], both[1:2])
    for index in range(6):
        both = smalls[6 + index : 7 + index, :]
        at = 3 * half + index * wanted
        sums_out[:, at : at + quarter] = jnp.where(low, both[:, :quarter], both[:, quarter:])
    cross.wait()
    came = unpack(cross_recv)
    row = 0
    for group in groups:
        value = owned(group)
        height = value.shape[0]
        grads_out[row : row + height, :] = (
            jnp.where(low, value[:, :quarter], value[:, quarter:]) + came[row : row + height]
        )
        row += height
    for at in range(HEAD):
        dx_copy(at).wait()


def fast_call(tokens, cot, lengths, residues, proj_in, proj_out, conv_own, vectors):
    _, rows, half = tokens.shape
    model = 2 * half
    inner = 2 * proj_in.shape[1]
    part_in = proj_in.shape[0]
    part_conv = conv_own.shape[1]
    f32, bf16 = jnp.float32, jnp.bfloat16
    tall = KERNEL_TAPS * part_conv + CONV_PAD
    any_spec = pl.BlockSpec(memory_space=pl.ANY)
    vmem_spec = pl.BlockSpec(memory_space=pltpu.VMEM)
    total = 2 * part_in + tall
    wanted = half // 2 + 64
    packed = (total + 31) // 32 * 16

    def sums(height):
        return [pltpu.VMEM((8, height, inner), f32), pltpu.VMEM((8, height, inner), bf16)] + [
            pltpu.VMEM((length, height, inner), bf16) for length in (8, 4, 2, 1)
        ]

    def sems(count):
        return pltpu.SemaphoreType.DMA((2, count))

    shapes = [
        ((rows, half), bf16),
        ((rows, half), bf16),
        ((rows, half), f32),
        ((rows, half), bf16),
        ((rows - (HEAD + 1) * BLOCK, half), bf16),
        ((BLOCK, half), bf16),
        ((total, half // 2), f32),
        ((1, 3 * half + 6 * wanted), f32),
        ((rows, half), bf16),
        ((2, 2, 2, 2, tall, inner), bf16),
        ((rows, model), f32),
        ((rows, inner), f32),
        ((rows, inner), f32),
        ((rows, inner), f32),
        ((rows, inner), f32),
    ]
    flops = 6 * rows * (2 * model * inner + KERNEL_TAPS * inner * inner)
    results = pl.pallas_call(
        fast_kernel,
        out_shape=[jax.ShapeDtypeStruct(shape, dtype) for shape, dtype in shapes],
        in_specs=[any_spec] * 2 + [vmem_spec] * 14,
        out_specs=[any_spec] * 6 + [vmem_spec] * 2 + [any_spec] * 7,
        scratch_shapes=[
            pltpu.VMEM((rows, 8), bf16),
            pltpu.VMEM((1, 3 * half + 6 * wanted), f32),
            pltpu.VMEM((1, 3 * half + 6 * wanted), f32),
            pltpu.VMEM((8, model), f32),
            pltpu.VMEM((8, inner), f32),
            pltpu.VMEM((2, 2, tall, inner), bf16),
            pltpu.VMEM((rows, model), bf16),
            pltpu.VMEM((rows + 2 * HALO, inner), bf16),
            pltpu.VMEM((rows, inner), bf16),
            pltpu.VMEM((2, rows, half), bf16),
            pltpu.VMEM((rows + 2 * HALO, inner), bf16),
            pltpu.VMEM((rows, half), bf16),
            pltpu.VMEM((2, 2, 2, 2, part_in, inner), bf16),
            pltpu.VMEM((2, 2, 2, 2, part_in, inner), bf16),
            pltpu.VMEM((KERNEL_TAPS, inner, inner), bf16),
        ]
        + sums(part_in) * 4
        + sums(tall - 2 * part_in)
        + [
            pltpu.VMEM((16, inner), f32),
            pltpu.VMEM((packed, inner), bf16),
            pltpu.VMEM((packed, inner), bf16),
            pltpu.VMEM((5, 16, inner), f32),
            pltpu.VMEM((5, 16, inner), f32),
            pltpu.SemaphoreType.DMA((3,)),
            sems(2),
            sems(CHUNKS + 1),
            sems(4),
            sems(4),
            sems(4),
            sems(CHUNKS),
            sems(rows // BLOCK),
            sems(HEAD),
            sems(2),
            sems(2),
            sems(4),
            sems(4),
            sems(4),
            sems(4),
            sems(4),
            sems(1),
            sems(5),
        ],
        compiler_params=pltpu.CompilerParams(
            collective_id=0, has_side_effects=True, vmem_limit_bytes=65280 * 2**10
        ),
        cost_estimate=pl.CostEstimate(flops=flops, bytes_accessed=120 * 2**20, transcendentals=0),
    )(tokens, cot, lengths, residues, proj_in, proj_out, conv_own, *vectors)
    return results[:8]


def finish_kernel(side_ref, tail_ref, cot_ref, whole_ref, out_ref):
    at = pl.ds(pl.multiple_of(pl.program_id(0) * BLOCK, BLOCK), BLOCK)
    out_ref[0] = tail_ref[at, :].astype(jnp.float32) + cot_ref[0].astype(jnp.float32)


def assemble_kernel(side_ref, out_own, out_back, dx_own, dx_back, cot, block_out, grad_tokens):
    side = side_ref[0]
    block_out[side] = out_own[...]
    block_out[1 - side] = out_back[...]
    grad_tokens[side] = dx_own[...]
    grad_tokens[1 - side] = dx_back[...].astype(jnp.float32) + cot[0].astype(jnp.float32)


def assemble_call(side, out_own, out_back, dx_own, dx_back, cot):
    rows, half = out_own.shape
    tile = 2 * BLOCK
    by_tile = pl.BlockSpec((tile, half), lambda i, side_ref: (i, 0))
    pair = pl.BlockSpec((2, tile, half), lambda i, side_ref: (0, i, 0))
    return pl.pallas_call(
        assemble_kernel,
        grid_spec=pltpu.PrefetchScalarGridSpec(
            num_scalar_prefetch=1,
            grid=(rows // tile,),
            in_specs=[by_tile] * 4
            + [pl.BlockSpec((1, tile, half), lambda i, side_ref: (1 - side_ref[0], i, 0))],
            out_specs=[pair, pair],
        ),
        out_shape=[
            jax.ShapeDtypeStruct((2, rows, half), jnp.bfloat16),
            jax.ShapeDtypeStruct((2, rows, half), jnp.float32),
        ],
        compiler_params=pltpu.CompilerParams(
            dimension_semantics=("arbitrary",), vmem_limit_bytes=56 * 2**20
        ),
        cost_estimate=pl.CostEstimate(flops=rows * half, bytes_accessed=24 * rows * half, transcendentals=0),
    )(side, out_own, out_back, dx_own, dx_back, cot)


def finish_call(side, tail, cot, grad_tokens, first):
    half = tail.shape[1]

    def theirs(i, side_ref):
        return (1 - side_ref[0], first + i, 0)

    return pl.pallas_call(
        finish_kernel,
        grid_spec=pltpu.PrefetchScalarGridSpec(
            num_scalar_prefetch=1,
            grid=(tail.shape[0] // BLOCK,),
            in_specs=[
                pl.BlockSpec(memory_space=pltpu.VMEM),
                pl.BlockSpec((1, BLOCK, half), theirs),
                pl.BlockSpec(memory_space=pl.ANY),
            ],
            out_specs=pl.BlockSpec((1, BLOCK, half), theirs),
        ),
        out_shape=jax.ShapeDtypeStruct(grad_tokens.shape, grad_tokens.dtype),
        input_output_aliases={3: 0},
        compiler_params=pltpu.CompilerParams(
            dimension_semantics=("arbitrary",), vmem_limit_bytes=63 * 2**20
        ),
        cost_estimate=pl.CostEstimate(flops=tail.size, bytes_accessed=8 * tail.size, transcendentals=0),
    )(side, tail, cot, grad_tokens)


def fast_body(
    tokens,
    cotangent,
    seq_lengths,
    residue_mask,
    first_gain,
    first_shift,
    proj_in,
    in_bias,
    mid_gain,
    mid_shift,
    conv_weight,
    conv_bias,
    last_gain,
    last_shift,
    proj_out,
    out_bias,
):
    micro, rows, half = tokens.shape
    inner_half = in_bias.shape[0]
    side = lax.axis_index("ch")

    def swap(value):
        return lax.ppermute(value, "ch", SWAP)

    part_in = proj_in.shape[0]
    part_conv = conv_weight.shape[1]
    vectors = (
        first_gain, first_shift, out_bias, in_bias, mid_gain, mid_shift, conv_bias, last_gain, last_shift
    )
    out_own, out_back, dx_own, dx_back, dx_tail, dx_end, grads, sums = fast_call(
        tokens, cotangent, seq_lengths, residue_mask, proj_in, proj_out.T, conv_weight, vectors
    )
    conv_part = grads[2 * part_in : 2 * part_in + KERNEL_TAPS * part_conv]

    side_array = side.astype(jnp.int32).reshape(1)
    tail_back = swap(dx_tail)
    block_out, grad_tokens = assemble_call(side_array, out_own, out_back, dx_own, dx_back, cotangent)
    dx_end, grad_tokens = lax.optimization_barrier((dx_end, grad_tokens))
    end_back = swap(dx_end)
    grad_tokens = finish_call(side_array, tail_back, cotangent, grad_tokens, HEAD)
    gy_end = lax.dynamic_index_in_dim(cotangent[:, rows - BLOCK :], 1 - side, 0, keepdims=True)
    end = end_back.astype(jnp.float32)[None] + gy_end.astype(jnp.float32)
    grad_tokens = lax.dynamic_update_slice(grad_tokens, end, (1 - side, rows - BLOCK, 0))
    wanted = inner_half + 64

    def narrow_part(index):
        at = 3 * half + index * wanted
        return sums[0, at : at + inner_half]

    return (
        block_out,
        grad_tokens,
        sums[0, :half],
        sums[0, half : 2 * half],
        grads[:part_in],
        narrow_part(0),
        narrow_part(1),
        narrow_part(2),
        conv_part.reshape(KERNEL_TAPS, part_conv, inner_half),
        narrow_part(3),
        narrow_part(4),
        narrow_part(5),
        grads[part_in : 2 * part_in].T,
        sums[0, 2 * half : 3 * half],
    )


def solution(mesh):
    placed = (
        P(None, "seq", "ch"),
        P(None, "seq", "ch"),
        P(),
        P(None, "seq"),
        P("ch"),
        P("ch"),
        P("seq", "ch"),
        P("ch"),
        P("ch"),
        P("ch"),
        P(None, "seq", "ch"),
        P("ch"),
        P("ch"),
        P("ch"),
        P("ch", "seq"),
        P("ch"),
    )
    run = fast_body if mesh.shape["seq"] == 16 else body
    return jax.shard_map(
        run,
        mesh=mesh,
        in_specs=placed,
        out_specs=(
            P(None, "seq", "ch"),
            P(None, "seq", "ch"),
            P("ch"),
            P("ch"),
            P("seq", "ch"),
            P("ch"),
            P("ch"),
            P("ch"),
            P(None, "seq", "ch"),
            P("ch"),
            P("ch"),
            P("ch"),
            P("ch", "seq"),
            P("ch"),
        ),
        check_vma=False,
    )
```

```python
import jax
import jax.numpy as jnp
from jax import lax
from jax.experimental import pallas as pl
from jax.experimental.pallas import tpu as pltpu
from jax.sharding import PartitionSpec as P

KERNEL_TAPS = 5
DILATION_STEP = 32
HALO = 64

EPSILON = 1e-05
ROOT_HALF = 0.7071067811865476
ROOT_TAU = 0.3989422804014327
SWAP = [(0, 1), (1, 0)]


def gelu_both(value):
    half = 0.5 * (1.0 + lax.erf(value * ROOT_HALF))
    return value * half, half + value * jnp.exp(-0.5 * value * value) * ROOT_TAU


def norm(value):
    middle = jnp.mean(value, axis=1, keepdims=True)
    centred = value - middle
    scale = lax.rsqrt(jnp.mean(centred * centred, axis=1, keepdims=True) + EPSILON)
    return centred * scale, scale


def norm_back(grad_zed, normed, scale, gain):
    grad_normed = grad_zed * gain
    first = jnp.mean(grad_normed, axis=1, keepdims=True)
    second = jnp.mean(grad_normed * normed, axis=1, keepdims=True)
    return scale * (grad_normed - first - normed * second)


def dot(left, right, over=((1,), (0,))):
    return lax.dot_general(left, right, (over, ((), ())), preferred_element_type=jnp.float32)


def column_sums(value):
    return jnp.sum(value, axis=0, keepdims=True)


def ordered(side, own, other):
    low = side == 0
    own, other = own.astype(jnp.float32), other.astype(jnp.float32)
    return jnp.where(low, own, other), jnp.where(low, other, own)


def windowed(framed_ref, taps, base, count):
    return jnp.concatenate(
        [
            framed_ref[pl.ds(base + tap * DILATION_STEP, count), :] * taps[:, tap : tap + 1]
            for tap in range(KERNEL_TAPS)
        ],
        axis=1,
    )


def first_kernel(side_ref, own_ref, other_ref, keep_ref, weight_ref, wide_ref, narrow_ref, a1_ref, s1_ref, h1_ref, a2_ref, s2_ref):
    x = jnp.concatenate(ordered(side_ref[0], own_ref[...], other_ref[...]), axis=1)
    normed, _ = norm(x)
    act, slope = gelu_both(normed * wide_ref[0:1, :] + wide_ref[1:2, :])
    act = act.astype(jnp.bfloat16)
    a1_ref[...] = act
    s1_ref[...] = slope
    h1 = dot(act, weight_ref[...]) + narrow_ref[0:1, :]
    h1_ref[...] = h1
    normed, _ = norm(h1)
    act, slope = gelu_both(normed * narrow_ref[1:2, :] + narrow_ref[2:3, :])
    keep = keep_ref[...]
    a2_ref[...] = (act * keep).astype(jnp.bfloat16)
    s2_ref[...] = slope * keep


def second_kernel(side_ref, own_ref, other_ref, taps_ref, framed_ref, conv_ref, weight_ref, wide_ref, narrow_ref, h3_ref, a3_ref, s3_ref, out_own_ref, out_other_ref):
    count = own_ref.shape[0]
    half = own_ref.shape[1]
    base = pl.multiple_of(pl.program_id(0) * count, count)
    h3 = dot(windowed(framed_ref, taps_ref[...], base, count), conv_ref[...]) + narrow_ref[3:4, :]
    h3_ref[...] = h3
    normed, _ = norm(h3)
    act, slope = gelu_both(normed * narrow_ref[4:5, :] + narrow_ref[5:6, :])
    act = act.astype(jnp.bfloat16)
    a3_ref[...] = act
    s3_ref[...] = slope
    mixed = dot(act, weight_ref[...], ((1,), (1,))) + wide_ref[2:3, :]
    left, right = mixed[:, :half], mixed[:, half:]
    low = side_ref[0] == 0
    out_own_ref[...] = (own_ref[...].astype(jnp.float32) + jnp.where(low, left, right)).astype(jnp.bfloat16)
    out_other_ref[...] = (other_ref[...].astype(jnp.float32) + jnp.where(low, right, left)).astype(jnp.bfloat16)


def third_kernel(side_ref, own_ref, other_ref, h3_ref, s3_ref, weight_ref, narrow_ref, dh3_ref, gy_ref, wide_sum_ref, sum_ref):
    @pl.when(pl.program_id(0) == 0)
    def _():
        wide_sum_ref[...] = jnp.zeros_like(wide_sum_ref)
        sum_ref[...] = jnp.zeros_like(sum_ref)

    gy = jnp.concatenate(ordered(side_ref[0], own_ref[...], other_ref[...]), axis=1)
    wide_sum_ref[0:1, :] += column_sums(gy)
    gy = gy.astype(jnp.bfloat16)
    gy_ref[...] = gy
    dz3 = dot(gy, weight_ref[...]) * s3_ref[...]
    normed, scale = norm(h3_ref[...])
    dh3 = norm_back(dz3, normed, scale, narrow_ref[4:5, :]).astype(jnp.bfloat16)
    dh3_ref[...] = dh3
    sum_ref[0:1, :] += column_sums(dh3.astype(jnp.float32))
    sum_ref[1:2, :] += column_sums(dz3 * normed)
    sum_ref[2:3, :] += column_sums(dz3)


def fourth_kernel(side_ref, own_ref, other_ref, gy_own_ref, taps_ref, framed_ref, conv_ref, h1_ref, s2_ref, s1_ref, weight_ref, wide_ref, narrow_ref, dh1_ref, dx_own_ref, dx_other_ref, wide_sum_ref, sum_ref):
    @pl.when(pl.program_id(0) == 0)
    def _():
        wide_sum_ref[...] = jnp.zeros_like(wide_sum_ref)
        sum_ref[...] = jnp.zeros_like(sum_ref)

    count = own_ref.shape[0]
    half = own_ref.shape[1]
    base = pl.multiple_of(pl.program_id(0) * count, count)
    dz2 = dot(windowed(framed_ref, taps_ref[...], base, count), conv_ref[...]) * s2_ref[...]
    normed, scale = norm(h1_ref[...])
    dh1 = norm_back(dz2, normed, scale, narrow_ref[1:2, :]).astype(jnp.bfloat16)
    dh1_ref[...] = dh1
    sum_ref[0:1, :] += column_sums(dh1.astype(jnp.float32))
    sum_ref[1:2, :] += column_sums(dz2 * normed)
    sum_ref[2:3, :] += column_sums(dz2)
    dz1 = dot(dh1, weight_ref[...], ((1,), (1,))) * s1_ref[...]
    x = jnp.concatenate(ordered(side_ref[0], own_ref[...], other_ref[...]), axis=1)
    normed, scale = norm(x)
    dx = norm_back(dz1, normed, scale, wide_ref[0:1, :])
    wide_sum_ref[0:1, :] += column_sums(dz1 * normed)
    wide_sum_ref[1:2, :] += column_sums(dz1)
    low = side_ref[0] == 0
    left, right = dx[:, :half], dx[:, half:]
    dx_own_ref[...] = jnp.where(low, left, right) + gy_own_ref[...].astype(jnp.float32)
    dx_other_ref[...] = jnp.where(low, right, left).astype(jnp.bfloat16)


def grad_kernel(left_ref, right_ref, out_ref):
    out_ref[...] = dot(left_ref[...], right_ref[...], ((0,), (0,)))


def conv_grad_kernel(framed_ref, taps_ref, right_ref, out_ref):
    tap = pl.program_id(0)
    count = right_ref.shape[0]
    base = pl.multiple_of(tap * DILATION_STEP, DILATION_STEP)
    left = framed_ref[pl.ds(base, count), :] * taps_ref[0]
    out_ref[0] = dot(left, right_ref[...], ((0,), (0,)))


VMEM_LIMIT = 56 * 2**20


def once(shape):
    return pl.BlockSpec(shape, lambda *_: (0,) * len(shape), pipeline_mode=pl.Buffered(1))


def by_rows(count, width):
    return pl.BlockSpec((count, width), lambda i, *_: (i, 0))


def row_call(kernel, side, rows, count, operands, outs, flops):
    in_specs = [by_rows(count, a.shape[1]) if how == "rows" else once(a.shape) for a, how in operands]
    out_specs = [
        by_rows(count, width) if how == "rows" else pl.BlockSpec((8, width), lambda i, *_: (0, 0))
        for width, _, how in outs
    ]
    out_shape = [
        jax.ShapeDtypeStruct((rows if how == "rows" else 8, width), dtype) for width, dtype, how in outs
    ]
    moved = sum(a.size * a.dtype.itemsize for a, _ in operands)
    moved += sum(o.size * o.dtype.itemsize for o in out_shape)
    return pl.pallas_call(
        kernel,
        grid_spec=pltpu.PrefetchScalarGridSpec(
            num_scalar_prefetch=1, grid=(rows // count,), in_specs=in_specs, out_specs=out_specs
        ),
        out_shape=out_shape,
        compiler_params=pltpu.CompilerParams(
            dimension_semantics=("arbitrary",), vmem_limit_bytes=VMEM_LIMIT
        ),
        cost_estimate=pl.CostEstimate(flops=flops // 32, bytes_accessed=moved // 32, transcendentals=0),
    )(side, *[a for a, _ in operands])


def matrix_grad(left, right, tiles):
    rows, height = left.shape
    width = right.shape[1]
    return pl.pallas_call(
        grad_kernel,
        grid=(tiles,),
        in_specs=[pl.BlockSpec((rows, height // tiles), lambda i: (0, i)), once((rows, width))],
        out_specs=pl.BlockSpec((height // tiles, width), lambda i: (i, 0)),
        out_shape=jax.ShapeDtypeStruct((height, width), jnp.float32),
        compiler_params=pltpu.CompilerParams(
            dimension_semantics=("arbitrary",), vmem_limit_bytes=VMEM_LIMIT
        ),
        cost_estimate=pl.CostEstimate(
            flops=rows * height * width // 16, bytes_accessed=rows * (height + width) // 16, transcendentals=0
        ),
    )(left, right)


def conv_grad(framed_rows, taps, right):
    rows, width = right.shape
    return pl.pallas_call(
        conv_grad_kernel,
        grid=(KERNEL_TAPS,),
        in_specs=[
            once(framed_rows.shape),
            pl.BlockSpec((1, rows, 1), lambda i: (i, 0, 0)),
            once((rows, width)),
        ],
        out_specs=pl.BlockSpec((1, width, width), lambda i: (i, 0, 0)),
        out_shape=jax.ShapeDtypeStruct((KERNEL_TAPS, width, width), jnp.float32),
        compiler_params=pltpu.CompilerParams(
            dimension_semantics=("arbitrary",), vmem_limit_bytes=VMEM_LIMIT
        ),
        cost_estimate=pl.CostEstimate(
            flops=KERNEL_TAPS * rows * width * width // 16, bytes_accessed=rows * width // 8, transcendentals=0
        ),
    )(framed_rows, taps, right)


def framed(block, width):
    count = lax.axis_size("seq")
    forward = [(i, i + 1) for i in range(count - 1)]
    backward = [(i + 1, i) for i in range(count - 1)]
    low = lax.ppermute(block[block.shape[0] - width :], "seq", forward)
    high = lax.ppermute(block[:width], "seq", backward)
    return jnp.concatenate([low, block, high], axis=0)


def scattered(value, order):
    count = lax.axis_size("seq")
    place = lax.axis_index("seq")
    bits = count.bit_length() - 1
    value = value.reshape((2,) * bits + value.shape[1:])
    left = list(range(bits))
    for bit in order:
        dim = left.index(bits - 1 - bit)
        left.remove(bits - 1 - bit)
        mine = (place >> bit) & 1
        keep = lax.dynamic_index_in_dim(value, mine, dim, keepdims=False)
        send = lax.dynamic_index_in_dim(value, 1 - mine, dim, keepdims=False).astype(jnp.bfloat16)
        came = lax.ppermute(send, "seq", [(i, i ^ (1 << bit)) for i in range(count)])
        value = keep + came.astype(jnp.float32)
    return value


def body(
    tokens,
    cotangent,
    seq_lengths,
    residue_mask,
    first_gain,
    first_shift,
    proj_in,
    in_bias,
    mid_gain,
    mid_shift,
    conv_weight,
    conv_bias,
    last_gain,
    last_shift,
    proj_out,
    out_bias,
):
    micro, rows, half = tokens.shape
    inner_half = in_bias.shape[0]
    inner = 2 * inner_half
    model = 2 * half
    seq_count = lax.axis_size("seq")
    count = 256
    side = lax.axis_index("ch")
    side_array = side.astype(jnp.int32).reshape(1)
    low_side = side == 0

    def swap(value):
        return lax.ppermute(value, "ch", SWAP)

    def whole(own, other, axis):
        return jnp.where(
            low_side,
            jnp.concatenate([own, other], axis=axis),
            jnp.concatenate([other, own], axis=axis),
        )

    def own_of(value):
        return lax.dynamic_index_in_dim(value, side, 0, keepdims=False)

    def other_of(value):
        return lax.dynamic_index_in_dim(value, 1 - side, 0, keepdims=False)

    own_vectors = jnp.concatenate(
        [first_gain, first_shift, out_bias, in_bias, mid_gain, mid_shift, conv_bias, last_gain, last_shift]
    )
    part_in = proj_in.shape[0]
    part_conv = conv_weight.shape[1]
    own_weights = jnp.concatenate(
        [proj_in, proj_out.T, conv_weight.reshape(KERNEL_TAPS * part_conv, inner_half)], axis=0
    )
    own_vectors, own_weights = lax.optimization_barrier((own_vectors, own_weights))
    other_vectors, other_weights = swap(own_vectors), swap(own_weights)
    tokens_tied, other_vectors, other_weights = lax.optimization_barrier(
        (other_of(tokens), other_vectors, other_weights)
    )
    both = whole(own_weights, other_weights, 1)
    vectors = jnp.where(
        low_side, jnp.stack([own_vectors, other_vectors]), jnp.stack([other_vectors, own_vectors])
    )
    x_own = own_of(tokens)
    x_other = swap(tokens_tied)
    gy_own = own_of(cotangent)
    gy_tied, _ = lax.optimization_barrier((other_of(cotangent), x_other))
    gy_other = swap(gy_tied)

    gathered = lax.all_gather(both, "seq", axis=0)
    weight_in = gathered[:, :part_in].reshape(model, inner)
    weight_out = gathered[:, part_in : 2 * part_in].reshape(model, inner)
    weight_conv = (
        gathered[:, 2 * part_in :]
        .reshape(seq_count, KERNEL_TAPS, part_conv, inner)
        .transpose(1, 0, 2, 3)
        .reshape(KERNEL_TAPS, inner, inner)
    )
    wide = jnp.stack([vectors[:, i * half : (i + 1) * half].reshape(-1) for i in range(3)])
    narrow = jnp.stack(
        [
            vectors[:, 3 * half + i * inner_half : 3 * half + (i + 1) * inner_half].reshape(-1)
            for i in range(6)
        ]
    )

    places = lax.axis_index("seq") * rows + jnp.arange(rows + 2 * HALO, dtype=jnp.int32) - HALO
    inside = (places >= 0) & (places < rows * seq_count)
    bounds = jnp.cumsum(own_of(seq_lengths))[:-1]
    segment = jnp.sum((places[:, None] >= bounds[None, :]).astype(jnp.int32), axis=1)
    segment = jnp.where(inside, segment, -1)
    middle = segment[HALO : HALO + rows]
    tap_list = [
        (segment[tap * DILATION_STEP : tap * DILATION_STEP + rows] == middle).astype(jnp.bfloat16)
        for tap in range(KERNEL_TAPS)
    ]
    taps = jnp.stack(tap_list, axis=1)
    keep = own_of(residue_mask).astype(jnp.float32)[:, None]
    f32, bf16 = jnp.float32, jnp.bfloat16
    product = 2 * rows * model * inner

    a1, s1, h1, a2, s2 = row_call(
        first_kernel,
        side_array,
        rows,
        count,
        [(x_own, "rows"), (x_other, "rows"), (keep, "rows"), (weight_in, "once"), (wide, "once"), (narrow, "once")],
        [(model, bf16, "rows"), (model, f32, "rows"), (inner, f32, "rows"), (inner, bf16, "rows"), (inner, f32, "rows")],
        product,
    )
    a2 = framed(a2, HALO)
    h3, a3, s3, out_own, out_other = row_call(
        second_kernel,
        side_array,
        rows,
        count,
        [
            (x_own, "rows"),
            (x_other, "rows"),
            (taps, "rows"),
            (a2, "once"),
            (weight_conv.reshape(KERNEL_TAPS * inner, inner), "once"),
            (weight_out, "once"),
            (wide, "once"),
            (narrow, "once"),
        ],
        [(inner, f32, "rows"), (inner, bf16, "rows"), (inner, f32, "rows"), (half, bf16, "rows"), (half, bf16, "rows")],
        4 * product,
    )
    out_back = swap(out_other)

    dh3, gy, wide_sum_3, sum_3 = row_call(
        third_kernel,
        side_array,
        rows,
        count,
        [(gy_own, "rows"), (gy_other, "rows"), (h3, "rows"), (s3, "rows"), (weight_out, "once"), (narrow, "once")],
        [(inner, bf16, "rows"), (model, bf16, "rows"), (model, f32, "sum"), (inner, f32, "sum")],
        product,
    )
    dh3_framed = framed(dh3, HALO)
    grad_out = matrix_grad(gy, a3, 2)
    grad_conv = conv_grad(a2, jnp.stack(tap_list, axis=0)[:, :, None], dh3)
    dh3_framed, out_back = lax.optimization_barrier((dh3_framed, out_back))
    flipped = jnp.flip(weight_conv, 0).transpose(0, 2, 1).reshape(KERNEL_TAPS * inner, inner)
    dh1, dx_own, dx_other, wide_sum_1, sum_1 = row_call(
        fourth_kernel,
        side_array,
        rows,
        count,
        [
            (x_own, "rows"),
            (x_other, "rows"),
            (gy_own, "rows"),
            (taps, "rows"),
            (dh3_framed, "once"),
            (flipped, "once"),
            (h1, "rows"),
            (s2, "rows"),
            (s1, "rows"),
            (weight_in, "once"),
            (wide, "once"),
            (narrow, "once"),
        ],
        [(inner, bf16, "rows"), (half, f32, "rows"), (half, bf16, "rows"), (model, f32, "sum"), (inner, f32, "sum")],
        4 * product,
    )
    dx_back = swap(dx_other)
    grad_in = matrix_grad(a1, dh1, 2)

    def placed(own, back):
        return jnp.where(low_side, jnp.stack([own, back], 0), jnp.stack([back, own], 0))

    block_out = placed(out_own, out_back)
    grad_tokens = placed(
        dx_own, dx_back.astype(f32) + other_of(cotangent).astype(f32)
    )

    bits = list(range(seq_count.bit_length() - 1))
    swapped_bits = [bits[0]] + bits[2:] + [bits[1]]
    part = jnp.concatenate(
        [
            scattered(grad_in.reshape(seq_count, part_in, inner), bits),
            scattered(grad_out.reshape(seq_count, part_in, inner), swapped_bits),
            scattered(
                grad_conv.reshape(KERNEL_TAPS, seq_count, part_conv, inner).transpose(1, 0, 2, 3), bits
            ).reshape(KERNEL_TAPS * part_conv, inner),
        ],
        axis=0,
    )
    left, right = part[:, :inner_half], part[:, inner_half:]
    part_other = swap(jnp.where(low_side, right, left).astype(bf16))
    part = jnp.where(low_side, left, right) + part_other.astype(f32)

    smalls = jnp.concatenate(
        [
            small.reshape(2, -1)
            for small in (wide_sum_1[0], wide_sum_1[1], wide_sum_3[0], sum_1[0], sum_1[1], sum_1[2], sum_3[0], sum_3[1], sum_3[2])
        ],
        axis=1,
    )
    totals = smalls
    for bit in bits:
        totals = totals + lax.ppermute(totals, "seq", [(i, i ^ (1 << bit)) for i in range(seq_count)])
    totals = own_of(totals) + swap(other_of(totals))
    sizes = [half] * 3 + [inner_half] * 6
    parts = []
    at = 0
    for size in sizes:
        parts.append(totals[at : at + size])
        at += size
    return (
        block_out,
        grad_tokens,
        parts[0],
        parts[1],
        part[:part_in],
        parts[3],
        parts[4],
        parts[5],
        part[2 * part_in :].reshape(KERNEL_TAPS, part_conv, inner_half),
        parts[6],
        parts[7],
        parts[8],
        part[part_in : 2 * part_in].T,
        parts[2],
    )


BLOCK = 256
CHUNKS = 4
CONV_PAD = 8
HEAD = 5
LEAD = 256


def fast_kernel(
    tokens, cot, lengths, residues, proj_in, proj_out, conv_own, *rest,
) -> None:
    vectors, refs = rest[:9], rest[9:]
    fast_steps(tokens, cot, lengths, residues, proj_in, proj_out, conv_own, vectors, *refs)


def fast_steps(
    tokens, cot, lengths, residues, proj_in, proj_out, conv_own, vectors,
    out_own, out_back, dx_own, dx_back, dx_tail, dx_end, grads_out, sums_out,
    x_other, g_conv, s1, h1, s2, h3, s3,
    masks, own_vectors, other_vectors, wide, narrow, stage,
    a1v, a2f, a3v, gyv, dh3f, out_send, w_in, w_out, w_conv,
    k_in, s_in, r0_in, r1_in, r2_in, r3_in,
    k_out, s_out, r0_out, r1_out, r2_out, r3_out,
    k_low, s_low, r0_low, r1_low, r2_low, r3_low,
    k_mid, s_mid, r0_mid, r1_mid, r2_mid, r3_mid,
    k_top, s_top, r0_top, r1_top, r2_top, r3_top,
    smalls, cross_send, cross_recv, small_send, small_recv, load_sems,
    swap_sems, token_sems, in_gather, out_gather, conv_gather, gy_sems, out_sems, dx_sems, a2_sems, dh3_sems, in_sems, out_rs_sems, low_sems, mid_sems, top_sems, cross_sems, small_sems,
):
    rows = a1v.shape[0]
    half = tokens.shape[2]
    inner = narrow.shape[1]
    part = rows // CHUNKS
    side = lax.axis_index("ch")
    place = lax.axis_index("seq")
    last = lax.axis_size("seq") - 1
    low = side == 0
    bits = [lax.rem(place // (1 << bit), 2) for bit in range(4)]
    across = {"ch": 1 - side}
    pairs = [{"seq": place + (1 << bit) * (1 - 2 * bits[bit])} for bit in range(4)]
    before = {"seq": lax.rem(place + last, last + 1)}
    after = {"seq": lax.rem(place + 1, last + 1)}

    def remote(src, dst, sems, at, device):
        return pltpu.make_async_remote_copy(
            src_ref=src,
            dst_ref=dst,
            send_sem=sems.at[0, at],
            recv_sem=sems.at[1, at],
            device_id=device,
            device_id_type=pl.DeviceIdType.MESH,
        )

    def block(ref, at):
        return ref.at[pl.ds(pl.multiple_of(at * BLOCK, BLOCK), BLOCK)]


    def gy_copy(at):
        piece = pl.ds(at * part, part)
        return remote(cot.at[1 - side, piece], gyv.at[side, piece], gy_sems, at, across)

    token_part = (rows - LEAD) // CHUNKS

    def token_copy(at):
        piece = pl.ds(pl.multiple_of(LEAD + at * token_part, 16), token_part)
        return remote(tokens.at[1 - side, piece], x_other.at[piece], token_sems, at, across)

    lead = pl.ds(0, LEAD)
    lead_copy = remote(tokens.at[1 - side, lead], x_other.at[lead], token_sems, CHUNKS, across)

    tail_rows = k_top.shape[1]
    own_gy = pltpu.make_async_copy(cot.at[side], gyv.at[side], load_sems.at[0])
    def out_copy(at):
        return remote(block(out_send, at), block(out_back, at), out_sems, at, across)

    def dx_copy(at):
        return remote(block(gyv.at[1 - side], at), block(dx_back, at), dx_sems, at, across)

    def halo_low(framed_rows, sems):
        return remote(framed_rows.at[pl.ds(HALO, HALO)], framed_rows.at[pl.ds(HALO + rows, HALO)], sems, 0, before)

    def halo_high(framed_rows, sems):
        return remote(framed_rows.at[pl.ds(rows, HALO)], framed_rows.at[pl.ds(0, HALO)], sems, 1, after)

    def halo_start(framed_rows, sems):
        @pl.when(place > 0)
        def _():
            halo_low(framed_rows, sems).start()

        @pl.when(place < last)
        def _():
            halo_high(framed_rows, sems).start()

    def halo_wait(framed_rows, sems):
        @pl.when(place > 0)
        def _():
            halo_low(framed_rows, sems).wait_send()
            halo_high(framed_rows, sems).wait_recv()

        @pl.when(place < last)
        def _():
            halo_high(framed_rows, sems).wait_send()
            halo_low(framed_rows, sems).wait_recv()

    blocks = rows // BLOCK
    per = part // BLOCK

    def middle_first(step):
        late = step // (blocks - 2)
        return (step + 1) * (1 - late) + late * (step - (blocks - 2)) * (blocks - 1)

    def in_order(step):
        return step

    def pipeline(step, order, ins, outs, tail=None, count=None):
        def spec(ref):
            return pl.BlockSpec((BLOCK, ref.shape[-1]), lambda i: (order(i), 0))

        out_specs = [spec(r) for r in outs]
        if tail is not None:
            ahead, end = tail
            most = blocks - 2 - HEAD
            outs = outs + [ahead, end]
            out_specs.append(
                pl.BlockSpec((BLOCK, half), lambda i: (jnp.minimum(jnp.maximum(i - HEAD, 0), most), 0))
            )
            out_specs.append(pl.BlockSpec((BLOCK, half), lambda i: (0, 0)))
        pltpu.emit_pipeline(step, grid=(count or blocks,), in_specs=[spec(r) for r in ins], out_specs=out_specs)(*ins, *outs)

    barrier = pltpu.get_barrier_semaphore()
    for device in [across] + pairs + [before, after]:
        pl.semaphore_signal(barrier, inc=1, device_id=device, device_id_type=pl.DeviceIdType.MESH)
    pl.semaphore_wait(barrier, 7)

    lead_copy.start()
    height = inner // 16
    part_in = proj_in.shape[0]
    quarter = half // 2
    wanted = quarter + 64
    packed = cross_send.shape[0]

    def pack(pieces):
        pieces = [piece.astype(jnp.float32) for piece in pieces]
        short = 2 * packed - sum(piece.shape[0] for piece in pieces)
        value = jnp.concatenate(pieces + [jnp.zeros((short, quarter), jnp.float32)], axis=0)
        cross_send[...] = jnp.concatenate([value[:packed], value[packed:]], axis=1).astype(jnp.bfloat16)

    def unpack(ref):
        value = ref[...].astype(jnp.float32)
        return jnp.concatenate([value[:, :quarter], value[:, quarter:]], axis=0)

    pack([proj_in[...], proj_out[...]] + [conv_own[tap] for tap in range(KERNEL_TAPS)])
    own_vectors[...] = jnp.zeros_like(own_vectors)
    at = 0
    for vector in vectors:
        width = vector.shape[0]
        own_vectors[:, at : at + width] = vector[...].reshape(1, width)
        at += width + width % 128
    swaps = [
        remote(cross_send, cross_recv, swap_sems, 0, across),
        remote(own_vectors, other_vectors, swap_sems, 1, across),
    ]
    for swap in swaps:
        swap.start()
    for at in range(CHUNKS):
        token_copy(at).start()
    for at in range(CHUNKS):
        gy_copy(at).start()
    own_gy.start()

    ends = jnp.where(low, lengths[0:1, :], lengths[1:2, :]).astype(jnp.float32)
    count = ends.shape[1]
    upper = lax.broadcasted_iota(jnp.int32, (count, count), 0) <= lax.broadcasted_iota(jnp.int32, (count, count), 1)
    ends = lax.dot_general(
        jnp.broadcast_to(ends, (8, count)),
        upper.astype(jnp.float32),
        (((1,), (0,)), ((), ())),
        precision=lax.Precision.HIGHEST,
        preferred_element_type=jnp.float32,
    )[0:1, :]

    def mask_block(at, _):
        base = pl.multiple_of(at * BLOCK, BLOCK)
        span = BLOCK + 2 * HALO
        spot = lax.broadcasted_iota(jnp.int32, (span, count), 0) + (place * rows + base - HALO)
        inside = (spot >= 0) & (spot < rows * (last + 1))
        reached = jnp.where(ends <= spot.astype(jnp.float32), 1.0, 0.0)
        segment = jnp.sum(jnp.where(inside, reached, -1.0 / count), axis=1, keepdims=True)
        own_segment = segment[HALO : HALO + BLOCK]
        lane = lax.broadcasted_iota(jnp.int32, (BLOCK, 8), 1)
        columns = jnp.zeros((BLOCK, 8), jnp.float32)
        for tap in range(KERNEL_TAPS):
            same = segment[tap * DILATION_STEP : tap * DILATION_STEP + BLOCK] == own_segment
            columns = jnp.where((lane == tap) & same, 1.0, columns)
        kept = residues[:, pl.ds(base, BLOCK)]
        kept = jnp.where(low, kept[0:1, :], kept[1:2, :]).astype(jnp.float32)
        square = (BLOCK, BLOCK)
        diagonal = lax.broadcasted_iota(jnp.int32, square, 0) == lax.broadcasted_iota(jnp.int32, square, 1)
        keep = jnp.sum(jnp.where(diagonal, kept, 0.0), axis=1, keepdims=True)
        columns = jnp.where(lane == KERNEL_TAPS, keep, columns)
        masks[pl.ds(base, BLOCK), :] = columns.astype(jnp.bfloat16)
        return 0

    lax.fori_loop(0, rows // BLOCK, mask_block, 0)
    smalls[...] = jnp.zeros_like(smalls)

    @pl.when(place == 0)
    def _():
        a2f[0:HALO, :] = jnp.zeros((HALO, inner), jnp.bfloat16)
        dh3f[0:HALO, :] = jnp.zeros((HALO, inner), jnp.bfloat16)

    @pl.when(place == last)
    def _():
        a2f[HALO + rows :, :] = jnp.zeros((HALO, inner), jnp.bfloat16)
        dh3f[HALO + rows :, :] = jnp.zeros((HALO, inner), jnp.bfloat16)

    def both(own, other):
        left, right = ordered(side, own, other)
        return jnp.concatenate([left, right], axis=1)

    for swap in swaps:
        swap.wait()
    rows_here = both(unpack(cross_send), unpack(cross_recv)).astype(jnp.bfloat16)
    here = (bits[3], bits[2], bits[1], bits[0])
    w_in[here] = rows_here[:part_in]
    w_out[here] = rows_here[part_in : 2 * part_in]
    stage[0, 0] = rows_here[2 * part_in : 2 * part_in + stage.shape[2]]
    own_conv = pltpu.make_async_copy(stage.at[0, 0], g_conv.at[here], load_sems.at[1])
    own_conv.start()
    for index in range(3):
        lanes = slice(index * half, (index + 1) * half)
        wide[index : index + 1, :] = both(own_vectors[:, lanes], other_vectors[:, lanes])
    for index in range(6):
        lanes = slice(3 * half + index * wanted, 3 * half + index * wanted + quarter)
        narrow[index : index + 1, :] = both(own_vectors[:, lanes], other_vectors[:, lanes])

    def gather_copy(group, level):
        ref, sems, order = group
        every = slice(None)
        at = tuple(every if bit in order[:level] else bits[bit] for bit in (3, 2, 1, 0))
        return remote(ref.at[at], ref.at[at], sems, level, pairs[order[level]])

    in_rows = (w_in, in_gather, (3, 2, 1, 0))
    out_rows = (w_out, out_gather, (1, 3, 2, 0))
    conv_rows = (g_conv, conv_gather, (3, 2, 1, 0))

    def gather_next(group, level):
        gather_copy(group, level).wait()
        if level < 3:
            gather_copy(group, level + 1).start()

    gather_copy(in_rows, 0).start()
    gather_copy(out_rows, 0).start()
    own_conv.wait()
    gather_next(in_rows, 0)
    gather_copy(conv_rows, 0).start()
    gather_next(in_rows, 1)
    gather_next(in_rows, 2)
    gather_next(conv_rows, 0)
    gather_next(out_rows, 0)
    gather_next(in_rows, 3)

    def first_chunk(at, _):
        token_copy(at).wait_recv()

        def first(own, other, s1_block, h1_block, s2_block):
            base = pl.multiple_of((at * per + pl.program_id(0)) * BLOCK, BLOCK)
            x = jnp.concatenate(ordered(side, own[...], other[...]), axis=1)
            normed, _ = norm(x)
            act, slope = gelu_both(normed * wide[0:1, :] + wide[1:2, :])
            act = act.astype(jnp.bfloat16)
            a1v[pl.ds(base, BLOCK), :] = act
            s1_block[...] = slope
            value = dot(act, w_in[...].reshape(2 * half, inner)) + narrow[0:1, :]
            h1_block[...] = value
            normed, _ = norm(value)
            act, slope = gelu_both(normed * narrow[1:2, :] + narrow[2:3, :])
            keep = masks[pl.ds(base, BLOCK), KERNEL_TAPS : KERNEL_TAPS + 1].astype(jnp.float32)
            a2f[pl.ds(HALO + base, BLOCK), :] = (act * keep).astype(jnp.bfloat16)
            s2_block[...] = slope * keep

        pipeline(first, lambda i: at * per + i, [tokens.at[side], x_other], [s1, h1, s2], count=per)
        for level, (group, ready) in enumerate(((conv_rows, 1), (out_rows, 1), (out_rows, 2))):

            @pl.when(at == level)
            def _():
                gather_next(group, ready)

        return 0

    lead_copy.wait_recv()
    lax.fori_loop(0, CHUNKS, first_chunk, 0)
    halo_start(a2f, a2_sems)
    gather_next(conv_rows, 2)
    gather_next(out_rows, 3)
    gather_next(conv_rows, 3)

    def conv_load(pair):
        return pltpu.make_async_copy(g_conv.at[pair // 2, pair % 2], stage, load_sems.at[2])

    def relay(pair, _):
        conv_load(pair).start()
        conv_load(pair).wait()
        for low_bit in range(2):
            even = stage[low_bit, 0].astype(jnp.float32)
            odd = stage[low_bit, 1].astype(jnp.float32)
            at = pl.multiple_of((2 * pair + low_bit) * 2 * height, 2 * height)
            for tap in range(KERNEL_TAPS):
                top = tap * height
                w_conv[tap, pl.ds(at, 2 * height), :] = jnp.concatenate(
                    [even[top : top + height], odd[top : top + height]], axis=0
                ).astype(jnp.bfloat16)

        return 0

    lax.fori_loop(0, 4, relay, 0)

    def second(own, other, h3_block, s3_block, own_block):
        step = pl.program_id(0)
        at = middle_first(step)
        base = pl.multiple_of(at * BLOCK, BLOCK)

        @pl.when(step == blocks - 2)
        def _():
            halo_wait(a2f, a2_sems)

        taps = masks[pl.ds(base, BLOCK), :]
        weight = w_conv[...].reshape(KERNEL_TAPS * inner, inner)
        value = dot(windowed(a2f, taps, base, BLOCK), weight) + narrow[3:4, :]
        h3_block[...] = value
        normed, _ = norm(value)
        act, slope = gelu_both(normed * narrow[4:5, :] + narrow[5:6, :])
        act = act.astype(jnp.bfloat16)
        a3v[pl.ds(base, BLOCK), :] = act
        s3_block[...] = slope
        mixed = dot(act, w_out[...].reshape(2 * half, inner), ((1,), (1,))) + wide[2:3, :]
        left, right = mixed[:, :half], mixed[:, half:]
        own_block[...] = (own[...].astype(jnp.float32) + jnp.where(low, left, right)).astype(jnp.bfloat16)
        out_send[pl.ds(base, BLOCK), :] = (
            other[...].astype(jnp.float32) + jnp.where(low, right, left)
        ).astype(jnp.bfloat16)
        out_copy(at).start()

    pipeline(second, middle_first, [tokens.at[side], x_other], [h3, s3, out_own])

    def add_small(row, value):
        smalls[row : row + 1, :] += value

    def add_wide(row, value):
        smalls[row : row + 1, :] += value[:, :half]
        smalls[row + 1 : row + 2, :] += value[:, half:]

    def third(h3_block, s3_block):
        at = pl.program_id(0)
        base = pl.multiple_of(at * BLOCK, BLOCK)
        for later in range(CHUNKS):

            @pl.when(at == later * per)
            def _():
                gy_copy(later).wait_recv()

        gy = jnp.concatenate([gyv[0, pl.ds(base, BLOCK), :], gyv[1, pl.ds(base, BLOCK), :]], axis=1)
        add_wide(4, column_sums(gy.astype(jnp.float32)))
        dz3 = dot(gy, w_out[...].reshape(2 * half, inner)) * s3_block[...]
        normed, scale = norm(h3_block[...])
        dh3 = norm_back(dz3, normed, scale, narrow[4:5, :]).astype(jnp.bfloat16)
        dh3f[pl.ds(HALO + base, BLOCK), :] = dh3
        add_small(9, column_sums(dh3.astype(jnp.float32)))
        add_small(10, column_sums(dz3 * normed))
        add_small(11, column_sums(dz3))

    own_gy.wait()
    pipeline(third, in_order, [h3, s3], [])
    halo_start(dh3f, dh3_sems)

    def slot(pair, order):
        two = (pair % 4) if order[0] == 1 else (pair % 4) // 2 + 2 * (pair % 2)
        return pair // 4 * 4 + two

    def split(group, at, even, odd):
        keep_ref, send_ref = group[0], group[1]
        mine_first = bits[0] == 0
        keep_ref[at] = jnp.where(mine_first, even, odd)
        send_ref[at] = jnp.where(mine_first, odd, even).astype(jnp.bfloat16)

    def wide_grad(left_of, right_ref, group):
        tall_rows = group[0].shape[1]

        def tile(at, _):
            value = dot(left_of(at), right_ref[...], ((0,), (0,)))
            for pair in range(4):
                top = 2 * pair * tall_rows
                split(
                    group,
                    at * 4 + slot(pair, group[4]),
                    value[top : top + tall_rows],
                    value[top + tall_rows : top + 2 * tall_rows],
                )
            return 0

        lax.fori_loop(0, 2, tile, 0)
        sum_copy(group, 0).start()

    def conv_grad_of(taps, group):
        right = dh3f.at[pl.ds(HALO, rows)]
        values = []
        for tap in taps:
            left = a2f[tap * DILATION_STEP : tap * DILATION_STEP + rows, :] * masks[:, tap : tap + 1]
            values.append(dot(left, right[...], ((0,), (0,))))
        if len(values) == 1:
            tail = [jnp.zeros((CONV_PAD, inner), jnp.float32)]
        else:
            tail = []
        for pair in range(8):
            top = 2 * pair * height
            split(
                group,
                slot(pair, group[4]),
                jnp.concatenate([v[top : top + height] for v in values] + tail, axis=0),
                jnp.concatenate([v[top + height : top + 2 * height] for v in values] + tail, axis=0),
            )
        sum_copy(group, 0).start()

    y_first, z_first = (1, 2, 3), (2, 1, 3)
    in_set = (k_in, s_in, (r0_in, r1_in, r2_in, r3_in), in_sems, y_first)
    out_set = (k_out, s_out, (r0_out, r1_out, r2_out, r3_out), out_rs_sems, z_first)
    low_set = (k_low, s_low, (r0_low, r1_low, r2_low, r3_low), low_sems, y_first)
    mid_set = (k_mid, s_mid, (r0_mid, r1_mid, r2_mid, r3_mid), mid_sems, z_first)
    top_set = (k_top, s_top, (r0_top, r1_top, r2_top, r3_top), top_sems, y_first)
    starts = (0, 0, 4, 6)
    lengths = (8, 4, 2, 1)

    def sum_copy(group, level):
        _, send, received, sems, order = group
        bit = 0 if level == 0 else order[level - 1]
        return remote(
            send.at[pl.ds(starts[level], lengths[level])], received[level], sems, level, pairs[bit]
        )

    def sum_step(group, level):
        keep, send, received, _, order = group
        sum_copy(group, level).wait()
        came = received[level]
        fixed = 0
        for at in range(level):
            fixed = fixed + bits[order[at]] * (1 << at)
        if level == 3:
            keep[fixed] = keep[fixed] + came[0].astype(jnp.float32)
            return
        mine = bits[order[level]]

        def one(item, _):
            other = 2 * item + 1 - mine
            same = 2 * item + mine
            send[starts[level + 1] + item] = (
                keep[other * (1 << level) + fixed] + came[other].astype(jnp.float32)
            ).astype(jnp.bfloat16)
            at = same * (1 << level) + fixed
            keep[at] = keep[at] + came[same].astype(jnp.float32)
            return 0

        lax.fori_loop(0, lengths[level + 1], one, 0)
        sum_copy(group, level + 1).start()

    def at_step(step, when, *steps):
        @pl.when(step == when)
        def _():
            for group, level in steps:
                sum_step(group, level)

    conv_grad_of((0, 1), low_set)
    conv_grad_of((2, 3), mid_set)
    conv_grad_of((4,), top_set)
    wide_grad(lambda at: gyv[at], a3v, out_set)

    def fourth(h1_block, s2_block):
        step = pl.program_id(0)
        base = pl.multiple_of(step * BLOCK, BLOCK)
        taps = masks[pl.ds(base, BLOCK), :]
        da2 = jnp.zeros((BLOCK, inner), jnp.float32)
        for tap in range(KERNEL_TAPS):
            window = dh3f[pl.ds(base + tap * DILATION_STEP, BLOCK), :] * taps[:, tap : tap + 1]
            da2 = da2 + dot(window, w_conv[KERNEL_TAPS - 1 - tap], ((1,), (1,)))
        dz2 = da2 * s2_block[...]
        normed, scale = norm(h1_block[...])
        dh1 = norm_back(dz2, normed, scale, narrow[1:2, :]).astype(jnp.bfloat16)
        a3v[pl.ds(base, BLOCK), :] = dh1
        add_small(6, column_sums(dh1.astype(jnp.float32)))
        add_small(7, column_sums(dz2 * normed))
        add_small(8, column_sums(dz2))
        at_step(step, 0, (low_set, 0), (mid_set, 0), (top_set, 0))
        at_step(step, 1, (out_set, 0))
        at_step(step, 5, (low_set, 1))
        at_step(step, 6, (mid_set, 1))
        at_step(step, 7, (top_set, 1))

    halo_wait(dh3f, dh3_sems)
    pipeline(fourth, in_order, [h1, s2], [])
    wide_grad(lambda at: a1v[:, pl.ds(pl.multiple_of(at * half, 128), half)], a3v, in_set)
    sum_step(out_set, 1)
    sum_step(low_set, 2)

    def fifth(own, other, s1_block, own_block, tail_block, end_block):
        step = pl.program_id(0)
        base = pl.multiple_of(step * BLOCK, BLOCK)
        dh1 = a3v[pl.ds(base, BLOCK), :]
        dz1 = dot(dh1, w_in[...].reshape(2 * half, inner), ((1,), (1,))) * s1_block[...]
        x = jnp.concatenate(ordered(side, own[...], other[...]), axis=1)
        normed, scale = norm(x)
        dx = norm_back(dz1, normed, scale, wide[0:1, :])
        add_wide(0, column_sums(dz1 * normed))
        add_wide(2, column_sums(dz1))
        left, right = dx[:, :half], dx[:, half:]
        own_block[...] = jnp.where(low, left, right) + gyv[side, pl.ds(base, BLOCK), :].astype(jnp.float32)
        sent = jnp.where(low, right, left).astype(jnp.bfloat16)
        gyv[1 - side, pl.ds(base, BLOCK), :] = sent
        end_block[...] = sent

        @pl.when(step < blocks - 1)
        def _():
            tail_block[...] = sent

        @pl.when(step < HEAD)
        def _():
            dx_copy(step).start()

        at_step(step, 0, (mid_set, 2), (in_set, 0))
        at_step(step, 2, (out_set, 2), (top_set, 2))
        at_step(step, 4, (low_set, 3))
        at_step(step, 5, (mid_set, 3))
        at_step(step, 6, (in_set, 1))
        at_step(step, 7, (top_set, 3), (out_set, 3))

    pipeline(fifth, in_order, [tokens.at[side], x_other, s1], [dx_own], (dx_tail, dx_end))


    def small_copy(level):
        device = pairs[level] if level < 4 else across
        return remote(small_send.at[level], small_recv.at[level], small_sems, level, device)

    def small_start(level):
        small_send[level] = smalls[...]
        small_copy(level).start()

    def small_step(level):
        small_copy(level).wait()
        smalls[...] += small_recv[level]

    small_start(0)
    sum_step(in_set, 2)
    small_step(0)
    small_start(1)
    small_step(1)
    small_start(2)
    small_step(2)
    small_start(3)
    sum_step(in_set, 3)
    small_step(3)
    small_start(4)

    def owned(group):
        keep, order = group[0], group[4]
        return keep[bits[order[0]] + 2 * bits[order[1]] + 4 * bits[order[2]]]

    groups = (in_set, out_set, low_set, mid_set, top_set)
    others = []
    for group in groups:
        value = owned(group)
        others.append(jnp.where(low, value[:, quarter:], value[:, :quarter]))
    pack(others)
    for at in range(blocks):
        out_copy(at).wait()
    cross = remote(cross_send, cross_recv, cross_sems, 0, across)
    cross.start()
    lead_copy.wait_send()
    for at in range(CHUNKS):
        token_copy(at).wait_send()
        gy_copy(at).wait_send()
    small_step(4)
    for index in range(3):
        both = smalls[2 * index : 2 * index + 2, :]
        sums_out[:, index * half : (index + 1) * half] = jnp.where(low, both[0:1], both[1:2])
    for index in range(6):
        both = smalls[6 + index : 7 + index, :]
        at = 3 * half + index * wanted
        sums_out[:, at : at + quarter] = jnp.where(low, both[:, :quarter], both[:, quarter:])
    cross.wait()
    came = unpack(cross_recv)
    row = 0
    for group in groups:
        value = owned(group)
        height = value.shape[0]
        grads_out[row : row + height, :] = (
            jnp.where(low, value[:, :quarter], value[:, quarter:]) + came[row : row + height]
        )
        row += height
    for at in range(HEAD):
        dx_copy(at).wait()


def fast_call(tokens, cot, lengths, residues, proj_in, proj_out, conv_own, vectors):
    _, rows, half = tokens.shape
    model = 2 * half
    inner = 2 * proj_in.shape[1]
    part_in = proj_in.shape[0]
    part_conv = conv_own.shape[1]
    f32, bf16 = jnp.float32, jnp.bfloat16
    tall = KERNEL_TAPS * part_conv + CONV_PAD
    any_spec = pl.BlockSpec(memory_space=pl.ANY)
    vmem_spec = pl.BlockSpec(memory_space=pltpu.VMEM)
    total = 2 * part_in + tall
    wanted = half // 2 + 64
    packed = (total + 31) // 32 * 16

    def sums(height):
        return [pltpu.VMEM((8, height, inner), f32), pltpu.VMEM((8, height, inner), bf16)] + [
            pltpu.VMEM((length, height, inner), bf16) for length in (8, 4, 2, 1)
        ]

    def sems(count):
        return pltpu.SemaphoreType.DMA((2, count))

    shapes = [
        ((rows, half), bf16),
        ((rows, half), bf16),
        ((rows, half), f32),
        ((rows, half), bf16),
        ((rows - (HEAD + 1) * BLOCK, half), bf16),
        ((BLOCK, half), bf16),
        ((total, half // 2), f32),
        ((1, 3 * half + 6 * wanted), f32),
        ((rows, half), bf16),
        ((2, 2, 2, 2, tall, inner), bf16),
        ((rows, model), f32),
        ((rows, inner), f32),
        ((rows, inner), f32),
        ((rows, inner), f32),
        ((rows, inner), f32),
    ]
    flops = 6 * rows * (2 * model * inner + KERNEL_TAPS * inner * inner)
    results = pl.pallas_call(
        fast_kernel,
        out_shape=[jax.ShapeDtypeStruct(shape, dtype) for shape, dtype in shapes],
        in_specs=[any_spec] * 2 + [vmem_spec] * 14,
        out_specs=[any_spec] * 6 + [vmem_spec] * 2 + [any_spec] * 7,
        scratch_shapes=[
            pltpu.VMEM((rows, 8), bf16),
            pltpu.VMEM((1, 3 * half + 6 * wanted), f32),
            pltpu.VMEM((1, 3 * half + 6 * wanted), f32),
            pltpu.VMEM((8, model), f32),
            pltpu.VMEM((8, inner), f32),
            pltpu.VMEM((2, 2, tall, inner), bf16),
            pltpu.VMEM((rows, model), bf16),
            pltpu.VMEM((rows + 2 * HALO, inner), bf16),
            pltpu.VMEM((rows, inner), bf16),
            pltpu.VMEM((2, rows, half), bf16),
            pltpu.VMEM((rows + 2 * HALO, inner), bf16),
            pltpu.VMEM((rows, half), bf16),
            pltpu.VMEM((2, 2, 2, 2, part_in, inner), bf16),
            pltpu.VMEM((2, 2, 2, 2, part_in, inner), bf16),
            pltpu.VMEM((KERNEL_TAPS, inner, inner), bf16),
        ]
        + sums(part_in) * 4
        + sums(tall - 2 * part_in)
        + [
            pltpu.VMEM((16, inner), f32),
            pltpu.VMEM((packed, inner), bf16),
            pltpu.VMEM((packed, inner), bf16),
            pltpu.VMEM((5, 16, inner), f32),
            pltpu.VMEM((5, 16, inner), f32),
            pltpu.SemaphoreType.DMA((3,)),
            sems(2),
            sems(CHUNKS + 1),
            sems(4),
            sems(4),
            sems(4),
            sems(CHUNKS),
            sems(rows // BLOCK),
            sems(HEAD),
            sems(2),
            sems(2),
            sems(4),
            sems(4),
            sems(4),
            sems(4),
            sems(4),
            sems(1),
            sems(5),
        ],
        compiler_params=pltpu.CompilerParams(
            collective_id=0, has_side_effects=True, vmem_limit_bytes=65280 * 2**10
        ),
        cost_estimate=pl.CostEstimate(flops=flops, bytes_accessed=120 * 2**20, transcendentals=0),
    )(tokens, cot, lengths, residues, proj_in, proj_out, conv_own, *vectors)
    return results[:8]


def finish_kernel(side_ref, tail_ref, cot_ref, whole_ref, out_ref):
    at = pl.ds(pl.multiple_of(pl.program_id(0) * BLOCK, BLOCK), BLOCK)
    out_ref[0] = tail_ref[at, :].astype(jnp.float32) + cot_ref[0].astype(jnp.float32)


def assemble_kernel(side_ref, out_own, out_back, dx_own, dx_back, cot, block_out, grad_tokens):
    side = side_ref[0]
    block_out[side] = out_own[...]
    block_out[1 - side] = out_back[...]
    grad_tokens[side] = dx_own[...]
    grad_tokens[1 - side] = dx_back[...].astype(jnp.float32) + cot[0].astype(jnp.float32)


def assemble_call(side, out_own, out_back, dx_own, dx_back, cot):
    rows, half = out_own.shape
    tile = 2 * BLOCK
    by_tile = pl.BlockSpec((tile, half), lambda i, side_ref: (i, 0))
    pair = pl.BlockSpec((2, tile, half), lambda i, side_ref: (0, i, 0))
    return pl.pallas_call(
        assemble_kernel,
        grid_spec=pltpu.PrefetchScalarGridSpec(
            num_scalar_prefetch=1,
            grid=(rows // tile,),
            in_specs=[by_tile] * 4
            + [pl.BlockSpec((1, tile, half), lambda i, side_ref: (1 - side_ref[0], i, 0))],
            out_specs=[pair, pair],
        ),
        out_shape=[
            jax.ShapeDtypeStruct((2, rows, half), jnp.bfloat16),
            jax.ShapeDtypeStruct((2, rows, half), jnp.float32),
        ],
        compiler_params=pltpu.CompilerParams(
            dimension_semantics=("arbitrary",), vmem_limit_bytes=56 * 2**20
        ),
        cost_estimate=pl.CostEstimate(flops=rows * half, bytes_accessed=24 * rows * half, transcendentals=0),
    )(side, out_own, out_back, dx_own, dx_back, cot)


def finish_call(side, tail, cot, grad_tokens, first):
    half = tail.shape[1]

    def theirs(i, side_ref):
        return (1 - side_ref[0], first + i, 0)

    return pl.pallas_call(
        finish_kernel,
        grid_spec=pltpu.PrefetchScalarGridSpec(
            num_scalar_prefetch=1,
            grid=(tail.shape[0] // BLOCK,),
            in_specs=[
                pl.BlockSpec(memory_space=pltpu.VMEM),
                pl.BlockSpec((1, BLOCK, half), theirs),
                pl.BlockSpec(memory_space=pl.ANY),
            ],
            out_specs=pl.BlockSpec((1, BLOCK, half), theirs),
        ),
        out_shape=jax.ShapeDtypeStruct(grad_tokens.shape, grad_tokens.dtype),
        input_output_aliases={3: 0},
        compiler_params=pltpu.CompilerParams(
            dimension_semantics=("arbitrary",), vmem_limit_bytes=63 * 2**20
        ),
        cost_estimate=pl.CostEstimate(flops=tail.size, bytes_accessed=8 * tail.size, transcendentals=0),
    )(side, tail, cot, grad_tokens)


def fast_body(
    tokens,
    cotangent,
    seq_lengths,
    residue_mask,
    first_gain,
    first_shift,
    proj_in,
    in_bias,
    mid_gain,
    mid_shift,
    conv_weight,
    conv_bias,
    last_gain,
    last_shift,
    proj_out,
    out_bias,
):
    micro, rows, half = tokens.shape
    inner_half = in_bias.shape[0]
    side = lax.axis_index("ch")

    def swap(value):
        return lax.ppermute(value, "ch", SWAP)

    part_in = proj_in.shape[0]
    part_conv = conv_weight.shape[1]
    vectors = (
        first_gain, first_shift, out_bias, in_bias, mid_gain, mid_shift, conv_bias, last_gain, last_shift
    )
    out_own, out_back, dx_own, dx_back, dx_tail, dx_end, grads, sums = fast_call(
        tokens, cotangent, seq_lengths, residue_mask, proj_in, proj_out.T, conv_weight, vectors
    )
    conv_part = grads[2 * part_in : 2 * part_in + KERNEL_TAPS * part_conv]

    side_array = side.astype(jnp.int32).reshape(1)
    tail_back = swap(dx_tail)
    block_out, grad_tokens = assemble_call(side_array, out_own, out_back, dx_own, dx_back, cotangent)
    dx_end, grad_tokens = lax.optimization_barrier((dx_end, grad_tokens))
    end_back = swap(dx_end)
    grad_tokens = finish_call(side_array, tail_back, cotangent, grad_tokens, HEAD)
    gy_end = lax.dynamic_index_in_dim(cotangent[:, rows - BLOCK :], 1 - side, 0, keepdims=True)
    end = end_back.astype(jnp.float32)[None] + gy_end.astype(jnp.float32)
    grad_tokens = lax.dynamic_update_slice(grad_tokens, end, (1 - side, rows - BLOCK, 0))
    wanted = inner_half + 64

    def narrow_part(index):
        at = 3 * half + index * wanted
        return sums[0, at : at + inner_half]

    return (
        block_out,
        grad_tokens,
        sums[0, :half],
        sums[0, half : 2 * half],
        grads[:part_in],
        narrow_part(0),
        narrow_part(1),
        narrow_part(2),
        conv_part.reshape(KERNEL_TAPS, part_conv, inner_half),
        narrow_part(3),
        narrow_part(4),
        narrow_part(5),
        grads[part_in : 2 * part_in].T,
        sums[0, 2 * half : 3 * half],
    )


def solution(mesh):
    placed = (
        P(None, "seq", "ch"),
        P(None, "seq", "ch"),
        P(),
        P(None, "seq"),
        P("ch"),
        P("ch"),
        P("seq", "ch"),
        P("ch"),
        P("ch"),
        P("ch"),
        P(None, "seq", "ch"),
        P("ch"),
        P("ch"),
        P("ch"),
        P("ch", "seq"),
        P("ch"),
    )
    run = fast_body if mesh.shape["seq"] == 16 else body
    return jax.shard_map(
        run,
        mesh=mesh,
        in_specs=placed,
        out_specs=(
            P(None, "seq", "ch"),
            P(None, "seq", "ch"),
            P("ch"),
            P("ch"),
            P("seq", "ch"),
            P("ch"),
            P("ch"),
            P("ch"),
            P(None, "seq", "ch"),
            P("ch"),
            P("ch"),
            P("ch"),
            P("ch", "seq"),
            P("ch"),
        ),
        check_vma=False,
    )
```
